128 devices in a mesh: dp: 32 (over y_lo, x, z), tensor: 4 (over y_hi, core).
Axes of the slice: x: 4, y: 4 (y_hi: 2, y_lo: 2; y = y_hi * 2 + y_lo), z: 4, core: 2. Of those that a mesh axis runs over, the one named last changes fastest.
Arguments:
- residual_in: bfloat16 [16384, 2048], P(('dp', 'tensor')), may hold values from -24 to 24
- segment_ids: int32 [16384], P('dp'), may hold values from 0 to 127, as said below
- out_grad: bfloat16 [16384, 2048], P(('dp', 'tensor')), may hold values from -24 to 24
- ln_gain: bfloat16 [2048], P(('dp', 'tensor')), may hold values from 0.5 to 1.5
- ln_bias: bfloat16 [2048], P(('dp', 'tensor')), may hold values from -3 to 3
- w_qkv: bfloat16 [2048, 3, 2048], P('dp', None, 'tensor'), may hold values from -0.125 to 0.125
- b_qkv: bfloat16 [3, 4, 512], P(None, 'tensor', 'dp'), may hold values from -3 to 3
- w_out: bfloat16 [2048, 2048], P('tensor', 'dp'), may hold values from -1 to 1
- b_attn_out: bfloat16 [2048], P(('dp', 'tensor')), may hold values from -3 to 3
- w_up: bfloat16 [2048, 8192], P('dp', 'tensor'), may hold values from -0.125 to 0.125
- b_up: bfloat16 [4, 2048], P('tensor', 'dp'), may hold values from -3 to 3
- w_down: bfloat16 [8192, 2048], P('tensor', 'dp'), may hold values from -0.0625 to 0.0625
- b_mlp_out: bfloat16 [2048], P(('dp', 'tensor')), may hold values from -3 to 3
Outputs:
- output: bfloat16 [16384, 2048], P(('dp', 'tensor'))
- grad_in: float32 [16384, 2048], P(('dp', 'tensor'))
- grad_ln_gain: float32 [2048], P(('dp', 'tensor'))
- grad_ln_bias: float32 [2048], P(('dp', 'tensor'))
- grad_w_qkv: float32 [2048, 3, 2048], P('dp', None, 'tensor')
- grad_b_qkv: float32 [3, 4, 512], P(None, 'tensor', 'dp')
- grad_w_out: float32 [2048, 2048], P('tensor', 'dp')
- grad_b_attn_out: float32 [2048], P(('dp', 'tensor'))
- grad_w_up: float32 [2048, 8192], P('dp', 'tensor')
- grad_b_up: float32 [4, 2048], P('tensor', 'dp')
- grad_w_down: float32 [8192, 2048], P('tensor', 'dp')
- grad_b_mlp_out: float32 [2048], P(('dp', 'tensor'))
The draws below stay inside these ranges and needn't reach their ends.
Inputs may be any that keep to these rules, and one draw needn't show every extreme that they name: `segment_ids`: each run of 512 tokens is one sequence; along it segment numbers never fall, and numbers of different sequences differ.
All inputs are finite; a program needn't handle non-finite values.
Results may differ from the reference program's by a relative error of at most 0.011.
Values may be sent and summed in bfloat16 or wider, within the bound.
No kernel may reach another device: no remote copies, remote signals or barrier semaphores. Data moves between devices by JAX's collectives and lax.ppermute only.
A program may use at most 320 MiB of HBM per device.

```python
import jax
import jax.numpy as jnp
from jax import lax

D = 2048
HEADS = 32
HD = 64
ROT = 32
FF = 8192
TOK_DEV = 128
SEQ = 512
TOKENS = 16384
N_TENSOR = 4


def draw_segment_ids(key, part):
    key = jax.random.fold_in(key, 11)
    key_first, key_second, key_third = jax.random.split(key, 3)
    sequences = TOKENS // SEQ
    first_cut = jax.random.randint(key_first, (sequences,), 1, TOK_DEV)
    second_cut = jax.random.randint(key_second, (sequences,), SEQ - TOK_DEV + 1, SEQ - 1)
    third_cut = jax.random.randint(key_third, (sequences,), second_cut + 1, SEQ)
    places = jnp.arange(SEQ, dtype=jnp.int32)[None, :]
    local_ids = (places >= first_cut[:, None]).astype(jnp.int32) + (places >= second_cut[:, None]).astype(jnp.int32) + (places >= third_cut[:, None]).astype(jnp.int32)
    offsets = 4 * jnp.arange(sequences, dtype=jnp.int32)[:, None]
    return (local_ids + offsets).reshape(TOKENS).astype(jnp.int32)


def raised(values, key, source, target, blocks, factor):
    owner, partner = [(jnp.arange(values.shape[position]) // (values.shape[position] // blocks)).reshape([-1 if axis == position else 1 for axis in range(values.ndim)]) for position in (source, target)]
    chosen = jax.random.permutation(key, blocks)[partner]
    strong = (owner == chosen) | (owner == (partner + blocks // 2) % blocks)
    return jnp.where(strong, factor * values, values)


def steps_of(own_key, extent, pieces, smallest, high):
    gain, own = 1.0, jax.random.fold_in(own_key, 6)
    for dim, parts in pieces:
        steps = jnp.exp(jax.random.uniform(jax.random.fold_in(own, dim), (parts,), jnp.float32, smallest / len(pieces), high / len(pieces)))
        gain = gain * jnp.repeat(steps, extent[dim] // parts).reshape([-1 if axis == dim else 1 for axis in range(len(extent))])
    return gain


def gaussian(key, dims, scale, bound, pieces=(), kind=jnp.bfloat16):
    values = jax.random.normal(key, dims, jnp.float32) * scale
    if len(pieces) > 0:
        values = steps_of(key, dims, pieces, -0.22, 0.18) * values
    return jnp.clip(values, min=-bound, max=bound).astype(kind)


def bell_draw_with(key, shape, spread, reach, cuts, heavy, kind=jnp.bfloat16):
    array = spread * jax.random.normal(key, shape, jnp.float32)
    if cuts:
        array = array * steps_of(key, shape, cuts, -0.22, 0.18)
    return jnp.clip(raised(array, jax.random.fold_in(key, 3), *heavy), -reach, reach).astype(kind)


def setup_inputs(seed: int = 0) -> dict:
    arg_keys = jax.random.split(jax.random.key(seed), 14)
    residual_in = bell_draw_with(arg_keys[0], (TOKENS, D), 1.0, 24.0, ((0, 128),), (0, 1, 128, 5.5))
    segment_ids = draw_segment_ids(jax.random.fold_in(arg_keys[13], 71), 0)
    out_grad = bell_draw_with(arg_keys[2], (TOKENS, D), 1.0, 24.0, ((0, 128),), (0, 1, 128, 5.5))
    ln_gain = jnp.clip(1.0 + 0.1 * jax.random.normal(arg_keys[3], (D,), jnp.float32), 0.5, 1.5).astype(jnp.bfloat16)
    ln_bias = gaussian(arg_keys[4], (D,), 0.3, 3.0, ((0, 128),))
    w_qkv = gaussian(arg_keys[5], (D, 3, D), D ** -0.5, 0.125, ((0, 32), (2, 4)))
    b_qkv = gaussian(arg_keys[6], (3, N_TENSOR, D // N_TENSOR), 0.3, 3.0, ((1, 4), (2, 32)))
    w_out = gaussian(arg_keys[7], (D, D), (D // 64) ** -0.5, 1.0, ((0, 4), (1, 32)))
    b_attn_out = gaussian(arg_keys[8], (D,), 0.3, 3.0, ((0, 128),))
    w_up = gaussian(arg_keys[9], (D, FF), D ** -0.5, 0.125, ((0, 32), (1, 4)))
    b_up = gaussian(arg_keys[10], (N_TENSOR, FF // N_TENSOR), 0.3, 3.0, ((0, 4), (1, 32)))
    w_down = gaussian(arg_keys[11], (FF, D), FF ** -0.5, 0.0625, ((0, 4), (1, 32)))
    b_mlp_out = gaussian(arg_keys[12], (D,), 0.3, 3.0, ((0, 128),))
    return {"residual_in": residual_in, "segment_ids": segment_ids, "out_grad": out_grad, "ln_gain": ln_gain, "ln_bias": ln_bias, "w_qkv": w_qkv, "b_qkv": b_qkv, "w_out": w_out, "b_attn_out": b_attn_out, "w_up": w_up, "b_up": b_up, "w_down": w_down, "b_mlp_out": b_mlp_out}


HIGH = lax.Precision.HIGHEST
EPS = 1e-05

@jax.custom_vjp
def low(v):
    return lax.optimization_barrier(v.astype(jnp.bfloat16)).astype(jnp.float32)

@jax.custom_vjp
def low_back(v):
    return v

def low_keep(v):
    return (low(v), None)

def low_pass(kept, grad):
    return (grad,)

def back_keep(v):
    return (v, None)

def back_low(kept, grad):
    return (low(grad),)
low.defvjp(low_keep, low_pass)
low_back.defvjp(back_keep, back_low)

def doc_positions(segments):
    length = segments.shape[0]
    places = jnp.arange(length, dtype=jnp.int32)
    boundary = jnp.concatenate([jnp.ones((1,), dtype=jnp.bool_), segments[1:] != segments[:-1]])
    doc_start = lax.cummax(jnp.where(boundary, places, jnp.zeros_like(places)), axis=0)
    return places - doc_start

def angle_tables(positions):
    half_rot = ROT // 2
    frequency = 10000.0 ** (-(2.0 * jnp.arange(half_rot, dtype=jnp.float32)) / ROT)
    angles = positions.astype(jnp.float32)[:, None] * frequency[None, :]
    return (jnp.cos(angles), jnp.sin(angles))

def rotate(values, cosine_table, sine_table):
    half_rot = ROT // 2
    front = values[..., :half_rot]
    behind = values[..., half_rot:2 * half_rot]
    remain = values[..., 2 * half_rot:]
    cosine_heads = cosine_table[:, None, :]
    sine_heads = sine_table[:, None, :]
    return jnp.concatenate([front * cosine_heads - behind * sine_heads, behind * cosine_heads + front * sine_heads, remain], axis=-1)

def layer_rows(token_rows, segments, params):
    ln_gain, ln_bias, w_qkv, b_qkv, w_out, b_attn_out, w_up, b_up, w_down, b_mlp_out = params
    length = token_rows.shape[0]
    average = lax.optimization_barrier(jnp.mean(token_rows, axis=-1, keepdims=True))
    centred = token_rows - average
    variance = lax.optimization_barrier(jnp.mean(centred * centred, axis=-1, keepdims=True))
    standard = centred * lax.rsqrt(variance + EPS)
    normed = low(standard * ln_gain + ln_bias)
    projected = jnp.einsum('td,dcf->tcf', normed, w_qkv, precision=HIGH) + b_qkv.reshape(3, D)
    projected = low_back(projected)
    positions = doc_positions(segments)
    cosine_table, sine_table = angle_tables(positions)
    head_split = projected.reshape(length, 3, HEADS, HD)
    queries = low(rotate(head_split[:, 0], cosine_table, sine_table))
    rotated_keys = low(rotate(head_split[:, 1], cosine_table, sine_table))
    values = low(head_split[:, 2])
    places = jnp.arange(length, dtype=jnp.int32)
    allowed = (segments[:, None] == segments[None, :]) & (places[None, :] <= places[:, None])
    scores = low_back(jnp.einsum('qhd,khd->hqk', queries, rotated_keys, precision=HIGH) * HD ** (-0.5))
    scores = jnp.where(allowed[None], scores, -1e+30)
    soft = low(jax.nn.softmax(scores, axis=-1))
    attended = jnp.einsum('hqk,khd->qhd', soft, values, precision=HIGH).reshape(length, D)
    attended = low(low_back(attended))
    hidden = low_back(jnp.dot(normed, w_up, precision=HIGH) + b_up.reshape(FF))
    hidden = low(jax.nn.gelu(hidden, approximate=True))
    branch = jnp.dot(attended, w_out, precision=HIGH) + jnp.dot(hidden, w_down, precision=HIGH)
    return token_rows + branch + b_attn_out + b_mlp_out

def reference(residual_in, segment_ids, out_grad, ln_gain, ln_bias, w_qkv, b_qkv, w_out, b_attn_out, w_up, b_up, w_down, b_mlp_out):
    params = tuple((weight.astype(jnp.float32) for weight in (ln_gain, ln_bias, w_qkv, b_qkv, w_out, b_attn_out, w_up, b_up, w_down, b_mlp_out)))
    sequences = TOKENS // SEQ
    inputs = residual_in.astype(jnp.float32)
    sequence_ids = segment_ids.reshape(sequences, SEQ)
    checked = jax.checkpoint(layer_rows)

    def forward(token_rows, weights):
        blocks = token_rows.reshape(sequences, SEQ, D)

        def one_sequence(pair):
            return checked(pair[0], pair[1], weights)
        return lax.map(one_sequence, (blocks, sequence_ids)).reshape(TOKENS, D)
    output, pullback = jax.vjp(forward, inputs, params)
    grad_in, gradients = pullback(out_grad.astype(jnp.float32))
    return (output.astype(jnp.bfloat16), grad_in, gradients[0], gradients[1], gradients[2], gradients[3], gradients[4], gradients[5], gradients[6], gradients[7], gradients[8], gradients[9])
```

```python
import jax
import jax.numpy as jnp
from jax import lax
from jax.experimental import pallas as pl
from jax.experimental.pallas import tpu as pltpu
from jax.sharding import Mesh, PartitionSpec as P

HD = 64
ROT = 32
EPS = 1e-05
MASKED = -1e30
D = 2048
SEQ = 512
BLK = 64
ORDER = (0, 1, 3, 2)
VMEM_LIMIT = 20 * 1024 * 1024
BF = jnp.bfloat16
F32 = jnp.float32
AXES = ("y_lo", "x", "z", "y_hi", "core")

bar = lax.optimization_barrier


def swap_ring(value, axis, step):
    masks = (1, 3) if step == 0 else (3, 1)
    table = [(i * 2 + c, (i ^ masks[c]) * 2 + c) for i in range(4) for c in range(2)]
    return lax.ppermute(value, (axis, "core"), table)


def swap_y(value, step):
    masks = (1, 3) if step == 0 else (3, 1)

    def place(y, c):
        return ((y % 2) * 2 + y // 2) * 2 + c

    table = [(place(y, c), place(y ^ masks[c], c)) for y in range(4) for c in range(2)]
    return lax.ppermute(value, ("y_lo", "y_hi", "core"), table)


def flip(value, axis):
    return lax.ppermute(value, axis, [(0, 1), (1, 0)])


def flip4(value, axis, mask):
    return lax.ppermute(value, axis, [(i, i ^ mask) for i in range(4)])


def swap_pair(a, b, axis_a, axis_b, step):
    a, b = bar((a, b))
    return bar((swap_ring(a, axis_a, step), swap_ring(b, axis_b, step)))


def copies(core, plan, shapes, *sources):
    def kernel(core_ref, *refs):
        inputs, outputs, sems = refs[: len(sources)], refs[len(sources) : -1], refs[-1]
        second_core = core_ref[0]
        started = []
        for i, (source, low, rows, target, at, at_second) in enumerate(plan):
            place = at if at == at_second else pl.multiple_of(at + second_core * (at_second - at), rows)
            copy = pltpu.make_async_copy(
                inputs[source].at[pl.ds(low, rows)], outputs[target].at[pl.ds(place, rows)], sems.at[i]
            )
            copy.start()
            started.append(copy)
        for copy in started:
            copy.wait()

    return pl.pallas_call(
        kernel,
        in_specs=[pl.BlockSpec(memory_space=pltpu.SMEM)] + [pl.BlockSpec(memory_space=pl.ANY)] * len(sources),
        out_specs=[pl.BlockSpec(memory_space=pltpu.VMEM)] * len(shapes),
        out_shape=[jax.ShapeDtypeStruct(shape, BF) for shape in shapes],
        scratch_shapes=[pltpu.SemaphoreType.DMA((len(plan),))],
        compiler_params=pltpu.CompilerParams(vmem_limit_bytes=VMEM_LIMIT),
        cost_estimate=pl.CostEstimate(flops=0, bytes_accessed=2 * 10**6, transcendentals=0),
        name="put_together",
    )(core, *sources)


class Gather:
    def __init__(self, core, a, b):
        self.core, self.a, self.b = core, a, b

    def send(self, step):
        if step % 2:
            return self.a, self.b
        rows, columns = self.a.shape
        plan = [(0, 0, rows, 0, 0, 0), (1, 0, rows, 0, rows, rows), (2, 0, rows, 1, 0, 0), (3, 0, rows, 1, rows, rows)]
        first_a, first_b = self.first
        return copies(self.core, plan, [(2 * rows, columns)] * 2, self.a, first_a, self.b, first_b)

    def take(self, step, got):
        if step % 2:
            self.first = got
            return
        rows, columns = self.a.shape
        plan = []
        for half in range(2):
            base = half * 4 * rows if step == 4 else 0
            target = 0 if step == 4 else half
            for source, low, at, at_second in ((0, 0, 0, 0), (1, 0, 1, 2), (2, 0, 2, 1), (2, rows, 3, 3)):
                plan.append((half * 3 + source, low, rows, target, base + at * rows, base + at_second * rows))
        shapes = [(8 * rows, columns)] if step == 4 else [(4 * rows, columns)] * 2
        outs = copies(
            self.core, plan, shapes, self.a, self.first[0], got[0], self.b, self.first[1], got[1]
        )
        if step == 4:
            self.all = outs[0]
        else:
            self.a, self.b = outs


def gather_step(step, a, b):
    axes = ("x", "z") if step < 3 else ("z", "x")
    return swap_pair(a, b, *axes, 1 - step % 2)


def scatter_step(step, a, b):
    axes = ("z", "x") if step < 3 else ("x", "z")
    return swap_pair(a, b, *axes, step % 2)


class Scatter:
    def __init__(self, core, parts):
        self.core, self.parts = core, parts
        self.width = sum(right.shape[1] for _, right in parts)

    def call(self, kernel, blocks, extras, extra_specs, outs, out_specs, scratch=()):
        tokens = self.parts[0][0].shape[0]
        count = len(self.parts)
        core = self.core[0]
        index = jnp.stack([core * 0 + low + core * (high - low) for low, high in blocks]).astype(jnp.int32)
        index = jnp.concatenate([index, self.core])

        def whole(kernel_refs):
            index_ref, refs = kernel_refs[0], kernel_refs[1:]
            lefts, rights = refs[:count], refs[count : 2 * count]
            value = [
                lax.dot_general(
                    left[...], right[...], (((0,), (0,)), ((), ())), preferred_element_type=F32
                )
                for left, right in zip(lefts, rights)
            ]
            value = value[0] if count == 1 else jnp.concatenate(value, axis=1)
            kernel(index_ref[len(blocks)], value, *refs[2 * count :])

        return pl.pallas_call(
            lambda *refs: whole(refs),
            grid_spec=pltpu.PrefetchScalarGridSpec(
                num_scalar_prefetch=1,
                grid=(len(blocks),),
                in_specs=[pl.BlockSpec((tokens, 256), lambda i, at: (0, at[i])) for _ in self.parts]
                + [pl.BlockSpec(right.shape, lambda i, at: (0, 0)) for _, right in self.parts]
                + extra_specs,
                out_specs=out_specs,
                scratch_shapes=scratch,
            ),
            out_shape=outs,
            compiler_params=pltpu.CompilerParams(vmem_limit_bytes=VMEM_LIMIT),
            cost_estimate=pl.CostEstimate(
                flops=len(blocks) * 512 * tokens * self.width, bytes_accessed=10**7, transcendentals=0
            ),
            name="gradient",
        )(index, *(left for left, _ in self.parts), *(right for _, right in self.parts), *extras)

    def fixed(self, rows, row=0):
        return pl.BlockSpec((rows, self.width), lambda i, at: (row, 0))

    def shape(self, rows, kind=BF):
        return jax.ShapeDtypeStruct((rows, self.width), kind)

    def send1(self):
        def kernel(core, value, a_ref, b_ref):
            step = pl.program_id(0)

            @pl.when(step < 2)
            def _():
                a_ref[...] = value.astype(BF)

            @pl.when(step >= 2)
            def _():
                b_ref[...] = value.astype(BF)

        block = (256, self.width)
        specs = [
            pl.BlockSpec(block, lambda i, at: (jnp.minimum(i, 1), 0)),
            pl.BlockSpec(block, lambda i, at: (jnp.maximum(i - 2, 0), 0)),
        ]
        return self.call(kernel, [(2, 1), (3, 3), (6, 5), (7, 7)], [], [], [self.shape(512)] * 2, specs)

    def send2(self, got):
        self.got = got

        def kernel(core, value, got_a, got_b, a_ref, b_ref):
            for step, got_ref, ref in ((0, got_a, a_ref), (1, got_b, b_ref)):

                @pl.when(pl.program_id(0) == step)
                def _():
                    ref[...] = (value + got_ref[...].astype(F32)).astype(BF)

        return self.call(
            kernel, [(1, 2), (5, 6)], got, [self.fixed(256, 1)] * 2, [self.shape(256)] * 2, [self.fixed(256)] * 2
        )

    def send3(self, last):
        def kernel(core, value, got_a, got_b, last_a, last_b, send_a, send_b, keep_a, keep_b, sum_ref):
            one = pl.ds(pl.multiple_of(BLK + core * BLK, BLK), BLK)
            two = pl.ds(pl.multiple_of(2 * BLK - core * BLK, BLK), BLK)
            for step, got_ref, last_ref, send_ref, keep_ref in (
                (0, got_a, last_a, send_a, keep_a),
                (1, got_b, last_b, send_b, keep_b),
            ):

                @pl.when(pl.program_id(0) == step)
                def _():
                    sum_ref[...] = value + got_ref[...].astype(F32) + last_ref[...].astype(F32)
                    keep_ref[:BLK, :] = sum_ref[:BLK, :]
                    keep_ref[BLK:, :] = sum_ref[one, :]
                    send_ref[:BLK, :] = sum_ref[two, :].astype(BF)
                    send_ref[BLK:, :] = sum_ref[3 * BLK :, :].astype(BF)

        out = self.call(
            kernel,
            [(0, 0), (4, 4)],
            [*self.got, *last],
            [self.fixed(256)] * 4,
            [self.shape(128)] * 2 + [self.shape(128, F32)] * 2,
            [self.fixed(128)] * 4,
            [pltpu.VMEM((256, self.width), F32)],
        )
        self.keep = out[2:]
        return out[:2]

    def send4(self, got):
        self.got = got
        return tuple((self.keep[h][BLK:] + got[h][BLK:].astype(F32)).astype(BF) for h in range(2))

    def finish(self, last):
        return tuple(
            self.keep[h][:BLK] + self.got[h][:BLK].astype(F32) + last[h].astype(F32) for h in range(2)
        )


def order_tokens(value, first, second):
    return jnp.concatenate([value, second[128:], first, second[:128]])


def join_cores(mine):
    other = flip(mine, "core")
    return jnp.concatenate([mine[:256], other[:256], mine[256:], other[256:]])


def apart(lefts, weights, norm=None):
    count = len(lefts)

    def kernel(*refs):
        value = sum(
            lax.dot_general(left[...], weight[...], (((1,), (1,)), ((), ())), preferred_element_type=F32)
            for left, weight in zip(refs[:count], refs[count : 2 * count])
        )
        refs = refs[2 * count :]
        if norm is not None:
            tokens, average, inverse = refs[:3]
            refs = refs[3:]
            standard = (tokens[...].astype(F32) - average[...]) * inverse[...]
            refs[2][...] = jnp.sum(value * standard, axis=0, keepdims=True)
            refs[3][...] = jnp.sum(value, axis=0, keepdims=True)
        near, away = refs[:2]
        for ref, at in ((near, 0), (away, 256)):
            ref[:128, :] = value[at : at + 128].astype(BF)
            ref[128:384, :] = value[at + 512 : at + 768].astype(BF)
            ref[384:, :] = value[at + 128 : at + 256].astype(BF)

    width = 512
    column = pl.BlockSpec((1024, 1), lambda i: (0, 0))
    row = pl.BlockSpec((1, width), lambda i: (0, i))
    flops = sum(2 * left.shape[0] * left.shape[1] * D for left in lefts)
    return pl.pallas_call(
        kernel,
        grid=(D // width,),
        in_specs=[pl.BlockSpec(left.shape, lambda i: (0, 0)) for left in lefts]
        + [
            pl.BlockSpec((width, left.shape[1]), lambda i, at=at: (i, at))
            for left, (_, at) in zip(lefts, weights)
        ]
        + ([] if norm is None else [pl.BlockSpec((1024, width), lambda i: (0, i)), column, column]),
        out_specs=[pl.BlockSpec((512, width), lambda i: (0, i))] * 2 + ([] if norm is None else [row] * 2),
        out_shape=[jax.ShapeDtypeStruct((512, D), BF)] * 2
        + ([] if norm is None else [jax.ShapeDtypeStruct((1, D), F32)] * 2),
        compiler_params=pltpu.CompilerParams(vmem_limit_bytes=VMEM_LIMIT),
        cost_estimate=pl.CostEstimate(flops=flops, bytes_accessed=2 * 10**7, transcendentals=0),
        name="apart",
    )(*lefts, *(weight for weight, _ in weights), *(norm or ()))


def scatter_tokens(near, away):
    total = near.astype(F32) + flip(away, "core").astype(F32)
    back = swap_y(total[256:].astype(BF), 1).astype(F32)
    last = swap_y((total[128:256] + back[128:]).astype(BF), 0).astype(F32)
    return total[:128] + back[:128] + last


SMALL_STEPS = (
    ("core", 1, 1),
    ("y_hi", 1, 2),
    ("z", 1, 4),
    ("z", 3, 12),
    ("x", 1, 16),
    ("x", 3, 48),
    ("y_lo", 1, 64),
)


def small_step(rows, step):
    axis, mask, _ = SMALL_STEPS[step]
    got = flip(rows, axis) if axis in ("core", "y_hi", "y_lo") else flip4(rows, axis, mask)
    return jnp.concatenate([rows, got])


def small_offsets():
    offsets = [0]
    for _, _, bits in SMALL_STEPS:
        offsets = offsets + [o ^ bits for o in offsets]
    return offsets


def onehot(rows, columns):
    return (rows[:, None] == columns[None, :]).astype(BF)


def doc_positions(segments):
    length = segments.shape[0]
    places = jnp.arange(length, dtype=jnp.int32)
    boundary = jnp.concatenate([jnp.ones((1,), dtype=jnp.bool_), segments[1:] != segments[:-1]])
    doc_start = lax.cummax(jnp.where(boundary, places, jnp.zeros_like(places)), axis=0)
    return places - doc_start


def rotary_tables(positions):
    lane = jnp.arange(128, dtype=jnp.int32) % HD
    half_rot = ROT // 2
    frequency = 10000.0 ** (-(2.0 * (lane % half_rot).astype(F32)) / ROT)
    angles = positions.astype(F32)[:, None] * jnp.where(lane < ROT, frequency, 0.0)
    sine = jnp.sin(angles)
    before = jnp.where(lane < half_rot, -sine, 0.0)
    after = jnp.where((lane >= half_rot) & (lane < ROT), sine, 0.0)
    return jnp.concatenate([jnp.cos(angles), before, after], axis=1)


def pick_blocks(value, blocks, size):
    return jnp.concatenate([lax.dynamic_slice_in_dim(value, b * size, size, 0) for b in blocks])


def attention_kernel(
    proj_ref, shift_ref, table_ref, column_ref, row_ref, d_out_ref, mixed_ref, d_proj_ref, sums_ref, mask_ref
):
    start, last = column_ref[:, 0:1], column_ref[:, 1:2]
    where = row_ref[0]
    mask_ref[...] = jnp.where((where >= start) & (where <= last), 0.0, MASKED)
    cosine, before, after = (table_ref[:, i * 128 : (i + 1) * 128] for i in range(3))
    lane = lax.broadcasted_iota(jnp.int32, (SEQ, 128), 1)

    def turn(value, sign):
        shifted = pltpu.roll(value, 112, 1) * before + pltpu.roll(value, 16, 1) * after
        return value * cosine + sign * shifted

    def part(index, pair):
        at = slice(index * 256 + pair * 128, index * 256 + pair * 128 + 128)
        return proj_ref[:, at] + shift_ref[:, at]

    def dot(a, b, dims):
        return lax.dot_general(a, b, (dims, ((), ())), preferred_element_type=F32)

    for pair in range(2):
        at = slice(pair * 128, pair * 128 + 128)
        queries = (turn(part(0, pair), 1.0).astype(BF).astype(F32) * HD**-0.5).astype(BF)
        keys = turn(part(1, pair), 1.0).astype(BF)
        values = part(2, pair).astype(BF)
        d_out = d_out_ref[:, at]
        results = []
        for head in range(2):
            own = (lane >= head * HD) & (lane < (head + 1) * HD)
            own_queries = jnp.where(own, queries, jnp.zeros_like(queries))
            own_d_out = jnp.where(own, d_out, jnp.zeros_like(d_out))
            scores = dot(own_queries, keys, ((1,), (1,))) + mask_ref[...]
            exponent = jnp.exp(scores - jnp.max(scores, axis=1, keepdims=True))
            soft = exponent * (1.0 / jnp.sum(exponent, axis=1, keepdims=True))
            soft_low = soft.astype(BF)
            mixed = dot(soft_low, values, ((1,), (0,)))
            d_soft = dot(own_d_out, values, ((1,), (1,)))
            inner = jnp.sum(soft * d_soft, axis=1, keepdims=True)
            d_scores = (soft * (d_soft - inner)).astype(BF)
            d_queries = dot(d_scores, keys, ((1,), (0,))) * HD**-0.5
            d_keys = dot(d_scores, own_queries, ((0,), (0,)))
            d_values = dot(soft_low, own_d_out, ((0,), (0,)))
            results.append((mixed, d_queries, d_keys, d_values))
        first, second = results
        mixed_ref[:, at] = jnp.where(lane < HD, first[0], second[0]).astype(BF)
        d_queries = turn(jnp.where(lane < HD, first[1], second[1]), -1.0).astype(BF)
        d_keys = turn(first[2] + second[2], -1.0).astype(BF)
        d_values = (first[3] + second[3]).astype(BF)
        for index, value in enumerate((d_queries, d_keys, d_values)):
            at = slice(index * 256 + pair * 128, index * 256 + pair * 128 + 128)
            d_proj_ref[:, at] = value
            sums_ref[0, :, at] = jnp.sum(value.astype(F32), axis=0, keepdims=True)


def attention(projected, shift, tables, columns, rows, d_attended):
    count = projected.shape[0] // SEQ
    return pl.pallas_call(
        attention_kernel,
        grid=(count,),
        in_specs=[
            pl.BlockSpec((SEQ, 768), lambda i: (i, 0)),
            pl.BlockSpec((1, 768), lambda i: (0, 0)),
            pl.BlockSpec((SEQ, 384), lambda i: (i, 0)),
            pl.BlockSpec((SEQ, 2), lambda i: (i, 0)),
            pl.BlockSpec((1, 1, SEQ), lambda i: (i, 0, 0)),
            pl.BlockSpec((SEQ, 256), lambda i: (i, 0)),
        ],
        out_specs=[
            pl.BlockSpec((SEQ, 256), lambda i: (i, 0)),
            pl.BlockSpec((SEQ, 768), lambda i: (i, 0)),
            pl.BlockSpec((1, 1, 768), lambda i: (i, 0, 0)),
        ],
        out_shape=[
            jax.ShapeDtypeStruct((count * SEQ, 256), BF),
            jax.ShapeDtypeStruct((count * SEQ, 768), BF),
            jax.ShapeDtypeStruct((count, 1, 768), F32),
        ],
        scratch_shapes=[pltpu.VMEM((SEQ, SEQ), F32)],
        compiler_params=pltpu.CompilerParams(vmem_limit_bytes=VMEM_LIMIT),
        cost_estimate=pl.CostEstimate(flops=count * 8 * 10**9, bytes_accessed=10**7, transcendentals=count * 10**6),
        name="attention",
    )(projected, shift, tables, columns, rows, d_attended)


def body(
    residual_in,
    segment_ids,
    out_grad,
    ln_gain,
    ln_bias,
    w_qkv,
    b_qkv,
    w_out,
    b_attn_out,
    w_up,
    b_up,
    w_down,
    b_mlp_out,
):
    y_lo, x, z, y_hi, core = (lax.axis_index(name) for name in AXES)
    core_id = core[None].astype(jnp.int32)
    low = y_lo == 0
    me = (((y_lo * 4 + x) * 4 + z) * 2 + y_hi) * 2 + core

    place = jnp.arange(D, dtype=jnp.int32)
    block, within = place // BLK, place % BLK
    rel_y, outer, inner = block // 16, (block % 16) // 4, block % 4
    outer, inner = outer ^ (outer >> 1), inner ^ (inner >> 1)
    rel_x = jnp.where(rel_y == 0, inner, outer)
    rel_z = jnp.where(rel_y == 0, outer, inner)
    natural = ((rel_y * 4 + (x ^ rel_x)) * 4 + (z ^ rel_z)) * BLK + within
    to_rel = onehot(place, natural)

    both = jnp.dot(jnp.concatenate([residual_in, out_grad]), to_rel, preferred_element_type=F32)
    residual = both[:128].astype(BF)
    gradient = both[128:].astype(BF)

    def halves(value, size):
        lower, upper = value[..., :size], value[..., size:]
        return jnp.where(low, lower, upper), jnp.where(low, upper, lower)

    up_own, up_away = halves(w_up, 1024)
    qkv_own, qkv_away = halves(w_qkv, 256)
    out_own, out_away = halves(w_out.T, 256)
    down_own, down_away = halves(w_down.T, 1024)
    attn_own = jnp.concatenate([qkv_own.reshape(BLK, 768), out_own], axis=1)
    attn_away = jnp.concatenate([qkv_away.reshape(BLK, 768), out_away], axis=1)
    small = jnp.concatenate(
        [
            ln_gain,
            ln_bias,
            b_attn_out,
            b_mlp_out,
            b_up.reshape(64),
            b_qkv.reshape(48),
            jnp.zeros((80,), BF),
        ]
    )[None]

    attn_got, rest_got = flip(attn_away, "y_lo"), flip(jnp.concatenate([up_away, down_away], axis=1), "y_lo")
    small = small_step(small, 0)
    attn_got, rest_got, residual, gradient, small = bar((attn_got, rest_got, residual, gradient, small))

    def by_row(own, got):
        return Gather(core_id, jnp.where(low, own, got), jnp.where(low, got, own))

    attn_gather = by_row(attn_own, attn_got)
    up_gather = by_row(up_own, rest_got[:, :1024])
    down_gather = by_row(down_own, rest_got[:, 1024:])

    token_first = swap_y(residual, 0)
    small = small_step(small, 1)
    got, small = bar((gather_step(1, *attn_gather.send(1)), small))
    attn_gather.take(1, got)
    small = small_step(small, 2)
    got, token_first, small = bar((gather_step(2, *attn_gather.send(2)), token_first, small))
    attn_gather.take(2, got)
    token_second = swap_y(jnp.concatenate([residual, token_first]), 1)
    small = small_step(small, 3)
    got, gradient, small = bar((gather_step(3, *attn_gather.send(3)), gradient, small))
    attn_gather.take(3, got)
    grad_first = swap_y(gradient, 0)
    small = small_step(small, 4)
    sends = up_gather.send(1)
    got, sends, token_second, grad_first, small = bar(
        (gather_step(4, *attn_gather.send(4)), sends, token_second, grad_first, small)
    )
    attn_gather.take(4, got)
    attn_all = attn_gather.all
    up_got = gather_step(1, *sends)
    grad_second = swap_y(jnp.concatenate([gradient, grad_first]), 1)
    tokens = join_cores(order_tokens(residual, token_first, token_second))
    small = small_step(small_step(small, 5), 6)
    tokens, up_got, small = bar((tokens, up_got, small))
    up_gather.take(1, up_got)

    owners = me ^ jnp.array(small_offsets(), dtype=jnp.int32)
    ids = jnp.arange(128, dtype=jnp.int32)
    mates = (y_lo * 16 + jnp.arange(16, dtype=jnp.int32)) * 4 + y_hi * 2 + core
    sorted_table = jnp.dot(
        onehot(jnp.concatenate([ids, mates]), owners), small, preferred_element_type=F32
    ).astype(BF)
    vectors = sorted_table[:128, :64].reshape(128, 4, 16).transpose(1, 0, 2).reshape(4, D)
    vectors = jnp.dot(vectors, to_rel, preferred_element_type=F32)
    gain, shift, out_shift = vectors[0], vectors[1], vectors[2] + vectors[3]
    up_shift = sorted_table[128:, 64:128].reshape(1024).astype(F32)
    qkv_shift = sorted_table[128:, 128:176].reshape(16, 3, 16).transpose(1, 0, 2).reshape(1, 768)
    qkv_shift = qkv_shift.astype(F32)

    near_blocks = [y_hi * 2 + core, (1 - y_hi) * 2 + core, y_hi * 2 + 1 - core, (1 - y_hi) * 2 + 1 - core]
    far_first, far_second = y_hi ^ core, y_hi ^ (1 - core)
    far_blocks = [far_first * 2 + core, far_second * 2 + core, far_second * 2 + 1 - core, far_first * 2 + 1 - core]
    far_segments = flip(segment_ids, "y_lo")
    places = jnp.arange(SEQ, dtype=jnp.int32)
    packed = jnp.concatenate(
        [
            pick_blocks(jnp.stack([places - doc_positions(s), places], axis=1), blocks, 128)
            for s, blocks in ((segment_ids, near_blocks), (far_segments, far_blocks))
        ]
    )
    rows = packed[:, 1].reshape(2, 1, SEQ)
    tables = rotary_tables(packed[:, 1] - packed[:, 0])

    up_got = gather_step(2, *up_gather.send(2))
    token_rows = tokens.astype(F32)
    average = jnp.mean(token_rows, axis=-1, keepdims=True)
    centred = token_rows - average
    variance = jnp.mean(centred * centred, axis=-1, keepdims=True)
    inverse = lax.rsqrt(variance + EPS)
    normed = (centred * inverse * gain + shift).astype(BF)
    normed, grad_second, up_got = bar((normed, grad_second, up_got))

    up_gather.take(2, up_got)
    up_got = gather_step(3, *up_gather.send(3))
    grad_all = join_cores(order_tokens(gradient, grad_first, grad_second))
    projected = jnp.dot(normed, attn_all[:, :768], preferred_element_type=F32)
    projected, grad_all, sends = bar((projected, grad_all, down_gather.send(1)))
    down_got = gather_step(1, *sends)
    d_attended = jnp.dot(grad_all, attn_all[:, 768:], preferred_element_type=F32).astype(BF)
    projected, d_attended, up_got, down_got = bar((projected, d_attended, up_got, down_got))

    up_gather.take(3, up_got)
    down_gather.take(1, down_got)
    up_got = gather_step(4, *up_gather.send(4))
    down_got = gather_step(2, *down_gather.send(2))
    first = attention(projected[:SEQ], qkv_shift, tables[:SEQ], packed[:SEQ], rows[:1], d_attended[:SEQ])
    first, down_got, projected, d_attended = bar((first, down_got, projected, d_attended))
    down_gather.take(2, down_got)
    down_got = gather_step(3, *down_gather.send(3))
    second = attention(projected[SEQ:], qkv_shift, tables[SEQ:], packed[SEQ:], rows[1:], d_attended[SEQ:])
    mixed, d_projected, sums = (jnp.concatenate(pair) for pair in zip(first, second))
    attn_sum = Scatter(core_id, [(normed, d_projected), (grad_all, mixed)])
    sends, up_got, normed, down_got = bar((attn_sum.send1(), up_got, normed, down_got))

    got = scatter_step(1, *sends)
    up_gather.take(4, up_got)
    up_all = up_gather.all
    down_gather.take(3, down_got)
    down_sends = down_gather.send(4)
    hidden_pre = jnp.dot(normed, up_all, preferred_element_type=F32) + up_shift
    hidden_low = jax.nn.gelu(hidden_pre, approximate=True).astype(BF)
    got, hidden_low, down_sends = bar((got, hidden_low, down_sends))
    down_got = gather_step(4, *down_sends)
    down_sum = Scatter(core_id, [(grad_all, hidden_low)])
    sends = down_sum.send1()
    attn_sends = attn_sum.send2(got)
    attn_sends, sends, down_got, hidden_pre, grad_all = bar((attn_sends, sends, down_got, hidden_pre, grad_all))

    down_gather.take(4, down_got)
    down_all = down_gather.all
    got = scatter_step(2, *attn_sends)
    down_got = scatter_step(1, *sends)
    d_hidden_raw = jnp.dot(grad_all, down_all, preferred_element_type=F32)
    _, gelu_back = jax.vjp(lambda u: jax.nn.gelu(u, approximate=True), hidden_pre)
    d_hidden = gelu_back(d_hidden_raw)[0].astype(BF)
    got, down_got, d_hidden = bar((got, down_got, d_hidden))
    up_sum = Scatter(core_id, [(normed, d_hidden)])
    up_sends = up_sum.send1()
    attn_sends = attn_sum.send3(got)
    down_sends = down_sum.send2(down_got)
    up_sends, attn_sends, down_sends, d_hidden = bar((up_sends, attn_sends, down_sends, d_hidden))

    up_got = scatter_step(1, *up_sends)
    got = scatter_step(3, *attn_sends)
    d_near, d_away, gain_part, shift_part = apart(
        [d_projected, d_hidden], [(attn_all, 0), (up_all, 0)], (tokens, average, inverse)
    )
    d_near, d_away, up_got, got, down_sends, hidden_low = bar(
        (d_near, d_away, up_got, got, down_sends, hidden_low)
    )
    d_got = flip(d_away, "core")
    down_got = scatter_step(2, *down_sends)
    got = scatter_step(4, *attn_sum.send4(got))
    up_sends = up_sum.send2(up_got)
    near, away = apart([mixed, hidden_low], [(attn_all, 3), (down_all, 0)])
    near, away, d_got, down_got, got, up_sends = bar((near, away, d_got, down_got, got, up_sends))

    attn_a, attn_b = attn_sum.finish(got)
    up_got = scatter_step(2, *up_sends)
    d_total = d_near.astype(F32) + d_got.astype(F32)
    d_back = swap_y(d_total[256:].astype(BF), 1)
    down_sends = down_sum.send3(down_got)
    up_got, d_back, down_sends = bar((up_got, d_back, down_sends))
    down_got = scatter_step(3, *down_sends)
    d_last = swap_y((d_total[128:256] + d_back[128:].astype(F32)).astype(BF), 0)
    got = flip(away, "core")
    up_sends = up_sum.send3(up_got)
    down_got, d_last, got, up_sends = bar((down_got, d_last, got, up_sends))
    d_normed = d_total[:128] + d_back[:128].astype(F32) + d_last.astype(F32)
    up_got = scatter_step(3, *up_sends)
    total = near.astype(F32) + got.astype(F32)
    back = swap_y(total[256:].astype(BF), 1)
    down_got = scatter_step(4, *down_sum.send4(down_got))
    up_got, back, down_got = bar((up_got, back, down_got))
    up_got = scatter_step(4, *up_sum.send4(up_got))
    last = swap_y((total[128:256] + back[128:].astype(F32)).astype(BF), 0)
    down_a, down_b = down_sum.finish(down_got)
    up_a, up_b = up_sum.finish(up_got)
    branch = total[:128] + back[:128].astype(F32) + last.astype(F32)
    output = residual.astype(F32) + branch + out_shift

    out_shift_part = jnp.sum(gradient.astype(F32), axis=0)
    local = residual.astype(F32)
    local = local - jnp.mean(local, axis=-1, keepdims=True)
    scale = lax.rsqrt(jnp.mean(local * local, axis=-1, keepdims=True) + EPS)
    local = local * scale
    d_standard = d_normed * gain
    mean_plain = jnp.mean(d_standard, axis=-1, keepdims=True)
    mean_cross = jnp.mean(d_standard * local, axis=-1, keepdims=True)
    grad_in = gradient.astype(F32) + scale * (d_standard - mean_plain - local * mean_cross)

    def to_natural(value):
        return lax.dot_general(value, to_rel, (((1,), (1,)), ((), ())), preferred_element_type=F32)

    output = to_natural(output.astype(BF)).astype(BF)
    grad_high = grad_in.astype(BF)
    grad_low = (grad_in - grad_high.astype(F32)).astype(BF)
    grad_in = to_natural(jnp.concatenate([grad_high, grad_low]))
    grad_in = grad_in[:128] + grad_in[128:]

    up_shift_part = jnp.sum(d_hidden.astype(F32), axis=0)
    qkv_shift_part = jnp.sum(sums, axis=(0, 1))
    rel = jnp.stack([gain_part[0], shift_part[0], out_shift_part]).reshape(3, 2, 4, 4, BLK)
    rel = jnp.stack([rel[:, 0].swapaxes(1, 2), rel[:, 1]], axis=1)
    rel = rel.transpose(2, 3, 0, 1, 4).reshape(4, 4, 384)
    plain = jnp.concatenate(
        [
            up_shift_part.reshape(4, 4, 64),
            qkv_shift_part.reshape(3, 4, 4, 16).transpose(1, 2, 0, 3).reshape(4, 4, 48),
            jnp.zeros((4, 4, 16), F32),
        ],
        axis=-1,
    )
    plain = jnp.stack([lax.dynamic_index_in_dim(plain, x ^ k, 0, False) for k in ORDER])
    plain = jnp.stack([lax.dynamic_index_in_dim(plain, z ^ k, 1, False) for k in ORDER], axis=1)
    small = jnp.concatenate([rel, plain], axis=-1)
    for axis in ("x", "z"):
        got = flip4(small[2:], axis, 3)
        small = small[:2] + got
        small = small[0] + flip4(small[1], axis, 1)
    plain = small[384:]
    mine = small[:384]
    for axis, index in (("y_lo", y_lo), ("y_hi", y_hi), ("core", core)):
        mine = mine.reshape(3, 2, -1)
        keep = jnp.where(index == 0, mine[:, 0], mine[:, 1])
        away = jnp.where(index == 0, mine[:, 1], mine[:, 0])
        mine = keep + flip(away, axis)
    grad_gain, grad_shift, grad_out_shift = mine[0], mine[1], mine[2]
    grad_up_shift = plain[:64].reshape(1, 64)
    grad_qkv_shift = plain[64:112].reshape(3, 1, 16)

    def whole(a, b):
        own, got = jnp.where(low, a, b), flip(jnp.where(low, b, a), "y_lo")
        return jnp.where(low, own, got), jnp.where(low, got, own)

    sum_down = jnp.concatenate(whole(down_a, down_b), axis=1).T
    sum_up = jnp.concatenate(whole(up_a, up_b), axis=1)
    lower, upper = whole(attn_a, attn_b)
    sum_qkv = jnp.concatenate(
        [lower[:, :768].reshape(BLK, 3, 256), upper[:, :768].reshape(BLK, 3, 256)], axis=2
    )
    sum_out = jnp.concatenate([lower[:, 768:], upper[:, 768:]], axis=1).T
    return (
        output,
        grad_in,
        grad_gain,
        grad_shift,
        sum_qkv,
        grad_qkv_shift,
        sum_out,
        grad_out_shift,
        sum_up,
        grad_up_shift,
        sum_down,
        grad_out_shift,
    )


def solution(mesh):
    fine = Mesh(mesh.devices.reshape(2, 4, 4, 2, 2), AXES)
    dp = ("y_lo", "x", "z")
    tensor = ("y_hi", "core")
    every = AXES
    in_specs = (
        P(every, None),
        P(dp),
        P(every, None),
        P(every),
        P(every),
        P(dp, None, tensor),
        P(None, tensor, dp),
        P(tensor, dp),
        P(every),
        P(dp, tensor),
        P(tensor, dp),
        P(tensor, dp),
        P(every),
    )
    out_specs = (
        P(every, None),
        P(every, None),
        P(every),
        P(every),
        P(dp, None, tensor),
        P(None, tensor, dp),
        P(tensor, dp),
        P(every),
        P(dp, tensor),
        P(tensor, dp),
        P(tensor, dp),
        P(every),
    )
    return jax.shard_map(body, mesh=fine, in_specs=in_specs, out_specs=out_specs, check_vma=False)
```

```python
import jax
import jax.numpy as jnp
from jax import lax
from jax.experimental import pallas as pl
from jax.experimental.pallas import tpu as pltpu
from jax.sharding import Mesh, PartitionSpec as P

HD = 64
ROT = 32
EPS = 1e-05
MASKED = -1e30
D = 2048
SEQ = 512
TOK = 128
BLK = 64
VMEM_LIMIT = 32 * 1024 * 1024
BF = jnp.bfloat16
F32 = jnp.float32
AXES = ("y_lo", "x", "z", "y_hi", "core")


bar = lax.optimization_barrier


def params(limit=VMEM_LIMIT):
    return pltpu.CompilerParams(vmem_limit_bytes=limit)


def cost():
    return pl.CostEstimate(flops=1000, bytes_accessed=1000, transcendentals=0)


def like(rows, columns, kind=BF):
    return pltpu.HBM((rows, columns), kind)


def in_hbm(*values):
    return tuple(pltpu.with_memory_space_constraint(value, pltpu.HBM) for value in values)


SMEM = pl.BlockSpec(memory_space=pltpu.SMEM)
VMEM = pl.BlockSpec(memory_space=pltpu.VMEM)
ANY = pl.BlockSpec(memory_space=pl.ANY)


def ring(value, axis, step):
    masks = (1, 3) if step == 0 else (3, 1)
    table = [(i * 2 + c, (i ^ masks[c]) * 2 + c) for i in range(4) for c in range(2)]
    return lax.ppermute(value, (axis, "core"), table)


def ring_pair(pair, axes, step):
    pair = bar(tuple(pair))
    return bar(tuple(ring(value, axis, step) for value, axis in zip(pair, axes)))


def swap_y(value, step):
    masks = (1, 3) if step == 0 else (3, 1)

    def place(y, c):
        return ((y % 2) * 2 + y // 2) * 2 + c

    table = [(place(y, c), place(y ^ masks[c], c)) for y in range(4) for c in range(2)]
    return lax.ppermute(value, ("y_lo", "y_hi", "core"), table)


def flip(value, axis):
    return lax.ppermute(value, axis, [(0, 1), (1, 0)])


def flip4(value, axis, mask):
    return lax.ppermute(value, axis, [(i, i ^ mask) for i in range(4)])


RING_STEPS = (("z", 1, 1), ("z", 3, 3), ("x", 1, 4), ("x", 3, 12))


def copies(places, plan, shapes, sources):
    count = len(sources)

    def kernel(places_ref, *refs):
        inputs, outputs, refs = refs[:count], refs[count : count + len(shapes)], refs[count + len(shapes) :]
        stages, sems = refs[: len(shapes)], refs[-1]
        moves = []
        for i, (source, row, rows, column, columns, target, to, place, unit, across) in enumerate(plan):
            if place is not None:
                to = pl.multiple_of(to + places_ref[place] * unit, rows)
            at = (pl.ds(to, rows), pl.ds(across, columns))
            stage = stages[target].at[at]
            arrive = pltpu.make_async_copy(
                inputs[source].at[pl.ds(row, rows), pl.ds(column, columns)], stage, sems.at[0, i]
            )
            arrive.start()
            moves.append((arrive, pltpu.make_async_copy(stage, outputs[target].at[at], sems.at[1, i])))
        for arrive, leave in moves:
            arrive.wait()
            leave.start()
        for _, leave in moves:
            leave.wait()

    return pl.pallas_call(
        kernel,
        in_specs=[SMEM] + [ANY] * count,
        out_specs=[ANY] * len(shapes),
        out_shape=[like(*shape) for shape in shapes],
        scratch_shapes=[pltpu.VMEM(shape, BF) for shape in shapes] + [pltpu.SemaphoreType.DMA((2, len(plan)))],
        compiler_params=params(),
        cost_estimate=cost(),
        name="put_together",
    )(places, *in_hbm(*sources))


class Gather:
    def __init__(self, places, left, right):
        self.places, self.pair = places, (left, right)

    def send(self, step):
        if step % 2:
            return self.pair
        rows, width = self.pair[0].shape
        plan = [
            (2 * h + k, 0, rows, 0, width, h, k * rows, None, 0, 0) for h in range(2) for k in range(2)
        ]
        sources = [value for both in zip(self.pair, self.first) for value in both]
        return copies(self.places, plan, [(2 * rows, width)] * 2, sources)

    def take(self, step, got):
        if step % 2:
            self.first = got
            return
        rows, width = self.pair[0].shape
        sources = [value for each in zip(self.pair, self.first, got) for value in each]
        plan = []
        for h in range(2):
            for k, (source, row) in enumerate(((0, 0), (1, 0), (2, 0), (2, rows))):
                source += 3 * h
                if step == 2:
                    plan.append((source, row, rows, 0, width, h, 0, 4 * h + k, rows, 0))
                    continue
                for i in range(4):
                    to, unit = ((i * 512, 128), (i * 128, 512))[h]
                    plan.append(
                        (source, row + i * 128, 128, 0, width, 0, to, 4 * (1 - h) + k, unit, h * width)
                    )
        shapes = [(4 * rows, width)] * 2 if step == 2 else [(4 * rows, 2 * width)]
        self.pair = copies(self.places, plan, shapes, sources)
        self.all = self.pair[0]


def gather_step(step, pair):
    return ring_pair(pair, ("x", "z") if step < 3 else ("z", "x"), 1 - step % 2)


def scatter_step(step, pair):
    return ring_pair(pair, ("x", "z") if step < 3 else ("z", "x"), step % 2)


class Scatter:
    def __init__(self, places, left, right):
        self.places = places
        tokens, width = right.shape
        self.width = half = width // 2

        def kernel(places_ref, left_ref, right_ref, *refs):
            outs, (lefts, rights, *stages), sems = refs[:6], refs[6:-1], refs[-1]
            fetch = [pltpu.make_async_copy(right_ref, rights, sems.at[0])]
            order = [2, 3, 1, 0]
            for i, k in enumerate(order):
                at = pl.ds(pl.multiple_of(places_ref[k] * 512, 512), 512)
                fetch.append(pltpu.make_async_copy(left_ref.at[:, at], lefts.at[:, at], sems.at[1 + i]))
            for copy in fetch:
                copy.start()
            fetch[0].wait()
            stored = []
            for h in range(2):
                for i, k in enumerate(order):
                    if h == 0:
                        fetch[1 + i].wait()
                        block = lefts[:, pl.ds(pl.multiple_of(places_ref[k] * 512, 512), 512)]
                    else:
                        z = places_ref[4 + k]
                        block = jnp.concatenate(
                            [lefts[:, pl.ds(pl.multiple_of(n * 512 + z * 128, 128), 128)] for n in range(4)], axis=1
                        )
                    value = lax.dot_general(
                        block,
                        rights[:, h * half : (h + 1) * half],
                        (((0,), (0,)), ((), ())),
                        preferred_element_type=F32,
                    ).astype(BF)
                    stage = stages[h].at[pl.ds(i * 512, 512)]
                    stage[...] = value
                    out = outs[h].at[pl.ds(i * 512, 512)] if i < 2 else outs[2 * i - 2 + h]
                    copy = pltpu.make_async_copy(stage, out, sems.at[5 + 4 * h + i])
                    copy.start()
                    stored.append(copy)
            for copy in stored:
                copy.wait()

        outs = pl.pallas_call(
            kernel,
            in_specs=[SMEM, ANY, ANY],
            out_specs=[ANY] * 6,
            out_shape=[like(1024, half)] * 2 + [like(512, half)] * 4,
            scratch_shapes=[
                pltpu.VMEM((tokens, D), BF),
                pltpu.VMEM((tokens, width), BF),
                pltpu.VMEM((2048, half), BF),
                pltpu.VMEM((2048, half), BF),
                pltpu.SemaphoreType.DMA((13,)),
            ],
            compiler_params=params(),
            cost_estimate=cost(),
            name="gradient",
        )(places, *in_hbm(left, right))
        self.first, self.next, self.keep = outs[:2], outs[2:4], outs[4:]

    def call(self, kernel, inputs, outs, scratch=(), steps=2):
        inputs = [value if isinstance(value, tuple) else (value, value.shape[0], 0) for value in inputs]
        return pl.pallas_call(
            kernel,
            grid=(steps,),
            in_specs=[SMEM]
            + [
                pl.BlockSpec((rows, value.shape[1] // steps), lambda i, at=at: (at, i)) for value, rows, at in inputs
            ],
            out_specs=[pl.BlockSpec((rows, columns // steps), lambda i: (0, i)) for rows, columns, _ in outs],
            out_shape=[like(*shape) for shape in outs],
            scratch_shapes=scratch,
            compiler_params=params(),
            cost_estimate=cost(),
            name="add",
        )(self.places, *in_hbm(*(value for value, _, _ in inputs)))

    def send2(self, got):
        self.got = got

        def kernel(places_ref, *refs):
            for h in range(2):
                refs[4 + h][...] = (refs[h][...].astype(F32) + refs[2 + h][...].astype(F32)).astype(BF)

        return self.call(
            kernel, [*self.next, *((value, 512, 1) for value in got)], [(512, self.width, BF)] * 2
        )

    def send3(self, last):
        def kernel(places_ref, *refs):
            total = refs[-1]
            for h in range(2):
                keep, arrived, later, send, own = (refs[2 * k + h] for k in range(5))
                total[...] = keep[...].astype(F32) + arrived[...].astype(F32) + later[...].astype(F32)
                own_at, first, second, across = (
                    pl.ds(pl.multiple_of(places_ref[4 * (1 - h) + k] * 128, 128), 128) for k in range(4)
                )
                send[:128, :] = total[second, :].astype(BF)
                send[128:, :] = total[across, :].astype(BF)
                own[:128, :] = total[first, :]
                own[128:, :] = total[own_at, :]

        outs = self.call(
            kernel,
            [*self.keep, *((value, 512, 0) for value in self.got), *last],
            [(256, self.width, BF)] * 2 + [(256, self.width, F32)] * 2,
            [pltpu.VMEM((512, self.width // 2), F32)],
        )
        self.keep = outs[2:]
        return outs[:2]

    def send4(self, got):
        self.got = got

        def kernel(places_ref, *refs):
            for h in range(2):
                refs[4 + h][...] = (refs[h][...] + refs[2 + h][...].astype(F32)).astype(BF)

        return self.call(
            kernel,
            [*((value, 128, 0) for value in self.keep), *((value, 128, 1) for value in got)],
            [(128, self.width, BF)] * 2,
        )

    def finish(self, last):
        def kernel(places_ref, *refs):
            total, width = refs[-1], self.width
            for h in range(2):
                keep, arrived, later = (refs[2 * k + h] for k in range(3))
                total[:, h * width : (h + 1) * width] = (
                    keep[...] + arrived[...].astype(F32) + later[...].astype(F32)
                )
            low = places_ref[8]
            refs[6][...] = total[pl.ds(pl.multiple_of(low * BLK, BLK), BLK), :]
            refs[7][...] = total[pl.ds(pl.multiple_of((1 - low) * BLK, BLK), BLK), :].astype(BF)

        return self.call(
            kernel,
            [*((value, 128, 1) for value in self.keep), *((value, 128, 0) for value in self.got), *last],
            [(BLK, 2 * self.width, F32), (BLK, 2 * self.width, BF)],
            [pltpu.VMEM((128, 2 * self.width), F32)],
            1,
        )


def attention_gradient(normed, d_projected, gradients, mixed):
    def kernel(normed_ref, d_ref, grad_ref, mixed_ref, out_ref):
        for left, right, at in ((normed_ref, d_ref, slice(0, 768)), (grad_ref, mixed_ref, slice(768, 1024))):
            out_ref[:, at] = lax.dot_general(
                left[...], right[...], (((0,), (0,)), ((), ())), preferred_element_type=F32
            ).astype(BF)

    def fixed(width):
        return pl.BlockSpec((1024, width), lambda i: (0, 0), pipeline_mode=pl.Buffered(1))

    column = pl.BlockSpec((1024, 512), lambda i: (0, i))
    return pl.pallas_call(
        kernel,
        grid=(D // 512,),
        in_specs=[column, fixed(768), column, fixed(256)],
        out_specs=pl.BlockSpec((512, 1024), lambda i: (i, 0)),
        out_shape=like(D, 1024),
        compiler_params=params(),
        cost_estimate=cost(),
        name="attention_gradient",
    )(*in_hbm(normed, d_projected, gradients, mixed))


def whole(low_index, own, got, layout):
    def kernel(low_ref, own_ref, got_ref, *outs):
        at = 0
        for (width, count), out in zip(layout, outs):
            mine = pl.ds(pl.multiple_of(low_ref[0] * width, width), width)
            theirs = pl.ds(pl.multiple_of((1 - low_ref[0]) * width, width), width)
            for i in range(count):
                out[i, :, mine] = own_ref[:, at : at + width].astype(F32)
                out[i, :, theirs] = got_ref[:, at : at + width].astype(F32)
                at += width

    return pl.pallas_call(
        kernel,
        in_specs=[SMEM, VMEM, VMEM],
        out_specs=[VMEM] * len(layout),
        out_shape=[pltpu.HBM((count, BLK, 2 * width), F32) for width, count in layout],
        compiler_params=params(),
        cost_estimate=cost(),
        name="whole",
    )(low_index, *in_hbm(own, got))


def inside(value):
    parts = [value[:, (low * 16 + n) * BLK : (low * 16 + n + 1) * BLK] for n in range(16) for low in range(2)]
    return jnp.concatenate(parts, axis=1)


def outside(value):
    parts = [value[:, (2 * n + low) * BLK : (2 * n + low + 1) * BLK] for low in range(2) for n in range(16)]
    return jnp.concatenate(parts, axis=1)


def prepare(low_index, residual, gradient, w_qkv, w_out, w_up, w_down):
    def kernel(low_ref, residual_ref, gradient_ref, qkv, out, up, down, tokens, grads, attn_own, attn_away, rest_own, rest_away):
        tokens[...] = inside(residual_ref[...])
        grads[...] = inside(gradient_ref[...])
        low = low_ref[0]
        for half, attn, rest in ((low, attn_own, rest_own), (1 - low, attn_away, rest_away)):
            narrow = pl.ds(pl.multiple_of(half * 256, 256), 256)
            wide = pl.ds(pl.multiple_of(half * 1024, 1024), 1024)
            for i in range(3):
                attn[:, i * 256 : (i + 1) * 256] = qkv[i, :, narrow]
            attn[:, 768:] = out[:, narrow]
            rest[:, :1024] = up[:, wide]
            rest[:, 1024:] = down[:, wide]

    return pl.pallas_call(
        kernel,
        in_specs=[SMEM] + [VMEM] * 6,
        out_specs=[VMEM] * 6,
        out_shape=[like(TOK, D)] * 2 + [like(BLK, 1024)] * 2 + [like(BLK, 2048)] * 2,
        compiler_params=params(),
        cost_estimate=cost(),
        name="prepare",
    )(low_index, *in_hbm(residual, gradient, w_qkv, w_out, w_up, w_down))


def norm_and_project(tokens, gain, shift, weights):
    rows = 256

    def kernel(token_ref, gain_ref, shift_ref, weight_ref, normed_ref, mean_ref, inv_ref, proj_ref):
        value = token_ref[...].astype(F32)
        mean = jnp.mean(value, axis=1, keepdims=True)
        value = value - mean
        inverse = lax.rsqrt(jnp.mean(value * value, axis=1, keepdims=True) + EPS)
        normed = (value * inverse * gain_ref[...] + shift_ref[...]).astype(BF)
        normed_ref[...] = normed
        mean_ref[...] = mean
        inv_ref[...] = inverse
        proj_ref[...] = jnp.dot(normed, weight_ref[...].reshape(D, 768), preferred_element_type=F32)

    def by_row(width):
        return pl.BlockSpec((rows, width), lambda i: (i, 0))

    def fixed(*shape):
        return pl.BlockSpec(shape, lambda i: (0,) * len(shape), pipeline_mode=pl.Buffered(1))

    return pl.pallas_call(
        kernel,
        grid=(1024 // rows,),
        in_specs=[by_row(D), fixed(1, D), fixed(1, D), fixed(16, 128, 768)],
        out_specs=[by_row(D), by_row(1), by_row(1), by_row(768)],
        out_shape=[like(1024, D), like(1024, 1, F32), like(1024, 1, F32), like(1024, 768, F32)],
        compiler_params=params(),
        cost_estimate=cost(),
        name="norm_and_project",
    )(*in_hbm(tokens, gain, shift, weights))


GELU_A = 0.7978845608028654
GELU_B = 0.044715


def hidden_units(normed, weights, shift):
    width = 256

    def kernel(left, weight, shift_ref, hidden_ref, slope_ref):
        u = jnp.dot(left[...], weight[...], preferred_element_type=F32) + shift_ref[...]
        square = u * u
        t = jnp.tanh(GELU_A * u * (1.0 + GELU_B * square))
        half = 0.5 * (1.0 + t)
        hidden_ref[...] = (u * half).astype(BF)
        slope = half + 0.5 * u * (1.0 - t * t) * GELU_A * (1.0 + 3.0 * GELU_B * square)
        slope_ref[...] = slope.astype(BF)

    column = pl.BlockSpec((1024, width), lambda i: (0, i))
    return pl.pallas_call(
        kernel,
        grid=(1024 // width,),
        in_specs=[
            pl.BlockSpec((1024, D), lambda i: (0, 0), pipeline_mode=pl.Buffered(1)),
            pl.BlockSpec((D, width), lambda i: (0, i)),
            pl.BlockSpec((1, width), lambda i: (0, i)),
        ],
        out_specs=[column, column],
        out_shape=[like(1024, 1024)] * 2,
        compiler_params=params(),
        cost_estimate=cost(),
        name="hidden_units",
    )(*in_hbm(normed, weights, shift))


def hidden_back(gradients, weights, slope):
    width = 256

    def kernel(left, weight, slope_ref, d_ref, sum_ref):
        value = jnp.dot(left[...], weight[...], preferred_element_type=F32) * slope_ref[...].astype(F32)
        value = value.astype(BF)
        d_ref[...] = value
        sum_ref[...] = jnp.sum(value.astype(F32), axis=0, keepdims=True)

    column = pl.BlockSpec((1024, width), lambda i: (0, i))
    return pl.pallas_call(
        kernel,
        grid=(1024 // width,),
        in_specs=[
            pl.BlockSpec((1024, D), lambda i: (0, 0), pipeline_mode=pl.Buffered(1)),
            pl.BlockSpec((D, width), lambda i: (0, 1024 // width + i)),
            column,
        ],
        out_specs=[column, pl.BlockSpec((1, width), lambda i: (0, i))],
        out_shape=[like(1024, 1024), like(1, 1024, F32)],
        compiler_params=params(),
        cost_estimate=cost(),
        name="hidden_back",
    )(*in_hbm(gradients, weights, slope))


def apart(places, lefts, weights, norm=None):
    count = len(lefts)

    def kernel(places_ref, *refs):
        value_ref = refs[-1]
        value = sum(
            lax.dot_general(
                left[...],
                weight[...].reshape(-1, weight.shape[2]),
                (((1,), (1,)), ((), ())),
                preferred_element_type=F32,
            )
            for left, weight in zip(refs[:count], refs[count : 2 * count])
        )
        refs = refs[2 * count : -1]
        if norm is not None:
            tokens, average, inverse = refs[:3]
            refs = refs[3:]
            standard = (tokens[...].astype(F32) - average[...]) * inverse[...]
            refs[2][0:1, :] = jnp.sum(value * standard, axis=0, keepdims=True)
            refs[2][1:2, :] = jnp.sum(value, axis=0, keepdims=True)
        value_ref[...] = value
        for h in range(2):
            for k in range(4):
                rows = pl.ds(pl.multiple_of(places_ref[4 * h + k] * TOK, TOK), TOK)
                refs[h][k * TOK : (k + 1) * TOK, :] = value_ref[rows, :].astype(BF)

    width = 512
    column = pl.BlockSpec((1024, 1), lambda i: (0, 0))
    return pl.pallas_call(
        kernel,
        grid=(D // width,),
        in_specs=[SMEM]
        + [pl.BlockSpec(left.shape, lambda i: (0, 0), pipeline_mode=pl.Buffered(1)) for left in lefts]
        + [
            pl.BlockSpec((4, 128, left.shape[1]), lambda i, at=at: (i, 0, at))
            for left, (_, at) in zip(lefts, weights)
        ]
        + ([] if norm is None else [pl.BlockSpec((1024, width), lambda i: (0, i)), column, column]),
        out_specs=[pl.BlockSpec((512, width), lambda i: (0, i))] * 2
        + ([] if norm is None else [pl.BlockSpec((2, width), lambda i: (0, i))]),
        out_shape=[like(512, D)] * 2 + ([] if norm is None else [like(2, D, F32)]),
        scratch_shapes=[pltpu.VMEM((1024, width), F32)],
        compiler_params=params(),
        cost_estimate=cost(),
        name="apart",
    )(places, *in_hbm(*lefts, *(weight for weight, _ in weights), *(norm or ())))


def token_sum1(near, got):
    def kernel(near_ref, got_ref, send_ref, keep_ref):
        send_ref[...] = (near_ref[256:, :].astype(F32) + got_ref[256:, :].astype(F32)).astype(BF)
        keep_ref[...] = near_ref[:256, :].astype(F32) + got_ref[:256, :].astype(F32)

    def part(rows):
        return pl.BlockSpec((rows, 512), lambda i: (0, i))

    return pl.pallas_call(
        kernel,
        grid=(D // 512,),
        in_specs=[part(512)] * 2,
        out_specs=[part(256)] * 2,
        out_shape=[like(256, D), like(256, D, F32)],
        compiler_params=params(),
        cost_estimate=cost(),
        name="token_sum1",
    )(*in_hbm(near, got))


def token_sum2(keep, back):
    def kernel(keep_ref, back_ref, send_ref):
        send_ref[...] = (keep_ref[...] + back_ref[...].astype(F32)).astype(BF)

    lower = pl.BlockSpec((TOK, 1024), lambda i: (1, i))
    return pl.pallas_call(
        kernel,
        grid=(D // 1024,),
        in_specs=[lower] * 2,
        out_specs=pl.BlockSpec((TOK, 1024), lambda i: (0, i)),
        out_shape=like(TOK, D),
        compiler_params=params(),
        cost_estimate=cost(),
        name="token_sum2",
    )(*in_hbm(keep, back))


ROWS = pl.BlockSpec((TOK // 4, D), lambda i: (i, 0))
ONE_ROW = pl.BlockSpec((1, D), lambda i: (0, 0))


def finish_output(keep, back, last, residual, shift):
    def kernel(keep_ref, back_ref, last_ref, residual_ref, shift_ref, out_ref):
        value = keep_ref[...] + back_ref[...].astype(F32) + last_ref[...].astype(F32)
        value = residual_ref[...].astype(F32) + value + shift_ref[...]
        out_ref[...] = outside(value.astype(BF))

    return pl.pallas_call(
        kernel,
        grid=(4,),
        in_specs=[ROWS] * 4 + [ONE_ROW],
        out_specs=ROWS,
        out_shape=like(TOK, D),
        compiler_params=params(),
        cost_estimate=cost(),
        name="finish_output",
    )(*in_hbm(keep, back, last, residual, shift))


def finish_grad(keep, back, last, residual, gradient, gain):
    def kernel(keep_ref, back_ref, last_ref, residual_ref, gradient_ref, gain_ref, out_ref):
        value = keep_ref[...] + back_ref[...].astype(F32) + last_ref[...].astype(F32)
        value = value * gain_ref[...]
        rows = residual_ref[...].astype(F32)
        rows = rows - jnp.mean(rows, axis=1, keepdims=True)
        inverse = lax.rsqrt(jnp.mean(rows * rows, axis=1, keepdims=True) + EPS)
        rows = rows * inverse
        plain = jnp.mean(value, axis=1, keepdims=True)
        cross = jnp.mean(value * rows, axis=1, keepdims=True)
        out_ref[...] = outside(gradient_ref[...].astype(F32) + inverse * (value - plain - rows * cross))

    return pl.pallas_call(
        kernel,
        grid=(4,),
        in_specs=[ROWS] * 5 + [ONE_ROW],
        out_specs=ROWS,
        out_shape=like(TOK, D, F32),
        compiler_params=params(),
        cost_estimate=cost(),
        name="finish_grad",
    )(*in_hbm(keep, back, last, residual, gradient, gain))


def doc_positions(segments):
    length = segments.shape[0]
    places = jnp.arange(length, dtype=jnp.int32)
    boundary = jnp.concatenate([jnp.ones((1,), dtype=jnp.bool_), segments[1:] != segments[:-1]])
    doc_start = lax.cummax(jnp.where(boundary, places, jnp.zeros_like(places)), axis=0)
    return places - doc_start


def rotary_tables(positions):
    lane = jnp.arange(128, dtype=jnp.int32) % HD
    half_rot = ROT // 2
    frequency = 10000.0 ** (-(2.0 * (lane % half_rot).astype(F32)) / ROT)
    angles = positions.astype(F32)[:, None] * jnp.where(lane < ROT, frequency, 0.0)
    sine = jnp.sin(angles)
    before = jnp.where(lane < half_rot, -sine, 0.0)
    after = jnp.where((lane >= half_rot) & (lane < ROT), sine, 0.0)
    return jnp.concatenate([jnp.cos(angles), before, after], axis=1)


def attention_kernel(
    proj_ref, shift_ref, table_ref, column_ref, row_ref, grad_ref, weight_ref, mixed_ref, d_proj_ref, sums_ref, mask_ref
):
    start, last = column_ref[:, 0:1], column_ref[:, 1:2]
    where = row_ref[0]
    mask_ref[...] = jnp.where((where >= start) & (where <= last), 0.0, MASKED)
    cosine, before, after = (table_ref[:, i * 128 : (i + 1) * 128] for i in range(3))
    lane = lax.broadcasted_iota(jnp.int32, (SEQ, 128), 1)

    def turn(value, sign):
        shifted = pltpu.roll(value, 112, 1) * before + pltpu.roll(value, 16, 1) * after
        return value * cosine + sign * shifted

    def part(index, pair):
        at = slice(index * 256 + pair * 128, index * 256 + pair * 128 + 128)
        return proj_ref[:, at] + shift_ref[:, at]

    def dot(a, b, dims):
        return lax.dot_general(a, b, (dims, ((), ())), preferred_element_type=F32)

    d_attended = jnp.dot(grad_ref[...], weight_ref[...].reshape(D, 256), preferred_element_type=F32).astype(BF)
    for pair in range(2):
        at = slice(pair * 128, pair * 128 + 128)
        queries = (turn(part(0, pair), 1.0).astype(BF).astype(F32) * HD**-0.5).astype(BF)
        keys = turn(part(1, pair), 1.0).astype(BF)
        values = part(2, pair).astype(BF)
        d_out = d_attended[:, at]
        results = []
        for head in range(2):
            own = (lane >= head * HD) & (lane < (head + 1) * HD)
            own_queries = jnp.where(own, queries, jnp.zeros_like(queries))
            own_d_out = jnp.where(own, d_out, jnp.zeros_like(d_out))
            scores = dot(own_queries, keys, ((1,), (1,))) + mask_ref[...]
            exponent = jnp.exp(scores - jnp.max(scores, axis=1, keepdims=True))
            soft = exponent * (1.0 / jnp.sum(exponent, axis=1, keepdims=True))
            soft_low = soft.astype(BF)
            mixed = dot(soft_low, values, ((1,), (0,)))
            d_soft = dot(own_d_out, values, ((1,), (1,)))
            inner = jnp.sum(soft * d_soft, axis=1, keepdims=True)
            d_scores = (soft * (d_soft - inner)).astype(BF)
            d_queries = dot(d_scores, keys, ((1,), (0,))) * HD**-0.5
            d_keys = dot(d_scores, own_queries, ((0,), (0,)))
            d_values = dot(soft_low, own_d_out, ((0,), (0,)))
            results.append((mixed, d_queries, d_keys, d_values))
        first, second = results
        mixed_ref[:, at] = jnp.where(lane < HD, first[0], second[0]).astype(BF)
        d_queries = turn(jnp.where(lane < HD, first[1], second[1]), -1.0).astype(BF)
        d_keys = turn(first[2] + second[2], -1.0).astype(BF)
        d_values = (first[3] + second[3]).astype(BF)
        for index, value in enumerate((d_queries, d_keys, d_values)):
            at = slice(index * 256 + pair * 128, index * 256 + pair * 128 + 128)
            d_proj_ref[:, at] = value
            sums_ref[0, :, at] = jnp.sum(value.astype(F32), axis=0, keepdims=True)


def attention(projected, shift, tables, columns, rows, gradients, weights):
    count = projected.shape[0] // SEQ
    return pl.pallas_call(
        attention_kernel,
        grid=(count,),
        in_specs=[
            pl.BlockSpec((SEQ, 768), lambda i: (i, 0)),
            pl.BlockSpec((1, 768), lambda i: (0, 0)),
            pl.BlockSpec((SEQ, 384), lambda i: (i, 0)),
            pl.BlockSpec((SEQ, 2), lambda i: (i, 0)),
            pl.BlockSpec((1, 1, SEQ), lambda i: (i, 0, 0)),
            pl.BlockSpec((SEQ, D), lambda i: (i, 0)),
            pl.BlockSpec((16, 128, 256), lambda i: (0, 0, 3), pipeline_mode=pl.Buffered(1)),
        ],
        out_specs=[
            pl.BlockSpec((SEQ, 256), lambda i: (i, 0)),
            pl.BlockSpec((SEQ, 768), lambda i: (i, 0)),
            pl.BlockSpec((1, 1, 768), lambda i: (i, 0, 0)),
        ],
        out_shape=[
            pltpu.HBM((count * SEQ, 256), BF),
            pltpu.HBM((count * SEQ, 768), BF),
            pltpu.HBM((count, 1, 768), F32),
        ],
        scratch_shapes=[pltpu.VMEM((SEQ, SEQ), F32)],
        compiler_params=pltpu.CompilerParams(vmem_limit_bytes=VMEM_LIMIT),
        cost_estimate=cost(),
        name="attention",
    )(*in_hbm(projected, shift, tables, columns, rows, gradients, weights))


def body(
    residual_in,
    segment_ids,
    out_grad,
    ln_gain,
    ln_bias,
    w_qkv,
    b_qkv,
    w_out,
    b_attn_out,
    w_up,
    b_up,
    w_down,
    b_mlp_out,
):
    y_lo, x, z, y_hi, core = (lax.axis_index(name).astype(jnp.int32) for name in AXES)
    low_index = y_lo[None]
    low = y_lo == 0

    def around(c):
        return [c, c ^ (1 + 2 * core), c ^ (3 - 2 * core), c ^ 2]

    ring_places = jnp.stack(around(x) + around(z) + [y_lo, 1 - y_lo])
    y_places = [
        y_lo * 2 + y_hi,
        (1 - y_lo) * 2 + (y_hi ^ core),
        (1 - y_lo) * 2 + (y_hi ^ (1 - core)),
        y_lo * 2 + (1 - y_hi),
    ]
    token_places = jnp.stack(
        y_places + [2 * k + core for k in range(4)] + [2 * k + 1 - core for k in range(4)]
    )
    part_places = jnp.stack(
        [2 * p + core for p in y_places] + [2 * y_places[k] + 1 - core for k in (0, 2, 1, 3)]
    )

    residual, gradient, attn_own, attn_away, rest_own, rest_away = prepare(
        low_index, residual_in, out_grad, w_qkv.transpose(1, 0, 2), w_out.T, w_up, w_down.T
    )
    small = jnp.concatenate(
        [ln_gain, ln_bias, b_attn_out, b_mlp_out, b_up.reshape(64), b_qkv.reshape(48), jnp.zeros((80,), BF)]
    )[None]

    def widen(rows, axis, index):
        got = flip(rows, axis)
        return jnp.where(index == 0, jnp.concatenate([rows, got]), jnp.concatenate([got, rows]))

    attn_got = flip(attn_away, "y_lo")
    token_first = swap_y(residual, 0)
    small = widen(widen(small, "core", core), "y_hi", y_hi)
    attn_got, token_first, small, gradient, rest_away = bar((attn_got, token_first, small, gradient, rest_away))
    small = jnp.pad(small.reshape(1, 1024), ((0, 15), (0, 0)))
    plan = [(source, 0, BLK, 0, 1024, 0, 0, 8 + source, BLK, 0) for source in range(2)]
    plan.append((2, 0, 16, 0, 1024, 0, 128, None, 0, 0))
    shard = copies(ring_places, plan, [(144, 1024)], [attn_own, attn_got, small])[0]

    def joined(own, first):
        plan = [(source, 0, TOK, 0, D, 0, TOK * source, None, 0, 0) for source in range(2)]
        return copies(token_places, plan, [(2 * TOK, D)], [own, first])[0]

    def of_core(own, first, second):
        plan = [
            (source, row, TOK, 0, D, 0, 0, k, TOK, 0)
            for k, (source, row) in enumerate(((0, 0), (1, 0), (2, 0), (2, TOK)))
        ]
        return copies(token_places, plan, [(SEQ, D)], [own, first, second])[0]

    def of_both(mine, other):
        plan = [
            (source, k * TOK, TOK, 0, D, 0, 0, 4 + 4 * source + k, TOK, 0) for source in range(2) for k in range(4)
        ]
        return copies(token_places, plan, [(1024, D)], [mine, other])[0]

    shard, tokens_sent, rest_away, gradient = bar((shard, joined(residual, token_first), rest_away, gradient))
    attn_all = lax.all_gather(shard, ("x", "z"), axis=0)
    token_second = swap_y(tokens_sent, 1)
    rest_got = flip(rest_away, "y_lo")
    token_second, rest_got, gradient = bar((token_second, rest_got, gradient))
    plan = [
        (source, 0, BLK, 1024 * h, 1024, h, 0, 8 + source, BLK, 0) for source in range(2) for h in range(2)
    ]
    rest_gather = Gather(ring_places, *copies(ring_places, plan, [(128, 1024)] * 2, [rest_own, rest_got]))
    mine, sends, gradient = bar((of_core(residual, token_first, token_second), rest_gather.send(1), gradient))
    other = flip(mine, "core")
    grad_first = swap_y(gradient, 0)
    got, other, mine, grad_first = bar((gather_step(1, sends), other, mine, grad_first))
    rest_gather.take(1, got)
    tokens, grads_sent, sends = bar((of_both(mine, other), joined(gradient, grad_first), rest_gather.send(2)))
    grad_second = swap_y(grads_sent, 1)
    table = flip(attn_all[:, 128, :][None], "y_lo")
    got, grad_second, table = bar((gather_step(2, sends), grad_second, table))
    rest_gather.take(2, got)
    mine, sends = bar((of_core(gradient, grad_first, grad_second), rest_gather.send(3)))
    other = flip(mine, "core")
    got = gather_step(3, sends)

    own_table = attn_all[:, 128, :][None]
    table = jnp.where(low, jnp.concatenate([own_table, table]), jnp.concatenate([table, own_table]))
    table = table.reshape(2, 16, 4, 256).astype(F32)
    vectors = table[..., :64].reshape(2, 16, 4, 4, 16).transpose(3, 1, 0, 2, 4).reshape(4, D)
    gain, shift, out_shift = vectors[0:1], vectors[1:2], vectors[2:3] + vectors[3:4]
    shifts = lax.dynamic_index_in_dim(table.reshape(2, 16, 4, 256), y_hi * 2 + core, 2, False)
    shifts = lax.dynamic_index_in_dim(shifts, y_lo, 0, False)
    up_shift = shifts[:, 64:128].reshape(1, 1024)
    qkv_shift = shifts[:, 128:176].reshape(16, 3, 16).transpose(1, 0, 2).reshape(1, 768)

    far_segments = flip(segment_ids, "y_lo")
    places = jnp.arange(SEQ, dtype=jnp.int32)
    positions = jnp.concatenate(
        [doc_positions(jnp.where(low, a, b)) for a, b in ((segment_ids, far_segments), (far_segments, segment_ids))]
    )
    place_pair = jnp.concatenate([places, places])
    columns = jnp.stack([place_pair - positions, place_pair], axis=1)
    rows = place_pair.reshape(2, 1, SEQ)
    tables = rotary_tables(positions)

    normed, average, inverse, projected = norm_and_project(tokens, gain, shift, attn_all)
    got, other, mine, normed, projected = bar((got, other, mine, normed, projected))
    rest_gather.take(3, got)
    sends, grad_all, projected = bar((rest_gather.send(4), of_both(mine, other), projected))
    rest_got = gather_step(4, sends)
    mixed, d_projected, sums = attention(projected, qkv_shift, tables, columns, rows, grad_all, attn_all)
    attn_sum = attention_gradient(normed, d_projected, grad_all, mixed)
    attn_sum, rest_got, normed = bar((attn_sum, rest_got, normed))
    attn_sum = lax.psum_scatter(attn_sum, ("x", "z"), scatter_dimension=0, tiled=True)

    rest_gather.take(4, rest_got)
    rest_all = rest_gather.all
    hidden, slope = hidden_units(normed, rest_all, up_shift)
    down_sum = Scatter(ring_places, grad_all, hidden)
    sends, mixed, hidden, slope, grad_all = bar((down_sum.first, mixed, hidden, slope, grad_all))
    down_got = scatter_step(1, sends)
    near, away = apart(part_places, [mixed, hidden], [(attn_all, 3), (rest_all.reshape(16, 128, 2048), 1)])
    d_hidden, up_shift_part = hidden_back(grad_all, rest_all, slope)
    near, away, d_hidden, down_got = bar((near, away, d_hidden, down_got))
    sends, away, d_hidden = bar((down_sum.send2(down_got), away, d_hidden))
    out_got = flip(away, "core")
    down_got = scatter_step(2, sends)
    up_sum = Scatter(ring_places, normed, d_hidden)
    up_sends, out_got, down_got = bar((up_sum.first, out_got, down_got))
    out_send, out_keep = token_sum1(near, out_got)
    up_sends, down_sends, out_send, d_hidden = bar((up_sends, down_sum.send3(down_got), out_send, d_hidden))

    up_got = scatter_step(1, up_sends)
    out_back = swap_y(out_send, 1)
    down_got = scatter_step(3, down_sends)
    d_near, d_away, vector_parts = apart(
        part_places,
        [d_projected, d_hidden],
        [(attn_all, 0), (rest_all.reshape(16, 128, 2048), 0)],
        (tokens, average, inverse),
    )
    d_away, up_got, out_back, down_got, vector_parts = bar((d_away, up_got, out_back, down_got, vector_parts))
    out_shift_part = jnp.sum(gradient.astype(F32), axis=0, keepdims=True)
    parts = jnp.concatenate([vector_parts, out_shift_part]).reshape(3, 16, 8, 16)
    parts = parts.transpose(1, 2, 0, 3).reshape(16, 384)
    sums = jnp.sum(sums, axis=(0, 1))
    line = jnp.concatenate(
        [
            parts,
            up_shift_part.reshape(16, 64),
            sums.reshape(3, 16, 16).transpose(1, 0, 2).reshape(16, 48),
            jnp.zeros((16, 16), F32),
        ],
        axis=1,
    )
    offsets = [0]
    for _, _, bits in RING_STEPS:
        offsets = offsets + [o ^ bits for o in offsets]
    here = (4 * x + z) ^ jnp.array(offsets, jnp.int32)
    order = (here[:, None] == jnp.arange(16, dtype=jnp.int32)[None, :]).astype(F32)
    line = jnp.dot(order, line, precision=lax.Precision.HIGHEST)

    def fold(line, step):
        axis, mask, _ = RING_STEPS[step]
        count = line.shape[0] // 2
        return line[:count] + flip4(line[count:], axis, mask)

    def narrow(part, axis, index):
        part = part.reshape(2, -1)
        return jnp.where(index == 0, part[0], part[1]) + flip(jnp.where(index == 0, part[1], part[0]), axis)

    up_sends, d_away, down_sends = bar((up_sum.send2(up_got), d_away, down_sum.send4(down_got)))
    d_got = flip(d_away, "core")
    up_got = scatter_step(2, up_sends)
    down_got = scatter_step(4, down_sends)
    out_send = token_sum2(out_keep, out_back)
    d_got, up_got, down_got, out_send, line = bar((d_got, up_got, down_got, out_send, line))
    d_send, d_keep = token_sum1(d_near, d_got)
    up_sends, d_send, line = bar((up_sum.send3(up_got), d_send, line))
    d_back = swap_y(d_send, 1)
    up_got = scatter_step(3, up_sends)
    out_last = swap_y(out_send, 0)
    line = fold(fold(line, 3), 2)
    down_result = down_sum.finish(down_got)
    d_back, up_got, out_last, line = bar((d_back, up_got, out_last, line))
    up_sends, d_send, line = bar((up_sum.send4(up_got), token_sum2(d_keep, d_back), line))
    up_got = scatter_step(4, up_sends)
    d_last = swap_y(d_send, 0)
    line = fold(fold(line, 1), 0)[0]
    down_far = flip(down_result[1], "y_lo")
    output = finish_output(out_keep, out_back, out_last, residual, out_shift)
    up_got, d_last, down_far, line, output, attn_sum = bar((up_got, d_last, down_far, line, output, attn_sum))
    up_result = up_sum.finish(up_got)
    up_far = flip(up_result[1], "y_lo")
    lower, upper = attn_sum[:BLK], attn_sum[BLK:]
    attn_own, attn_away = jnp.where(low, lower, upper), jnp.where(low, upper, lower)
    attn_far = flip(attn_away, "y_lo")
    grad_in = finish_grad(d_keep, d_back, d_last, residual, gradient, gain)
    sum_down = whole(low_index, down_result[0], down_far, ((1024, 1),))[0]
    part = narrow(narrow(narrow(line[:384], "y_lo", y_lo), "y_hi", y_hi), "core", core)
    sum_qkv, sum_out = whole(low_index, attn_own, attn_far, ((256, 3), (256, 1)))
    sum_up = whole(low_index, up_result[0], up_far, ((1024, 1),))[0]
    grad_gain, grad_shift, grad_out_shift = part[:16], part[16:32], part[32:]
    return (
        output,
        grad_in,
        grad_gain,
        grad_shift,
        sum_qkv.transpose(1, 0, 2),
        line[448:496].reshape(3, 1, 16),
        sum_out[0].T,
        grad_out_shift,
        sum_up[0],
        line[384:448].reshape(1, 64),
        sum_down[0].T,
        grad_out_shift,
    )


def solution(mesh):
    fine = Mesh(mesh.devices.reshape(2, 4, 4, 2, 2), AXES)
    dp = ("y_lo", "x", "z")
    tensor = ("y_hi", "core")
    every = AXES
    in_specs = (
        P(every, None),
        P(dp),
        P(every, None),
        P(every),
        P(every),
        P(dp, None, tensor),
        P(None, tensor, dp),
        P(tensor, dp),
        P(every),
        P(dp, tensor),
        P(tensor, dp),
        P(tensor, dp),
        P(every),
    )
    out_specs = (
        P(every, None),
        P(every, None),
        P(every),
        P(every),
        P(dp, None, tensor),
        P(None, tensor, dp),
        P(tensor, dp),
        P(every),
        P(dp, tensor),
        P(tensor, dp),
        P(tensor, dp),
        P(every),
    )
    return jax.shard_map(body, mesh=fine, in_specs=in_specs, out_specs=out_specs, check_vma=False)
```

```python
import jax
import jax.numpy as jnp
from jax import lax
from jax.experimental import pallas as pl
from jax.experimental.pallas import tpu as pltpu
from jax.sharding import Mesh, PartitionSpec as P

HD = 64
ROT = 32
EPS = 1e-05
MASKED = -1e30
D = 2048
SEQ = 512
TOK = 128
BLK = 64
VMEM_LIMIT = 24 * 1024 * 1024
BF = jnp.bfloat16
F32 = jnp.float32
AXES = ("y_lo", "x", "z", "y_hi", "core")


bar = lax.optimization_barrier


def params(limit=VMEM_LIMIT):
    return pltpu.CompilerParams(vmem_limit_bytes=limit)


def cost():
    return pl.CostEstimate(flops=1000, bytes_accessed=1000, transcendentals=0)


def like(rows, columns, kind=BF):
    return pltpu.HBM((rows, columns), kind)


def in_hbm(*values):
    return tuple(pltpu.with_memory_space_constraint(value, pltpu.HBM) for value in values)


def in_vmem(value):
    return pltpu.with_memory_space_constraint(value, pltpu.VMEM)


SMEM = pl.BlockSpec(memory_space=pltpu.SMEM)
VMEM = pl.BlockSpec(memory_space=pltpu.VMEM)
ANY = pl.BlockSpec(memory_space=pl.ANY)


def ring(value, axis, step):
    masks = (1, 3) if step == 0 else (3, 1)
    table = [(i * 2 + c, (i ^ masks[c]) * 2 + c) for i in range(4) for c in range(2)]
    return lax.ppermute(value, (axis, "core"), table)


def ring_pair(pair, axes, step):
    pair = bar(tuple(pair))
    return bar(tuple(ring(value, axis, step) for value, axis in zip(pair, axes)))


def swap_y(value, step):
    masks = (1, 3) if step == 0 else (3, 1)

    def place(y, c):
        return ((y % 2) * 2 + y // 2) * 2 + c

    table = [(place(y, c), place(y ^ masks[c], c)) for y in range(4) for c in range(2)]
    return lax.ppermute(value, ("y_lo", "y_hi", "core"), table)


def flip(value, axis):
    return lax.ppermute(value, axis, [(0, 1), (1, 0)])


def copies(places, *jobs):
    sources = [source for _, _, given, _ in jobs for source in given]
    shapes = [(shape, stay) for _, made, _, stay in jobs for shape in made]
    plans, low, made = [], 0, 0
    for plan, results, given, stay in jobs:
        for source, row, rows, column, columns, target, to, place, unit, across in plan:
            plans.append((source + low, row, rows, column, columns, target + made, to, place, unit, across, stay))
        low += len(given)
        made += len(results)

    def kernel(places_ref, *refs):
        inputs, refs = refs[: len(sources)], refs[len(sources) :]
        outputs, spare, sems = refs[: len(shapes)], list(refs[len(shapes) : -1]), refs[-1]
        stages = [output if stay else spare.pop(0) for output, (_, stay) in zip(outputs, shapes)]
        moves = []
        for i, (source, row, rows, column, columns, target, to, place, unit, across, stay) in enumerate(plans):
            if place is not None:
                to = pl.multiple_of(to + places_ref[place] * unit, rows)
            at = (pl.ds(to, rows), pl.ds(across, columns))
            stage = stages[target].at[at]
            arrive = pltpu.make_async_copy(
                inputs[source].at[pl.ds(row, rows), pl.ds(column, columns)], stage, sems.at[0, i]
            )
            arrive.start()
            leave = None if stay else pltpu.make_async_copy(stage, outputs[target].at[at], sems.at[1, i])
            moves.append((arrive, leave))
        for arrive, leave in moves:
            arrive.wait()
            if leave is not None:
                leave.start()
        for _, leave in moves:
            if leave is not None:
                leave.wait()

    outs = pl.pallas_call(
        kernel,
        in_specs=[SMEM] + [ANY] * len(sources),
        out_specs=[VMEM if stay else ANY for _, stay in shapes],
        out_shape=[pltpu.VMEM(shape, BF) if stay else like(*shape) for shape, stay in shapes],
        scratch_shapes=[pltpu.VMEM(shape, BF) for shape, stay in shapes if not stay]
        + [pltpu.SemaphoreType.DMA((2, len(plans)))],
        compiler_params=params(),
        cost_estimate=cost(),
        name="put_together",
    )(places, *in_hbm(*sources))
    results = []
    for _, made, _, _ in jobs:
        results.append(outs[: len(made)])
        outs = outs[len(made) :]
    return results


def flip4(value, axis, mask):
    return lax.ppermute(value, axis, [(i, i ^ mask) for i in range(4)])


RING_STEPS = (("z", 1, 1), ("z", 3, 3), ("x", 1, 4), ("x", 3, 12))


class Gather:
    def __init__(self, left, right):
        self.pair = (left, right)

    def sending(self, got):
        self.first = got
        rows, width = self.pair[0].shape
        plan = [(2 * h + k, 0, rows, 0, width, h, k * rows, None, 0, 0) for h in range(2) for k in range(2)]
        sources = [value for both in zip(self.pair, self.first) for value in both]
        return plan, [(2 * rows, width)] * 2, sources, False

    def joining(self, got, last):
        self.last = got
        rows, width = self.pair[0].shape
        sources = [value for each in zip(self.pair, self.first, got) for value in each]
        if last:
            return self.ordered(0), [(2048, width)], sources[:3], False
        plan = []
        for h in range(2):
            for k, (source, row) in enumerate(((0, 0), (1, 0), (2, 0), (2, rows))):
                plan.append((source + 3 * h, row, rows, 0, width, h, 0, 4 * h + k, rows, 0))
        return plan, [(4 * rows, width)] * 2, sources, False

    def ordered(self, h):
        rows, width = self.pair[0].shape
        plan = []
        for k, (source, row) in enumerate(((0, 0), (1, 0), (2, 0), (2, rows))):
            for i in range(4):
                to, unit = ((i * 512, 128), (i * 128, 512))[h]
                plan.append((source, row + i * 128, 128, 0, width, 0, to, 4 * (1 - h) + k, unit, 0))
        return plan

    def right(self):
        return self.ordered(1), (self.pair[1], self.first[1], self.last[1])


def gather_step(step, pair):
    return ring_pair(pair, ("x", "z") if step < 3 else ("z", "x"), 1 - step % 2)


def scatter_step(step, pair):
    return ring_pair(pair, ("x", "z") if step < 3 else ("z", "x"), step % 2)


class Scatter:
    def __init__(self, places, left, right):
        self.places = places
        tokens, width = right.shape
        self.width = half = width // 2

        def kernel(places_ref, left_ref, right_ref, *refs):
            outs, (rights, *stages), sems = refs[:6], refs[6:-1], refs[-1]
            fetch = [
                pltpu.make_async_copy(right_ref.at[:, pl.ds(h * half, half)], rights.at[h], sems.at[h]) for h in range(2)
            ]
            for copy in fetch:
                copy.start()
            order = [2, 3, 1, 0]
            stored = []
            for h in range(2):
                fetch[h].wait()
                for i, k in enumerate(order):
                    if h == 0:
                        block = left_ref[:, pl.ds(pl.multiple_of(places_ref[k] * 512, 512), 512)]
                    else:
                        z = places_ref[4 + k]
                        block = jnp.concatenate(
                            [left_ref[:, pl.ds(pl.multiple_of(n * 512 + z * 128, 128), 128)] for n in range(4)], axis=1
                        )
                    value = lax.dot_general(
                        block,
                        rights[h],
                        (((0,), (0,)), ((), ())),
                        preferred_element_type=F32,
                    ).astype(BF)
                    stage = stages[h].at[pl.ds(i * 512, 512)]
                    stage[...] = value
                    out = outs[h].at[pl.ds(i * 512, 512)] if i < 2 else outs[2 * i - 2 + h]
                    copy = pltpu.make_async_copy(stage, out, sems.at[2 + 4 * h + i])
                    copy.start()
                    stored.append(copy)
            for copy in stored:
                copy.wait()

        outs = pl.pallas_call(
            kernel,
            in_specs=[SMEM, VMEM, ANY],
            out_specs=[ANY] * 6,
            out_shape=[like(1024, half)] * 2 + [like(512, half)] * 4,
            scratch_shapes=[
                pltpu.VMEM((2, tokens, half), BF),
                pltpu.VMEM((2048, half), BF),
                pltpu.VMEM((2048, half), BF),
                pltpu.SemaphoreType.DMA((10,)),
            ],
            compiler_params=params(),
            cost_estimate=cost(),
            name="gradient",
        )(places, in_vmem(left), *in_hbm(right))
        self.first, self.next, self.keep = outs[:2], outs[2:4], outs[4:]

    def send2(self, got):
        self.got = got

        def kernel(places_ref, *refs):
            for h in range(2):
                refs[4 + h][...] = (refs[h][...].astype(F32) + refs[2 + h][...].astype(F32)).astype(BF)

        return kernel, [*self.next, *((value, 512, 1) for value in got)], [(512, self.width, BF)] * 2, ()

    def send3(self, last):
        def kernel(places_ref, *refs):
            total = refs[-1]
            for h in range(2):
                keep, arrived, later, send, own = (refs[2 * k + h] for k in range(5))
                total[...] = keep[...].astype(F32) + arrived[...].astype(F32) + later[...].astype(F32)
                own_at, first, second, across = (
                    pl.ds(pl.multiple_of(places_ref[4 * (1 - h) + k] * 128, 128), 128) for k in range(4)
                )
                send[:128, :] = total[second, :].astype(BF)
                send[128:, :] = total[across, :].astype(BF)
                own[:128, :] = total[first, :]
                own[128:, :] = total[own_at, :]

        return (
            kernel,
            [*self.keep, *((value, 512, 0) for value in self.got), *last],
            [(256, self.width, BF)] * 2 + [(256, self.width, F32)] * 2,
            [pltpu.VMEM((512, self.width // 2), F32)],
        )

    def send4(self, got):
        self.got = got

        def kernel(places_ref, *refs):
            for h in range(2):
                refs[4 + h][...] = (refs[h][...] + refs[2 + h][...].astype(F32)).astype(BF)

        return (
            kernel,
            [*((value, 128, 0) for value in self.keep), *((value, 128, 1) for value in got)],
            [(128, self.width, BF)] * 2,
            (),
        )

    def finish(self, last):
        def kernel(places_ref, *refs):
            total, width = refs[-1], self.width
            for h in range(2):
                keep, arrived, later = (refs[2 * k + h] for k in range(3))
                total[:, h * width : (h + 1) * width] = (
                    keep[...] + arrived[...].astype(F32) + later[...].astype(F32)
                )
            low = places_ref[8]
            refs[6][...] = total[pl.ds(pl.multiple_of(low * BLK, BLK), BLK), :]
            refs[7][...] = total[pl.ds(pl.multiple_of((1 - low) * BLK, BLK), BLK), :].astype(BF)

        return (
            kernel,
            [*((value, 128, 1) for value in self.keep), *((value, 128, 0) for value in self.got), *last],
            [(BLK, 2 * self.width, F32), (BLK, 2 * self.width, BF)],
            [pltpu.VMEM((128, 2 * self.width), F32)],
        )


def add(places, *jobs, steps=2):
    jobs = [
        (kernel, [v if isinstance(v, tuple) else (v, v.shape[0], 0) for v in inputs], outs, scratch)
        for kernel, inputs, outs, scratch in jobs
    ]
    inputs = [value for _, given, _, _ in jobs for value in given]
    outs = [out for _, _, made, _ in jobs for out in made]

    def kernel(places_ref, *refs):
        given, made, spare = refs[: len(inputs)], refs[len(inputs) : len(inputs) + len(outs)], refs[len(inputs) + len(outs) :]
        for one, ins, results, scratch in jobs:
            one(places_ref, *given[: len(ins)], *made[: len(results)], *spare[: len(scratch)])
            given, made, spare = given[len(ins) :], made[len(results) :], spare[len(scratch) :]

    results = pl.pallas_call(
        kernel,
        grid=(steps,),
        in_specs=[SMEM]
        + [pl.BlockSpec((rows, value.shape[1] // steps), lambda i, at=at: (at, i)) for value, rows, at in inputs],
        out_specs=[pl.BlockSpec((rows, columns // steps), lambda i: (0, i)) for rows, columns, _ in outs],
        out_shape=[like(*shape) for shape in outs],
        scratch_shapes=[each for _, _, _, scratch in jobs for each in scratch],
        compiler_params=params(),
        cost_estimate=cost(),
        name="add",
    )(places, *in_hbm(*(value for value, _, _ in inputs)))
    split = []
    for _, _, made, _ in jobs:
        split.append(results[: len(made)])
        results = results[len(made) :]
    return split


def attention_gradient(normed, d_projected, gradients, mixed):
    def kernel(normed_ref, d_ref, grad_ref, mixed_ref, out_ref):
        rows = pl.ds(pl.multiple_of(pl.program_id(0) * 512, 512), 512)
        for left, right, at in ((normed_ref, d_ref, slice(0, 768)), (grad_ref, mixed_ref, slice(768, 1024))):
            out_ref[:, at] = lax.dot_general(
                left[:, rows], right[...], (((0,), (0,)), ((), ())), preferred_element_type=F32
            ).astype(BF)

    def fixed(width):
        return pl.BlockSpec((1024, width), lambda i: (0, 0), pipeline_mode=pl.Buffered(1))

    return pl.pallas_call(
        kernel,
        grid=(D // 512,),
        in_specs=[VMEM, fixed(768), VMEM, fixed(256)],
        out_specs=pl.BlockSpec((512, 1024), lambda i: (i, 0)),
        out_shape=like(D, 1024),
        compiler_params=params(),
        cost_estimate=cost(),
        name="attention_gradient",
    )(in_vmem(normed), *in_hbm(d_projected), in_vmem(gradients), *in_hbm(mixed))


def whole(low_index, *jobs):
    layouts = [each for _, _, layout in jobs for each in layout]

    def kernel(low_ref, *refs):
        halves, outs = refs[: 2 * len(jobs)], list(refs[2 * len(jobs) :])
        for k, (_, _, layout) in enumerate(jobs):
            at = 0
            for width, count in layout:
                out = outs.pop(0)
                mine = pl.ds(pl.multiple_of(low_ref[0] * width, width), width)
                theirs = pl.ds(pl.multiple_of((1 - low_ref[0]) * width, width), width)
                for i in range(count):
                    out[i, :, mine] = halves[2 * k][:, at : at + width].astype(F32)
                    out[i, :, theirs] = halves[2 * k + 1][:, at : at + width].astype(F32)
                    at += width

    return pl.pallas_call(
        kernel,
        in_specs=[SMEM] + [VMEM] * (2 * len(jobs)),
        out_specs=[VMEM] * len(layouts),
        out_shape=[pltpu.HBM((count, BLK, 2 * width), F32) for width, count in layouts],
        compiler_params=params(),
        cost_estimate=cost(),
        name="whole",
    )(low_index, *in_hbm(*(half for own, got, _ in jobs for half in (own, got))))


def inside(value):
    parts = [value[:, (low * 16 + n) * BLK : (low * 16 + n + 1) * BLK] for n in range(16) for low in range(2)]
    return jnp.concatenate(parts, axis=1)


def outside(value):
    parts = [value[:, (2 * n + low) * BLK : (2 * n + low + 1) * BLK] for low in range(2) for n in range(16)]
    return jnp.concatenate(parts, axis=1)


def prepare(low_index, residual, gradient, w_qkv, w_out, w_up, w_down):
    def kernel(low_ref, residual_ref, gradient_ref, qkv, out, up, down, tokens, grads, attn_own, attn_away, rest_own, rest_away):
        tokens[...] = inside(residual_ref[...])
        grads[...] = inside(gradient_ref[...])
        low = low_ref[0]
        for half, attn, rest in ((low, attn_own, rest_own), (1 - low, attn_away, rest_away)):
            narrow = pl.ds(pl.multiple_of(half * 256, 256), 256)
            wide = pl.ds(pl.multiple_of(half * 1024, 1024), 1024)
            for i in range(3):
                attn[:, i * 256 : (i + 1) * 256] = qkv[i, :, narrow]
            attn[:, 768:] = out[:, narrow]
            rest[:, :1024] = up[:, wide]
            rest[:, 1024:] = down[:, wide]

    return pl.pallas_call(
        kernel,
        in_specs=[SMEM] + [VMEM] * 6,
        out_specs=[VMEM] * 6,
        out_shape=[like(TOK, D)] * 2 + [like(BLK, 1024)] * 2 + [like(BLK, 2048)] * 2,
        compiler_params=params(),
        cost_estimate=cost(),
        name="prepare",
    )(low_index, *in_hbm(residual, gradient, w_qkv, w_out, w_up, w_down))


def norm_and_project(core_index, mine, other, gain, shift, weights):
    def kernel(core_ref, mine_ref, other_ref, gain_ref, shift_ref, weight_ref, standard_ref, normed_ref, proj_ref):
        rows = (mine_ref[...], other_ref[...])
        first = core_ref[0] == 0
        value = jnp.concatenate([jnp.where(first, *rows), jnp.where(first, *rows[::-1])]).astype(F32)
        value = value - jnp.mean(value, axis=1, keepdims=True)
        value = value * lax.rsqrt(jnp.mean(value * value, axis=1, keepdims=True) + EPS)
        standard_ref[...] = value.astype(BF)
        normed = (value * gain_ref[...] + shift_ref[...]).astype(BF)
        normed_ref[...] = normed
        proj_ref[...] = jnp.dot(normed, weight_ref[...].reshape(D, 768), preferred_element_type=F32)

    def by_row(rows, width):
        return pl.BlockSpec((rows, width), lambda i: (i, 0))

    def fixed(*shape):
        return pl.BlockSpec(shape, lambda i: (0,) * len(shape), pipeline_mode=pl.Buffered(1))

    return pl.pallas_call(
        kernel,
        grid=(4,),
        in_specs=[SMEM, by_row(TOK, D), by_row(TOK, D), fixed(1, D), fixed(1, D), fixed(16, 128, 768)],
        out_specs=[by_row(256, D), by_row(256, D), by_row(256, 768)],
        out_shape=[like(1024, D), like(1024, D), like(1024, 768, F32)],
        compiler_params=params(),
        cost_estimate=cost(),
        name="norm_and_project",
    )(core_index, *in_hbm(mine, other, gain, shift, weights))


GELU_A = 0.7978845608028654
GELU_B = 0.044715


def hidden_units(places, normed, weights, shift, plan, pieces):
    width = 256
    steps = 1024 // width

    def kernel(places_ref, left, weight, shift_ref, *refs):
        inputs, (hidden_ref, slope_ref, whole_ref, stage, sems) = refs[: len(pieces)], refs[len(pieces) :]
        moves = []
        for i, (source, row, rows, _, _, _, to, place, unit, _) in enumerate(plan):
            at = pl.ds(pl.multiple_of(to + places_ref[place] * unit, rows), rows)
            moves.append(
                (
                    pltpu.make_async_copy(inputs[source].at[pl.ds(row, rows)], stage.at[at], sems.at[0, i]),
                    pltpu.make_async_copy(stage.at[at], whole_ref.at[at], sems.at[1, i]),
                )
            )

        @pl.when(pl.program_id(0) == 0)
        def _():
            for arrive, _ in moves:
                arrive.start()

        u = jnp.dot(left[...], weight[...], preferred_element_type=F32) + shift_ref[...]
        square = u * u
        t = jnp.tanh(GELU_A * u * (1.0 + GELU_B * square))
        half = 0.5 * (1.0 + t)
        hidden_ref[...] = (u * half).astype(BF)
        slope = half + 0.5 * u * (1.0 - t * t) * GELU_A * (1.0 + 3.0 * GELU_B * square)
        slope_ref[...] = slope.astype(BF)

        @pl.when(pl.program_id(0) == 1)
        def _():
            for arrive, leave in moves:
                arrive.wait()
                leave.start()

        @pl.when(pl.program_id(0) == steps - 1)
        def _():
            for _, leave in moves:
                leave.wait()

    column = pl.BlockSpec((1024, width), lambda i: (0, i))
    return pl.pallas_call(
        kernel,
        grid=(steps,),
        in_specs=[SMEM, VMEM, pl.BlockSpec((D, width), lambda i: (0, i)), pl.BlockSpec((1, width), lambda i: (0, i))]
        + [ANY] * len(pieces),
        out_specs=[column, column, ANY],
        out_shape=[like(1024, 1024), like(1024, 1024), like(D, 1024)],
        scratch_shapes=[pltpu.VMEM((D, 1024), BF), pltpu.SemaphoreType.DMA((2, len(plan)))],
        compiler_params=params(),
        cost_estimate=cost(),
        name="hidden_units",
    )(places, in_vmem(normed), *in_hbm(weights, shift, *pieces))


def hidden_back(gradients, weights, slope):
    width = 256

    def kernel(left, weight, slope_ref, d_ref, sum_ref):
        value = jnp.dot(left[...], weight[...], preferred_element_type=F32) * slope_ref[...].astype(F32)
        value = value.astype(BF)
        d_ref[...] = value
        sum_ref[...] = jnp.sum(value.astype(F32), axis=0, keepdims=True)

    column = pl.BlockSpec((1024, width), lambda i: (0, i))
    return pl.pallas_call(
        kernel,
        grid=(1024 // width,),
        in_specs=[
            VMEM,
            pl.BlockSpec((D, width), lambda i: (0, i)),
            column,
        ],
        out_specs=[column, pl.BlockSpec((1, width), lambda i: (0, i))],
        out_shape=[like(1024, 1024), like(1, 1024, F32)],
        compiler_params=params(),
        cost_estimate=cost(),
        name="hidden_back",
    )(in_vmem(gradients), *in_hbm(weights, slope))


def apart(places, lefts, weights, standard=None):
    count = len(lefts)

    def kernel(places_ref, *refs):
        value_ref = refs[-1]
        value = sum(
            lax.dot_general(
                left[...],
                weight[...].reshape(-1, weight.shape[2]),
                (((1,), (1,)), ((), ())),
                preferred_element_type=F32,
            )
            for left, weight in zip(refs[:count], refs[count : 2 * count])
        )
        refs = refs[2 * count : -1]
        if standard is not None:
            standard_ref, refs = refs[0], refs[1:]
            refs[2][0:1, :] = jnp.sum(value * standard_ref[...].astype(F32), axis=0, keepdims=True)
            refs[2][1:2, :] = jnp.sum(value, axis=0, keepdims=True)
        value_ref[...] = value
        for h in range(2):
            for k in range(4):
                rows = pl.ds(pl.multiple_of(places_ref[4 * h + k] * TOK, TOK), TOK)
                refs[h][k * TOK : (k + 1) * TOK, :] = value_ref[rows, :].astype(BF)

    width = 512
    return pl.pallas_call(
        kernel,
        grid=(D // width,),
        in_specs=[SMEM]
        + [pl.BlockSpec(left.shape, lambda i: (0, 0), pipeline_mode=pl.Buffered(1)) for left in lefts]
        + [
            pl.BlockSpec((4, 128, left.shape[1]), lambda i, at=at: (i, 0, at))
            for left, (_, at) in zip(lefts, weights)
        ]
        + ([] if standard is None else [pl.BlockSpec((1024, width), lambda i: (0, i))]),
        out_specs=[pl.BlockSpec((512, width), lambda i: (0, i))] * 2
        + ([] if standard is None else [pl.BlockSpec((2, width), lambda i: (0, i))]),
        out_shape=[like(512, D)] * 2 + ([] if standard is None else [like(2, D, F32)]),
        scratch_shapes=[pltpu.VMEM((1024, width), F32)],
        compiler_params=params(),
        cost_estimate=cost(),
        name="apart",
    )(places, *in_hbm(*lefts, *(weight for weight, _ in weights), *(() if standard is None else (standard,))))


def token_sum1(near, got):
    def kernel(places_ref, near_ref, got_ref, send_ref):
        send_ref[...] = (near_ref[...].astype(F32) + got_ref[...].astype(F32)).astype(BF)

    return kernel, [(near, 256, 1), (got, 256, 1)], [(256, D, BF)], ()


def token_sum2(near, got, back):
    def kernel(places_ref, near_ref, got_ref, back_ref, send_ref):
        value = near_ref[...].astype(F32) + got_ref[...].astype(F32) + back_ref[...].astype(F32)
        send_ref[...] = value.astype(BF)

    return kernel, [(near, TOK, 1), (got, TOK, 1), (back, TOK, 1)], [(TOK, D, BF)], ()


ROWS = pl.BlockSpec((TOK // 4, D), lambda i: (i, 0))
ONE_ROW = pl.BlockSpec((1, D), lambda i: (0, 0))


def finish_output(near, got, back, last, residual, shift):
    def kernel(near_ref, got_ref, back_ref, last_ref, residual_ref, shift_ref, out_ref):
        value = sum(ref[...].astype(F32) for ref in (near_ref, got_ref, back_ref, last_ref))
        value = residual_ref[...].astype(F32) + value + shift_ref[...]
        out_ref[...] = outside(value.astype(BF))

    return pl.pallas_call(
        kernel,
        grid=(4,),
        in_specs=[ROWS] * 5 + [ONE_ROW],
        out_specs=ROWS,
        out_shape=like(TOK, D),
        compiler_params=params(),
        cost_estimate=cost(),
        name="finish_output",
    )(*in_hbm(near, got, back, last, residual, shift))


def finish_grad(near, got, back, last, residual, gradient, gain):
    def kernel(near_ref, got_ref, back_ref, last_ref, residual_ref, gradient_ref, gain_ref, out_ref):
        value = sum(ref[...].astype(F32) for ref in (near_ref, got_ref, back_ref, last_ref))
        value = value * gain_ref[...]
        rows = residual_ref[...].astype(F32)
        rows = rows - jnp.mean(rows, axis=1, keepdims=True)
        inverse = lax.rsqrt(jnp.mean(rows * rows, axis=1, keepdims=True) + EPS)
        rows = rows * inverse
        plain = jnp.mean(value, axis=1, keepdims=True)
        cross = jnp.mean(value * rows, axis=1, keepdims=True)
        out_ref[...] = outside(gradient_ref[...].astype(F32) + inverse * (value - plain - rows * cross))

    return pl.pallas_call(
        kernel,
        grid=(4,),
        in_specs=[ROWS] * 6 + [ONE_ROW],
        out_specs=ROWS,
        out_shape=like(TOK, D, F32),
        compiler_params=params(),
        cost_estimate=cost(),
        name="finish_grad",
    )(*in_hbm(near, got, back, last, residual, gradient, gain))


def doc_positions(segments):
    length = segments.shape[0]
    places = jnp.arange(length, dtype=jnp.int32)
    boundary = jnp.concatenate([jnp.ones((1,), dtype=jnp.bool_), segments[1:] != segments[:-1]])
    doc_start = lax.cummax(jnp.where(boundary, places, jnp.zeros_like(places)), axis=0)
    return places - doc_start


def rotary_tables(positions):
    lane = jnp.arange(128, dtype=jnp.int32) % HD
    half_rot = ROT // 2
    frequency = 10000.0 ** (-(2.0 * (lane % half_rot).astype(F32)) / ROT)
    angles = positions.astype(F32)[:, None] * jnp.where(lane < ROT, frequency, 0.0)
    sine = jnp.sin(angles)
    before = jnp.where(lane < half_rot, -sine, 0.0)
    after = jnp.where((lane >= half_rot) & (lane < ROT), sine, 0.0)
    return jnp.concatenate([jnp.cos(angles), before, after], axis=1)


def attention_kernel(
    proj_ref, shift_ref, table_ref, column_ref, row_ref, grad_ref, weight_ref, mixed_ref, d_proj_ref, sums_ref, mask_ref
):
    start, last = column_ref[:, 0:1], column_ref[:, 1:2]
    where = row_ref[0]
    mask_ref[...] = jnp.where((where >= start) & (where <= last), 0.0, MASKED)
    cosine, before, after = (table_ref[:, i * 128 : (i + 1) * 128] for i in range(3))
    lane = lax.broadcasted_iota(jnp.int32, (SEQ, 128), 1)

    def turn(value, sign):
        shifted = pltpu.roll(value, 112, 1) * before + pltpu.roll(value, 16, 1) * after
        return value * cosine + sign * shifted

    def part(index, pair):
        at = slice(index * 256 + pair * 128, index * 256 + pair * 128 + 128)
        return proj_ref[:, at] + shift_ref[:, at]

    def dot(a, b, dims):
        return lax.dot_general(a, b, (dims, ((), ())), preferred_element_type=F32)

    d_attended = jnp.dot(grad_ref[...], weight_ref[...].reshape(D, 256), preferred_element_type=F32).astype(BF)
    for pair in range(2):
        at = slice(pair * 128, pair * 128 + 128)
        queries = (turn(part(0, pair), 1.0).astype(BF).astype(F32) * HD**-0.5).astype(BF)
        keys = turn(part(1, pair), 1.0).astype(BF)
        values = part(2, pair).astype(BF)
        d_out = d_attended[:, at]
        results = []
        for head in range(2):
            own = (lane >= head * HD) & (lane < (head + 1) * HD)
            own_queries = jnp.where(own, queries, jnp.zeros_like(queries))
            own_d_out = jnp.where(own, d_out, jnp.zeros_like(d_out))
            scores = dot(own_queries, keys, ((1,), (1,))) + mask_ref[...]
            exponent = jnp.exp(scores - jnp.max(scores, axis=1, keepdims=True))
            soft = exponent * (1.0 / jnp.sum(exponent, axis=1, keepdims=True))
            soft_low = soft.astype(BF)
            mixed = dot(soft_low, values, ((1,), (0,)))
            d_soft = dot(own_d_out, values, ((1,), (1,)))
            inner = jnp.sum(soft * d_soft, axis=1, keepdims=True)
            d_scores = (soft * (d_soft - inner)).astype(BF)
            d_queries = dot(d_scores, keys, ((1,), (0,))) * HD**-0.5
            d_keys = dot(d_scores, own_queries, ((0,), (0,)))
            d_values = dot(soft_low, own_d_out, ((0,), (0,)))
            results.append((mixed, d_queries, d_keys, d_values))
        first, second = results
        mixed_ref[:, at] = jnp.where(lane < HD, first[0], second[0]).astype(BF)
        d_queries = turn(jnp.where(lane < HD, first[1], second[1]), -1.0).astype(BF)
        d_keys = turn(first[2] + second[2], -1.0).astype(BF)
        d_values = (first[3] + second[3]).astype(BF)
        for index, value in enumerate((d_queries, d_keys, d_values)):
            at = slice(index * 256 + pair * 128, index * 256 + pair * 128 + 128)
            d_proj_ref[:, at] = value
            sums_ref[0, :, at] = jnp.sum(value.astype(F32), axis=0, keepdims=True)


def attention(projected, shift, tables, columns, rows, gradients, weights):
    count = projected.shape[0] // SEQ
    return pl.pallas_call(
        attention_kernel,
        grid=(count,),
        in_specs=[
            pl.BlockSpec((SEQ, 768), lambda i: (i, 0)),
            pl.BlockSpec((1, 768), lambda i: (0, 0)),
            pl.BlockSpec((SEQ, 384), lambda i: (i, 0)),
            pl.BlockSpec((SEQ, 2), lambda i: (i, 0)),
            pl.BlockSpec((1, 1, SEQ), lambda i: (i, 0, 0)),
            pl.BlockSpec((SEQ, D), lambda i: (i, 0)),
            pl.BlockSpec((16, 128, 256), lambda i: (0, 0, 3), pipeline_mode=pl.Buffered(1)),
        ],
        out_specs=[
            pl.BlockSpec((SEQ, 256), lambda i: (i, 0)),
            pl.BlockSpec((SEQ, 768), lambda i: (i, 0)),
            pl.BlockSpec((1, 1, 768), lambda i: (i, 0, 0)),
        ],
        out_shape=[
            pltpu.HBM((count * SEQ, 256), BF),
            pltpu.HBM((count * SEQ, 768), BF),
            pltpu.HBM((count, 1, 768), F32),
        ],
        scratch_shapes=[pltpu.VMEM((SEQ, SEQ), F32)],
        compiler_params=pltpu.CompilerParams(vmem_limit_bytes=VMEM_LIMIT),
        cost_estimate=cost(),
        name="attention",
    )(*in_hbm(projected, shift, tables, columns, rows, gradients, weights))


def body(
    residual_in,
    segment_ids,
    out_grad,
    ln_gain,
    ln_bias,
    w_qkv,
    b_qkv,
    w_out,
    b_attn_out,
    w_up,
    b_up,
    w_down,
    b_mlp_out,
):
    y_lo, x, z, y_hi, core = (lax.axis_index(name).astype(jnp.int32) for name in AXES)
    low_index = y_lo[None]
    low = y_lo == 0

    def around(c):
        return [c, c ^ (1 + 2 * core), c ^ (3 - 2 * core), c ^ 2]

    y_places = [
        y_lo * 2 + y_hi,
        (1 - y_lo) * 2 + (y_hi ^ core),
        (1 - y_lo) * 2 + (y_hi ^ (1 - core)),
        y_lo * 2 + (1 - y_hi),
    ]
    ring_places = jnp.stack(
        around(x)
        + around(z)
        + [y_lo, 1 - y_lo]
        + y_places
        + [2 * k + core for k in range(4)]
        + [2 * k + 1 - core for k in range(4)]
    )
    part_places = jnp.stack(
        [2 * p + core for p in y_places] + [2 * y_places[k] + 1 - core for k in (0, 2, 1, 3)]
    )

    small = jnp.concatenate(
        [ln_gain, ln_bias, b_attn_out, b_mlp_out, b_up.reshape(64), b_qkv.reshape(48), jnp.zeros((80,), BF)]
    )[None]
    small, residual_in = bar((small, residual_in))
    residual, gradient, attn_own, attn_away, rest_own, rest_away = prepare(
        low_index, residual_in, out_grad, w_qkv.transpose(1, 0, 2), w_out.T, w_up, w_down.T
    )

    def widen(rows, axis, index):
        got = flip(rows, axis)
        return jnp.where(index == 0, jnp.concatenate([rows, got]), jnp.concatenate([got, rows]))

    attn_got = flip(attn_away, "y_lo")
    small = widen(small, "core", core)
    small = widen(small, "y_hi", y_hi)
    attn_got, small, residual, gradient, rest_away = bar((attn_got, small, residual, gradient, rest_away))
    small = jnp.pad(small.reshape(1, 1024), ((0, 15), (0, 0)))

    def token_positions():
        far_segments = flip(segment_ids, "y_lo")
        places = jnp.arange(SEQ, dtype=jnp.int32)
        positions = jnp.concatenate(
            [doc_positions(jnp.where(low, a, b)) for a, b in ((segment_ids, far_segments), (far_segments, segment_ids))]
        )
        places = jnp.concatenate([places, places])
        columns = jnp.stack([places - positions, places], axis=1)
        return columns, places.reshape(2, 1, SEQ), rotary_tables(positions)

    def joined(own, first):
        plan = [(source, 0, TOK, 0, D, 0, TOK * source, None, 0, 0) for source in range(2)]
        return plan, [(2 * TOK, D)], [own, first], False

    def of_core(own, first, second):
        plan = [
            (source, row, TOK, 0, D, 0, 0, 10 + k, TOK, 0)
            for k, (source, row) in enumerate(((0, 0), (1, 0), (2, 0), (2, TOK)))
        ]
        return plan, [(SEQ, D)], [own, first, second], False

    def of_both(mine, other, stay=False):
        plan = [
            (source, k * TOK, TOK, 0, D, 0, 0, 14 + 4 * source + k, TOK, 0) for source in range(2) for k in range(4)
        ]
        return plan, [(1024, D)], [mine, other], stay

    plan = [(source, 0, BLK, 0, 1024, 0, 0, 8 + source, BLK, 0) for source in range(2)]
    plan.append((2, 0, 16, 0, 1024, 0, 128, None, 0, 0))
    ((shard,),) = copies(ring_places, (plan, [(144, 1024)], [attn_own, attn_got, small], False))
    shard, residual, gradient, rest_away = bar((shard, residual, gradient, rest_away))
    attn_all = lax.all_gather(shard, ("x", "z"), axis=0)
    token_first = swap_y(residual, 0)
    rest_got = flip(rest_away, "y_lo")
    token_first, rest_got, gradient = bar((token_first, rest_got, gradient))
    plan = [
        (source, 0, BLK, 1024 * h, 1024, h, 0, 8 + source, BLK, 0) for source in range(2) for h in range(2)
    ]
    (tokens_sent,), sends = copies(
        ring_places, joined(residual, token_first), (plan, [(128, 1024)] * 2, [rest_own, rest_got], False)
    )
    rest_gather = Gather(*sends)
    tokens_sent, sends, gradient = bar((tokens_sent, sends, gradient))
    token_second = swap_y(tokens_sent, 1)
    grad_first = swap_y(gradient, 0)
    got = gather_step(1, sends)
    token_second, grad_first, got = bar((token_second, grad_first, got))
    (mine,), (grads_sent,), sends = copies(
        ring_places,
        of_core(residual, token_first, token_second),
        joined(gradient, grad_first),
        rest_gather.sending(got),
    )
    mine, grads_sent, sends = bar((mine, grads_sent, sends))
    other = flip(mine, "core")
    grad_second = swap_y(grads_sent, 1)
    positions = token_positions()
    got, other, mine, grad_second, positions = bar((gather_step(2, sends), other, mine, grad_second, positions))
    tokens = (mine, other)
    rest_gather.pair, (mine,) = copies(
        ring_places, rest_gather.joining(got, False), of_core(gradient, grad_first, grad_second)
    )
    sends, mine, table = bar((rest_gather.pair, mine, attn_all[:, 128, :][None]))
    other = flip(mine, "core")
    other_table = flip(table, "y_lo")
    other, mine, other_table, table, sends, tokens = bar((other, mine, other_table, table, sends, tokens))
    got = gather_step(3, sends)
    columns, rows, tables = positions

    table = jnp.where(low, jnp.concatenate([table, other_table]), jnp.concatenate([other_table, table]))
    table = table.reshape(2, 16, 4, 256).astype(F32)
    vectors = table[..., :64].reshape(2, 16, 4, 4, 16).transpose(3, 1, 0, 2, 4).reshape(4, D)
    gain, shift, out_shift = vectors[0:1], vectors[1:2], vectors[2:3] + vectors[3:4]
    shifts = lax.dynamic_index_in_dim(table.reshape(2, 16, 4, 256), y_hi * 2 + core, 2, False)
    shifts = lax.dynamic_index_in_dim(shifts, y_lo, 0, False)
    up_shift = shifts[:, 64:128].reshape(1, 1024)
    qkv_shift = shifts[:, 128:176].reshape(16, 3, 16).transpose(1, 0, 2).reshape(1, 768)

    standard, normed, projected = norm_and_project(core[None], *tokens, gain, shift, attn_all)
    got, other, mine, normed, projected = bar((got, other, mine, normed, projected))
    sends, (grad_all,) = copies(ring_places, rest_gather.sending(got), of_both(mine, other))
    sends, grad_all, projected = bar((sends, grad_all, projected))
    rest_got = gather_step(4, sends)
    mixed, d_projected, sums = attention(projected, qkv_shift, tables, columns, rows, grad_all, attn_all)
    attn_sum = attention_gradient(normed, d_projected, grad_all, mixed)
    attn_sum, rest_got, normed = bar((attn_sum, rest_got, normed))
    attn_sum = lax.psum_scatter(attn_sum, ("x", "z"), scatter_dimension=0, tiled=True)

    ((up_all,),) = copies(ring_places, rest_gather.joining(rest_got, True))
    hidden, slope, down_all = hidden_units(ring_places, normed, up_all, up_shift, *rest_gather.right())
    down_sum = Scatter(ring_places, grad_all, hidden)
    sends, mixed, hidden, slope, grad_all = bar((down_sum.first, mixed, hidden, slope, grad_all))
    down_got = scatter_step(1, sends)
    d_hidden, up_shift_part = hidden_back(grad_all, down_all, slope)
    near, away = apart(part_places, [mixed, hidden], [(attn_all, 3), (down_all.reshape(16, 128, 1024), 0)])
    near, away, d_hidden, down_got = bar((near, away, d_hidden, down_got))
    (down_sends,) = add(ring_places, down_sum.send2(down_got))
    down_sends, away, d_hidden = bar((down_sends, away, d_hidden))
    down_got = scatter_step(2, down_sends)
    out_got = flip(away, "core")
    up_sum = Scatter(ring_places, normed, d_hidden)
    up_sends, down_got, out_got = bar((up_sum.first, down_got, out_got))
    down_sends, (out_send,) = add(ring_places, down_sum.send3(down_got), token_sum1(near, out_got))
    down_sum.keep = down_sends[2:]

    up_sends, down_sends, out_send, d_hidden = bar((up_sends, down_sends[:2], out_send, d_hidden))
    up_got = scatter_step(1, up_sends)
    out_back = swap_y(out_send, 1)
    down_got = scatter_step(3, down_sends)
    d_near, d_away, vector_parts = apart(
        part_places,
        [d_projected, d_hidden],
        [(attn_all, 0), (up_all.reshape(16, 128, 1024), 0)],
        standard,
    )
    d_away, up_got, out_back, down_got, vector_parts = bar((d_away, up_got, out_back, down_got, vector_parts))
    up_sends, down_sends, (out_send,) = add(
        ring_places, up_sum.send2(up_got), down_sum.send4(down_got), token_sum2(near, out_got, out_back)
    )
    up_sends, down_sends, out_send, d_away, vector_parts = bar(
        (up_sends, down_sends, out_send, d_away, vector_parts)
    )
    d_got = flip(d_away, "core")
    up_got = scatter_step(2, up_sends)
    out_last = swap_y(out_send, 0)
    out_shift_part = jnp.sum(gradient.astype(F32), axis=0, keepdims=True)
    parts = jnp.concatenate([vector_parts, out_shift_part]).reshape(3, 16, 8, 16)
    parts = parts.transpose(1, 2, 0, 3).reshape(16, 384)
    sums = jnp.sum(sums, axis=(0, 1))
    line = jnp.concatenate(
        [
            parts,
            up_shift_part.reshape(16, 64),
            sums.reshape(3, 16, 16).transpose(1, 0, 2).reshape(16, 48),
            jnp.zeros((16, 16), F32),
        ],
        axis=1,
    )
    offsets = [0]
    for _, _, bits in RING_STEPS:
        offsets = offsets + [o ^ bits for o in offsets]
    here = (4 * x + z) ^ jnp.array(offsets, jnp.int32)
    order = (here[:, None] == jnp.arange(16, dtype=jnp.int32)[None, :]).astype(F32)
    line = jnp.dot(order, line, precision=lax.Precision.HIGHEST)

    def fold(line, step):
        axis, mask, _ = RING_STEPS[step]
        count = line.shape[0] // 2
        return line[:count] + flip4(line[count:], axis, mask)

    def narrow(part, axis, index):
        part = part.reshape(2, -1)
        return jnp.where(index == 0, part[0], part[1]) + flip(jnp.where(index == 0, part[1], part[0]), axis)

    line = fold(fold(line, 3), 2)
    d_got, up_got, down_sends, out_last, line = bar((d_got, up_got, down_sends, out_last, line))
    up_sends, (d_send,) = add(ring_places, up_sum.send3(up_got), token_sum1(d_near, d_got))
    up_sum.keep = up_sends[2:]
    up_sends, d_send, line = bar((up_sends[:2], d_send, line))
    d_back = swap_y(d_send, 1)
    up_got = scatter_step(3, up_sends)
    line = fold(fold(line, 1), 0)[0]
    part = narrow(line[:384], "y_lo", y_lo)
    d_back, up_got, part, down_sends = bar((d_back, up_got, part, down_sends))
    up_sends, (d_send,) = add(ring_places, up_sum.send4(up_got), token_sum2(d_near, d_got, d_back))
    up_sends, d_send, part, down_sends = bar((up_sends, d_send, part, down_sends))
    d_last = swap_y(d_send, 0)
    up_got = scatter_step(4, up_sends)
    down_got = scatter_step(4, down_sends)
    d_last, up_got, down_got, part, attn_sum, out_last = bar((d_last, up_got, down_got, part, attn_sum, out_last))
    up_result, down_result = add(ring_places, up_sum.finish(up_got), down_sum.finish(down_got), steps=1)
    lower, upper = attn_sum[:BLK], attn_sum[BLK:]
    attn_own, attn_away = jnp.where(low, lower, upper), jnp.where(low, upper, lower)
    up_away, down_away, attn_away, part, d_last, out_last = bar(
        (up_result[1], down_result[1], attn_away, part, d_last, out_last)
    )
    up_far = flip(up_away, "y_lo")
    down_far = flip(down_away, "y_lo")
    attn_far = flip(attn_away, "y_lo")
    part = narrow(narrow(part, "y_hi", y_hi), "core", core)
    grad_in = finish_grad(d_near, d_got, d_back, d_last, residual, gradient, gain)
    output = finish_output(near, out_got, out_back, out_last, residual, out_shift)
    attn_far, up_far, down_far, part, output, grad_in = bar((attn_far, up_far, down_far, part, output, grad_in))
    sum_up, sum_qkv, sum_out, sum_down = whole(
        low_index,
        (up_result[0], up_far, ((1024, 1),)),
        (attn_own, attn_far, ((256, 3), (256, 1))),
        (down_result[0], down_far, ((1024, 1),)),
    )
    grad_gain, grad_shift, grad_out_shift = part[:16], part[16:32], part[32:]
    return (
        output,
        grad_in,
        grad_gain,
        grad_shift,
        sum_qkv.transpose(1, 0, 2),
        line[448:496].reshape(3, 1, 16),
        sum_out[0].T,
        grad_out_shift,
        sum_up[0],
        line[384:448].reshape(1, 64),
        sum_down[0].T,
        grad_out_shift,
    )


def solution(mesh):
    fine = Mesh(mesh.devices.reshape(2, 4, 4, 2, 2), AXES)
    dp = ("y_lo", "x", "z")
    tensor = ("y_hi", "core")
    every = AXES
    in_specs = (
        P(every, None),
        P(dp),
        P(every, None),
        P(every),
        P(every),
        P(dp, None, tensor),
        P(None, tensor, dp),
        P(tensor, dp),
        P(every),
        P(dp, tensor),
        P(tensor, dp),
        P(tensor, dp),
        P(every),
    )
    out_specs = (
        P(every, None),
        P(every, None),
        P(every),
        P(every),
        P(dp, None, tensor),
        P(None, tensor, dp),
        P(tensor, dp),
        P(every),
        P(dp, tensor),
        P(tensor, dp),
        P(tensor, dp),
        P(every),
    )
    return jax.shard_map(body, mesh=fine, in_specs=in_specs, out_specs=out_specs, check_vma=False)
```

```python
import jax
import jax.numpy as jnp
from jax import lax
from jax.experimental import pallas as pl
from jax.experimental.pallas import tpu as pltpu
from jax.sharding import Mesh, PartitionSpec as P

HD = 64
ROT = 32
EPS = 1e-05
MASKED = -1e30
D = 2048
SEQ = 512
TOK = 128
BLK = 64
VMEM_LIMIT = 24 * 1024 * 1024
BF = jnp.bfloat16
F32 = jnp.float32
AXES = ("y_lo", "x", "z", "y_hi", "core")


bar = lax.optimization_barrier


def params(limit=VMEM_LIMIT):
    return pltpu.CompilerParams(vmem_limit_bytes=limit)


def cost():
    return pl.CostEstimate(flops=1000, bytes_accessed=1000, transcendentals=0)


def like(rows, columns, kind=BF):
    return pltpu.HBM((rows, columns), kind)


class Arrived:
    def __init__(self, value):
        self.value, self.shape = value, value.shape


def in_hbm(*values):
    return tuple(
        value.value if isinstance(value, Arrived) else pltpu.with_memory_space_constraint(value, pltpu.HBM)
        for value in values
    )


def in_vmem(value):
    return pltpu.with_memory_space_constraint(value, pltpu.VMEM)


SMEM = pl.BlockSpec(memory_space=pltpu.SMEM)
VMEM = pl.BlockSpec(memory_space=pltpu.VMEM)
ANY = pl.BlockSpec(memory_space=pl.ANY)


def ring(value, axis, step):
    masks = (1, 3) if step == 0 else (3, 1)
    table = [(i * 2 + c, (i ^ masks[c]) * 2 + c) for i in range(4) for c in range(2)]
    return lax.ppermute(value, (axis, "core"), table)


def ring_pair(pair, axes, step):
    pair = bar(tuple(pair))
    return bar(tuple(ring(value, axis, step) for value, axis in zip(pair, axes)))


def swap_y(value, step):
    masks = (1, 3) if step == 0 else (3, 1)

    def place(y, c):
        return ((y % 2) * 2 + y // 2) * 2 + c

    table = [(place(y, c), place(y ^ masks[c], c)) for y in range(4) for c in range(2)]
    return lax.ppermute(value, ("y_lo", "y_hi", "core"), table)


def flip(value, axis):
    return lax.ppermute(value, axis, [(0, 1), (1, 0)])


def copies(places, *jobs):
    sources = [source for _, _, given, _ in jobs for source in given]
    shapes = [(shape, stay) for _, made, _, stay in jobs for shape in made]
    plans, low, made = [], 0, 0
    for plan, results, given, stay in jobs:
        for source, row, rows, column, columns, target, to, place, unit, across in plan:
            plans.append((source + low, row, rows, column, columns, target + made, to, place, unit, across, stay))
        low += len(given)
        made += len(results)

    def kernel(places_ref, *refs):
        inputs, refs = refs[: len(sources)], refs[len(sources) :]
        outputs, spare, sems = refs[: len(shapes)], list(refs[len(shapes) : -1]), refs[-1]
        stages = [output if stay else spare.pop(0) for output, (_, stay) in zip(outputs, shapes)]
        moves = []
        for i, (source, row, rows, column, columns, target, to, place, unit, across, stay) in enumerate(plans):
            if place is not None:
                to = pl.multiple_of(to + places_ref[place] * unit, rows)
            at = (pl.ds(to, rows), pl.ds(across, columns))
            stage = stages[target].at[at]
            arrive = pltpu.make_async_copy(
                inputs[source].at[pl.ds(row, rows), pl.ds(column, columns)], stage, sems.at[0, i]
            )
            arrive.start()
            leave = None if stay else pltpu.make_async_copy(stage, outputs[target].at[at], sems.at[1, i])
            moves.append((arrive, leave))
        for arrive, leave in moves:
            arrive.wait()
            if leave is not None:
                leave.start()
        for _, leave in moves:
            if leave is not None:
                leave.wait()

    outs = pl.pallas_call(
        kernel,
        in_specs=[SMEM] + [ANY] * len(sources),
        out_specs=[VMEM if stay else ANY for _, stay in shapes],
        out_shape=[pltpu.VMEM(shape, BF) if stay else like(*shape) for shape, stay in shapes],
        scratch_shapes=[pltpu.VMEM(shape, BF) for shape, stay in shapes if not stay]
        + [pltpu.SemaphoreType.DMA((2, len(plans)))],
        compiler_params=params(),
        cost_estimate=cost(),
        name="put_together",
    )(places, *in_hbm(*sources))
    results = []
    for _, made, _, _ in jobs:
        results.append(outs[: len(made)])
        outs = outs[len(made) :]
    return results


def flip4(value, axis, mask):
    return lax.ppermute(value, axis, [(i, i ^ mask) for i in range(4)])


RING_STEPS = (("z", 1, 1), ("z", 3, 3), ("x", 1, 4), ("x", 3, 12))


class Gather:
    def __init__(self, left, right):
        self.pair = (left, right)

    def sending(self, got):
        self.first = tuple(Arrived(value) for value in got)
        rows, width = self.pair[0].shape
        plan = [(2 * h + k, 0, rows, 0, width, h, k * rows, None, 0, 0) for h in range(2) for k in range(2)]
        sources = [value for both in zip(self.pair, self.first) for value in both]
        return plan, [(2 * rows, width)] * 2, sources, False

    def joining(self, got, last):
        self.last = tuple(Arrived(value) for value in got)
        rows, width = self.pair[0].shape
        sources = [value for each in zip(self.pair, self.first, self.last) for value in each]
        if last:
            return self.ordered(0), [(2048, width)], sources[:3], False
        plan = []
        for h in range(2):
            for k, (source, row) in enumerate(((0, 0), (1, 0), (2, 0), (2, rows))):
                plan.append((source + 3 * h, row, rows, 0, width, h, 0, 4 * h + k, rows, 0))
        return plan, [(4 * rows, width)] * 2, sources, False

    def ordered(self, h):
        rows, width = self.pair[0].shape
        plan = []
        for k, (source, row) in enumerate(((0, 0), (1, 0), (2, 0), (2, rows))):
            for i in range(4):
                to, unit = ((i * 512, 128), (i * 128, 512))[h]
                plan.append((source, row + i * 128, 128, 0, width, 0, to, 4 * (1 - h) + k, unit, 0))
        return plan

    def right(self):
        return self.ordered(1), (self.pair[1], self.first[1], self.last[1])


def gather_step(step, pair):
    return ring_pair(pair, ("x", "z") if step < 3 else ("z", "x"), 1 - step % 2)


def scatter_step(step, pair):
    return ring_pair(pair, ("x", "z") if step < 3 else ("z", "x"), step % 2)


class Scatter:
    def __init__(self, places, index, left, right):
        self.places, self.index = places, index
        tokens, width = right.shape
        self.width = half = width // 2

        def kernel(places_ref, left_ref, right_ref, *refs):
            outs, (rights, *stages), sems = refs[:6], refs[6:-1], refs[-1]
            fetch = [
                pltpu.make_async_copy(right_ref.at[:, pl.ds(h * half, half)], rights.at[h], sems.at[h]) for h in range(2)
            ]
            for copy in fetch:
                copy.start()
            order = [2, 3, 1, 0]
            stored = []
            for h in range(2):
                fetch[h].wait()
                for i, k in enumerate(order):
                    if h == 0:
                        block = left_ref[:, pl.ds(pl.multiple_of(places_ref[k] * 512, 512), 512)]
                    else:
                        z = places_ref[4 + k]
                        block = jnp.concatenate(
                            [left_ref[:, pl.ds(pl.multiple_of(n * 512 + z * 128, 128), 128)] for n in range(4)], axis=1
                        )
                    value = lax.dot_general(
                        block,
                        rights[h],
                        (((0,), (0,)), ((), ())),
                        preferred_element_type=F32,
                    ).astype(BF)
                    stage = stages[h].at[pl.ds(i * 512, 512)]
                    stage[...] = value
                    out = outs[h].at[pl.ds(i * 512, 512)] if i < 2 else outs[2 * i - 2 + h]
                    copy = pltpu.make_async_copy(stage, out, sems.at[2 + 4 * h + i])
                    copy.start()
                    stored.append(copy)
            for copy in stored:
                copy.wait()

        outs = pl.pallas_call(
            kernel,
            in_specs=[SMEM, VMEM, ANY],
            out_specs=[ANY] * 6,
            out_shape=[like(1024, half)] * 2 + [like(512, half)] * 4,
            scratch_shapes=[
                pltpu.VMEM((2, tokens, half), BF),
                pltpu.VMEM((2048, half), BF),
                pltpu.VMEM((2048, half), BF),
                pltpu.SemaphoreType.DMA((10,)),
            ],
            compiler_params=params(),
            cost_estimate=cost(),
            name="gradient",
        )(places, in_vmem(left), *in_hbm(right))
        self.first, self.next, self.keep = outs[:2], outs[2:4], outs[4:]

    def part(self, got, rows, at):
        half = self.width // 2
        alone = got[0].shape[1] == self.width
        return [
            (Arrived(value), rows, at, half, (lambda i: i) if alone else (lambda i: 2 * i + self.index)) for value in got
        ]

    def send2(self, got):
        self.got = got

        def kernel(places_ref, *refs):
            for h in range(2):
                refs[4 + h][...] = (refs[h][...].astype(F32) + refs[2 + h][...].astype(F32)).astype(BF)

        return kernel, [*self.next, *self.part(got, 512, 1)], [(512, self.width, BF)] * 2, ()

    def send3(self, last):
        def kernel(places_ref, *refs):
            total = refs[-1]
            for h in range(2):
                keep, arrived, later, send, own = (refs[2 * k + h] for k in range(5))
                total[...] = keep[...].astype(F32) + arrived[...].astype(F32) + later[...].astype(F32)
                own_at, first, second, across = (
                    pl.ds(pl.multiple_of(places_ref[4 * (1 - h) + k] * 128, 128), 128) for k in range(4)
                )
                send[:128, :] = total[second, :].astype(BF)
                send[128:, :] = total[across, :].astype(BF)
                own[:128, :] = total[first, :].astype(BF)
                own[128:, :] = total[own_at, :].astype(BF)

        return (
            kernel,
            [*self.keep, *self.part(self.got, 512, 0), *self.part(last, 512, 0)],
            [(256, self.width, BF)] * 4,
            [pltpu.VMEM((512, self.width // 2), F32)],
        )

    def send4(self, got):
        self.got = got

        def kernel(places_ref, *refs):
            for h in range(2):
                refs[4 + h][...] = (refs[h][...].astype(F32) + refs[2 + h][...].astype(F32)).astype(BF)

        return (
            kernel,
            [*((value, 128, 0) for value in self.keep), *self.part(got, 128, 1)],
            [(128, self.width, BF)] * 2,
            (),
        )

    def finish(self, last):
        width, half = self.width, self.width // 2

        def kernel(places_ref, *refs):
            total = refs[-1]
            for h in range(2):
                for i in range(2):
                    at = slice(i * half, (i + 1) * half)
                    keep, arrived, later = refs[h][:, at], refs[2 + 2 * h + i][...], refs[6 + 2 * h + i][...]
                    total[:, h * width + i * half : h * width + (i + 1) * half] = (
                        keep.astype(F32) + arrived.astype(F32) + later.astype(F32)
                    )
            low = places_ref[8]
            refs[10][...] = total[pl.ds(pl.multiple_of(low * BLK, BLK), BLK), :]
            refs[11][...] = total[pl.ds(pl.multiple_of((1 - low) * BLK, BLK), BLK), :].astype(BF)

        def parts(got):
            return [
                (Arrived(value), 128, 0, half, lambda i, k=k: 2 * k + self.index) for value in got for k in range(2)
            ]

        return (
            kernel,
            [*((value, 128, 1) for value in self.keep), *parts(self.got), *parts(last)],
            [(BLK, 2 * width, F32), (BLK, 2 * width, BF)],
            [pltpu.VMEM((128, 2 * width), F32)],
        )


def add(places, *jobs, steps=2):
    def full(value, rows, at, columns=None, across=lambda i: i):
        return value, rows, at, columns or value.shape[1] // steps, across

    jobs = [
        (kernel, [full(*v) if isinstance(v, tuple) else full(v, v.shape[0], 0) for v in inputs], outs, scratch)
        for kernel, inputs, outs, scratch in jobs
    ]
    inputs = [value for _, given, _, _ in jobs for value in given]
    outs = [out for _, _, made, _ in jobs for out in made]

    def kernel(places_ref, *refs):
        given, made, spare = refs[: len(inputs)], refs[len(inputs) : len(inputs) + len(outs)], refs[len(inputs) + len(outs) :]
        for one, ins, results, scratch in jobs:
            one(places_ref, *given[: len(ins)], *made[: len(results)], *spare[: len(scratch)])
            given, made, spare = given[len(ins) :], made[len(results) :], spare[len(scratch) :]

    results = pl.pallas_call(
        kernel,
        grid=(steps,),
        in_specs=[SMEM]
        + [
            pl.BlockSpec((rows, columns), lambda i, at=at, across=across: (at, across(i)))
            for _, rows, at, columns, across in inputs
        ],
        out_specs=[pl.BlockSpec((rows, columns // steps), lambda i: (0, i)) for rows, columns, _ in outs],
        out_shape=[like(*shape) for shape in outs],
        scratch_shapes=[each for _, _, _, scratch in jobs for each in scratch],
        compiler_params=params(),
        cost_estimate=cost(),
        name="add",
    )(places, *in_hbm(*(value for value, *_ in inputs)))
    split = []
    for _, _, made, _ in jobs:
        split.append(results[: len(made)])
        results = results[len(made) :]
    return split


def together(*jobs):
    first = jobs[0][2][:2]

    def kernel(places_ref, *refs):
        counts = [len(inputs) for _, inputs, _, _ in jobs]
        refs, shared, rest = refs[: sum(counts)], refs[sum(counts) : sum(counts) + 2], list(refs[sum(counts) + 2 :])
        made = [[rest.pop(0) for _ in outs[2:]] for _, _, outs, _ in jobs]
        spare = [[rest.pop(0) for _ in scratch] for _, _, _, scratch in jobs]
        for k, (one, inputs, _, _) in enumerate(jobs):
            widths = [ref.shape[1] // len(jobs) for ref in shared]
            views = [ref.at[:, pl.ds(k * width, width)] for ref, width in zip(shared, widths)]
            one(places_ref, *refs[: counts[k]], *views, *made[k], *spare[k])
            refs = refs[counts[k] :]

    return (
        kernel,
        [value for _, inputs, _, _ in jobs for value in inputs],
        [(rows, len(jobs) * columns, kind) for rows, columns, kind in first]
        + [out for _, _, outs, _ in jobs for out in outs[2:]],
        [each for _, _, _, scratch in jobs for each in scratch],
    )


def attention_gradient(normed, d_projected, gradients, mixed):
    def kernel(normed_ref, d_ref, grad_ref, mixed_ref, out_ref):
        rows = pl.ds(pl.multiple_of(pl.program_id(0) * 512, 512), 512)
        for left, right, at in ((normed_ref, d_ref, slice(0, 768)), (grad_ref, mixed_ref, slice(768, 1024))):
            out_ref[:, at] = lax.dot_general(
                left[:, rows], right[...], (((0,), (0,)), ((), ())), preferred_element_type=F32
            ).astype(BF)

    def fixed(width):
        return pl.BlockSpec((1024, width), lambda i: (0, 0), pipeline_mode=pl.Buffered(1))

    return pl.pallas_call(
        kernel,
        grid=(D // 512,),
        in_specs=[VMEM, fixed(768), VMEM, fixed(256)],
        out_specs=pl.BlockSpec((512, 1024), lambda i: (i, 0)),
        out_shape=like(D, 1024),
        compiler_params=params(),
        cost_estimate=cost(),
        name="attention_gradient",
    )(in_vmem(normed), *in_hbm(d_projected), in_vmem(gradients), *in_hbm(mixed))


def whole(low_index, *jobs):
    layouts = [each for _, _, layout in jobs for each in layout]

    def kernel(low_ref, *refs):
        halves, outs = refs[: 2 * len(jobs)], list(refs[2 * len(jobs) :])
        for k, (_, _, layout) in enumerate(jobs):
            at = 0
            for width, count in layout:
                out = outs.pop(0)
                mine = pl.ds(pl.multiple_of(low_ref[0] * width, width), width)
                theirs = pl.ds(pl.multiple_of((1 - low_ref[0]) * width, width), width)
                for i in range(count):
                    out[i, :, mine] = halves[2 * k][:, at : at + width].astype(F32)
                    out[i, :, theirs] = halves[2 * k + 1][:, at : at + width].astype(F32)
                    at += width

    return pl.pallas_call(
        kernel,
        in_specs=[SMEM] + [VMEM] * (2 * len(jobs)),
        out_specs=[VMEM] * len(layouts),
        out_shape=[pltpu.HBM((count, BLK, 2 * width), F32) for width, count in layouts],
        compiler_params=params(),
        cost_estimate=cost(),
        name="whole",
    )(low_index, *in_hbm(*(half for own, got, _ in jobs for half in (own, Arrived(got)))))


def inside(value):
    parts = [value[:, (low * 16 + n) * BLK : (low * 16 + n + 1) * BLK] for n in range(16) for low in range(2)]
    return jnp.concatenate(parts, axis=1)


def outside(value):
    parts = [value[:, (2 * n + low) * BLK : (2 * n + low + 1) * BLK] for low in range(2) for n in range(16)]
    return jnp.concatenate(parts, axis=1)


def prepare(low_index, residual, gradient, w_qkv, w_out, w_up, w_down, vectors):
    def kernel(low_ref, residual_ref, gradient_ref, qkv, out, up, down, *refs):
        *parts, tokens, grads, attn_own, attn_away, rest_own, rest_away, row = refs
        row[...] = jnp.concatenate([part[...].astype(F32) for part in parts] + [jnp.zeros((1, 80), F32)], axis=1).astype(BF)
        tokens[...] = inside(residual_ref[...])
        grads[...] = inside(gradient_ref[...])
        low = low_ref[0]
        for half, attn, rest in ((low, attn_own, rest_own), (1 - low, attn_away, rest_away)):
            narrow = pl.ds(pl.multiple_of(half * 256, 256), 256)
            wide = pl.ds(pl.multiple_of(half * 1024, 1024), 1024)
            for i in range(3):
                attn[:, i * 256 : (i + 1) * 256] = qkv[i, :, narrow]
            attn[:, 768:] = out[:, narrow]
            rest[:, :1024] = up[:, wide]
            rest[:, 1024:] = down[:, wide]

    return pl.pallas_call(
        kernel,
        in_specs=[SMEM] + [VMEM] * (6 + len(vectors)),
        out_specs=[VMEM] * 7,
        out_shape=[like(TOK, D)] * 2 + [like(BLK, 1024)] * 2 + [like(BLK, 2048)] * 2 + [like(1, 256)],
        compiler_params=params(),
        cost_estimate=cost(),
        name="prepare",
    )(low_index, *in_hbm(residual, gradient, w_qkv, w_out, w_up, w_down, *vectors))


def norm_and_project(core_index, mine, other, gain, shift, weights):
    def kernel(core_ref, mine_ref, other_ref, gain_ref, shift_ref, weight_ref, standard_ref, normed_ref, proj_ref):
        rows = (mine_ref[...], other_ref[...])
        first = core_ref[0] == 0
        value = jnp.concatenate([jnp.where(first, *rows), jnp.where(first, *rows[::-1])]).astype(F32)
        value = value - jnp.mean(value, axis=1, keepdims=True)
        value = value * lax.rsqrt(jnp.mean(value * value, axis=1, keepdims=True) + EPS)
        standard_ref[...] = value.astype(BF)
        normed = (value * gain_ref[...] + shift_ref[...]).astype(BF)
        normed_ref[...] = normed
        proj_ref[...] = jnp.dot(normed, weight_ref[...].reshape(D, 768), preferred_element_type=F32)

    def by_row(rows, width):
        return pl.BlockSpec((rows, width), lambda i: (i, 0))

    def fixed(*shape):
        return pl.BlockSpec(shape, lambda i: (0,) * len(shape), pipeline_mode=pl.Buffered(1))

    return pl.pallas_call(
        kernel,
        grid=(4,),
        in_specs=[SMEM, by_row(TOK, D), by_row(TOK, D), fixed(1, D), fixed(1, D), fixed(16, 128, 768)],
        out_specs=[by_row(256, D), by_row(256, D), by_row(256, 768)],
        out_shape=[like(1024, D), like(1024, D), like(1024, 768, F32)],
        compiler_params=params(),
        cost_estimate=cost(),
        name="norm_and_project",
    )(core_index, *in_hbm(mine, other, gain, shift, weights))


GELU_A = 0.7978845608028654
GELU_B = 0.044715


def hidden_units(places, normed, weights, shift, plan, pieces):
    width = 256
    steps = 1024 // width

    def kernel(places_ref, left, weight, shift_ref, *refs):
        inputs, (hidden_ref, slope_ref, whole_ref, stage, sems) = refs[: len(pieces)], refs[len(pieces) :]
        moves = []
        for i, (source, row, rows, _, _, _, to, place, unit, _) in enumerate(plan):
            at = pl.ds(pl.multiple_of(to + places_ref[place] * unit, rows), rows)
            moves.append(
                (
                    pltpu.make_async_copy(inputs[source].at[pl.ds(row, rows)], stage.at[at], sems.at[0, i]),
                    pltpu.make_async_copy(stage.at[at], whole_ref.at[at], sems.at[1, i]),
                )
            )

        @pl.when(pl.program_id(0) == 0)
        def _():
            for arrive, _ in moves:
                arrive.start()

        u = jnp.dot(left[...], weight[...], preferred_element_type=F32) + shift_ref[...]
        square = u * u
        t = jnp.tanh(GELU_A * u * (1.0 + GELU_B * square))
        half = 0.5 * (1.0 + t)
        hidden_ref[...] = (u * half).astype(BF)
        slope = half + 0.5 * u * (1.0 - t * t) * GELU_A * (1.0 + 3.0 * GELU_B * square)
        slope_ref[...] = slope.astype(BF)

        @pl.when(pl.program_id(0) == 1)
        def _():
            for arrive, leave in moves:
                arrive.wait()
                leave.start()

        @pl.when(pl.program_id(0) == steps - 1)
        def _():
            for _, leave in moves:
                leave.wait()

    column = pl.BlockSpec((1024, width), lambda i: (0, i))
    return pl.pallas_call(
        kernel,
        grid=(steps,),
        in_specs=[SMEM, VMEM, pl.BlockSpec((D, width), lambda i: (0, i)), pl.BlockSpec((1, width), lambda i: (0, i))]
        + [ANY] * len(pieces),
        out_specs=[column, column, ANY],
        out_shape=[like(1024, 1024), like(1024, 1024), like(D, 1024)],
        scratch_shapes=[pltpu.VMEM((D, 1024), BF), pltpu.SemaphoreType.DMA((2, len(plan)))],
        compiler_params=params(),
        cost_estimate=cost(),
        name="hidden_units",
    )(places, in_vmem(normed), *in_hbm(weights, shift, *pieces))


def hidden_back_kernel(left, weight, slope_ref, d_ref, sum_ref):
    value = jnp.dot(left[...], weight[...], preferred_element_type=F32) * slope_ref[...].astype(F32)
    value = value.astype(BF)
    d_ref[...] = value
    sum_ref[...] = jnp.sum(value.astype(F32), axis=0, keepdims=True)


def hidden_back_and_apart(places, gradients, weights, slope, lefts, others):
    width = 256
    kernel_apart, in_specs, out_specs, out_shape, scratch = apart_parts(lefts, others)
    count = len(in_specs)

    def kernel(places_ref, left, weight, slope_ref, *refs):
        given, (d_ref, sum_ref, *made) = refs[:count], refs[count:]
        hidden_back_kernel(left, weight, slope_ref, d_ref, sum_ref)
        kernel_apart(places_ref, *given, *made)

    column = pl.BlockSpec((1024, width), lambda i: (0, i))
    return pl.pallas_call(
        kernel,
        grid=(4,),
        in_specs=[SMEM, VMEM, pl.BlockSpec((D, width), lambda i: (0, i)), column] + in_specs,
        out_specs=[column, pl.BlockSpec((1, width), lambda i: (0, i))] + out_specs,
        out_shape=[like(1024, 1024), like(1, 1024, F32)] + out_shape,
        scratch_shapes=scratch,
        compiler_params=params(32 * 1024 * 1024),
        cost_estimate=cost(),
        name="hidden_back_and_apart",
    )(places, in_vmem(gradients), *in_hbm(weights, slope, *lefts, *(weight for weight, _ in others)))


def apart_parts(lefts, weights, standard=None):
    count = len(lefts)

    def kernel(places_ref, *refs):
        value_ref = refs[-1]
        value = sum(
            lax.dot_general(
                left[...],
                weight[...].reshape(-1, weight.shape[2]),
                (((1,), (1,)), ((), ())),
                preferred_element_type=F32,
            )
            for left, weight in zip(refs[:count], refs[count : 2 * count])
        )
        refs = refs[2 * count : -1]
        if standard is not None:
            standard_ref, refs = refs[0], refs[1:]
            refs[2][0:1, :] = jnp.sum(value * standard_ref[...].astype(F32), axis=0, keepdims=True)
            refs[2][1:2, :] = jnp.sum(value, axis=0, keepdims=True)
        value_ref[...] = value
        for h in range(2):
            for k in range(4):
                rows = pl.ds(pl.multiple_of(places_ref[4 * h + k] * TOK, TOK), TOK)
                refs[h][k * TOK : (k + 1) * TOK, :] = value_ref[rows, :].astype(BF)

    width = 512
    extra = standard is not None
    in_specs = [pl.BlockSpec(left.shape, lambda i: (0, 0), pipeline_mode=pl.Buffered(1)) for left in lefts]
    in_specs += [
        pl.BlockSpec((4, 128, left.shape[1]), lambda i, at=at: (i, 0, at)) for left, (_, at) in zip(lefts, weights)
    ]
    in_specs += [pl.BlockSpec((1024, width), lambda i: (0, i))] * extra
    out_specs = [pl.BlockSpec((512, width), lambda i: (0, i))] * 2 + [pl.BlockSpec((2, width), lambda i: (0, i))] * extra
    out_shape = [like(512, D)] * 2 + [like(2, D, F32)] * extra
    return kernel, in_specs, out_specs, out_shape, [pltpu.VMEM((1024, width), F32)]


def apart(places, lefts, weights, standard):
    kernel, in_specs, out_specs, out_shape, scratch = apart_parts(lefts, weights, standard)
    return pl.pallas_call(
        kernel,
        grid=(4,),
        in_specs=[SMEM] + in_specs,
        out_specs=out_specs,
        out_shape=out_shape,
        scratch_shapes=scratch,
        compiler_params=params(),
        cost_estimate=cost(),
        name="apart",
    )(places, *in_hbm(*lefts, *(weight for weight, _ in weights), standard))


def token_sum1(near, got):
    def kernel(places_ref, near_ref, got_ref, send_ref):
        send_ref[...] = (near_ref[...].astype(F32) + got_ref[...].astype(F32)).astype(BF)

    return kernel, [(near, 256, 1), (Arrived(got), 256, 1)], [(256, D, BF)], ()


def token_sum2(near, got, back):
    def kernel(places_ref, near_ref, got_ref, back_ref, send_ref):
        value = near_ref[...].astype(F32) + got_ref[...].astype(F32) + back_ref[...].astype(F32)
        send_ref[...] = value.astype(BF)

    return kernel, [(near, TOK, 1), (Arrived(got), TOK, 1), (Arrived(back), TOK, 1)], [(TOK, D, BF)], ()


ROWS = pl.BlockSpec((TOK // 4, D), lambda i: (i, 0))
ONE_ROW = pl.BlockSpec((1, D), lambda i: (0, 0))


def finish_output(near, got, back, last, residual, shift):
    def kernel(near_ref, got_ref, back_ref, last_ref, residual_ref, shift_ref, out_ref):
        value = sum(ref[...].astype(F32) for ref in (near_ref, got_ref, back_ref, last_ref))
        value = residual_ref[...].astype(F32) + value + shift_ref[...]
        out_ref[...] = outside(value.astype(BF))

    return pl.pallas_call(
        kernel,
        grid=(4,),
        in_specs=[ROWS] * 5 + [ONE_ROW],
        out_specs=ROWS,
        out_shape=like(TOK, D),
        compiler_params=params(),
        cost_estimate=cost(),
        name="finish_output",
    )(*in_hbm(near, Arrived(got), Arrived(back), Arrived(last), residual, shift))


def finish_grad(near, got, back, last, residual, gradient, gain):
    def kernel(near_ref, got_ref, back_ref, last_ref, residual_ref, gradient_ref, gain_ref, out_ref):
        value = sum(ref[...].astype(F32) for ref in (near_ref, got_ref, back_ref, last_ref))
        value = value * gain_ref[...]
        rows = residual_ref[...].astype(F32)
        rows = rows - jnp.mean(rows, axis=1, keepdims=True)
        inverse = lax.rsqrt(jnp.mean(rows * rows, axis=1, keepdims=True) + EPS)
        rows = rows * inverse
        plain = jnp.mean(value, axis=1, keepdims=True)
        cross = jnp.mean(value * rows, axis=1, keepdims=True)
        out_ref[...] = outside(gradient_ref[...].astype(F32) + inverse * (value - plain - rows * cross))

    return pl.pallas_call(
        kernel,
        grid=(4,),
        in_specs=[ROWS] * 6 + [ONE_ROW],
        out_specs=ROWS,
        out_shape=like(TOK, D, F32),
        compiler_params=params(),
        cost_estimate=cost(),
        name="finish_grad",
    )(*in_hbm(near, Arrived(got), Arrived(back), Arrived(last), residual, gradient, gain))


def doc_positions(segments):
    length = segments.shape[0]
    places = jnp.arange(length, dtype=jnp.int32)
    boundary = jnp.concatenate([jnp.ones((1,), dtype=jnp.bool_), segments[1:] != segments[:-1]])
    doc_start = lax.cummax(jnp.where(boundary, places, jnp.zeros_like(places)), axis=0)
    return places - doc_start


def rotary_tables(positions):
    lane = jnp.arange(128, dtype=jnp.int32) % HD
    half_rot = ROT // 2
    frequency = 10000.0 ** (-(2.0 * (lane % half_rot).astype(F32)) / ROT)
    angles = positions.astype(F32)[:, None] * jnp.where(lane < ROT, frequency, 0.0)
    sine = jnp.sin(angles)
    before = jnp.where(lane < half_rot, -sine, 0.0)
    after = jnp.where((lane >= half_rot) & (lane < ROT), sine, 0.0)
    return jnp.concatenate([jnp.cos(angles), before, after], axis=1)


def attention_kernel(
    proj_ref, shift_ref, table_ref, column_ref, row_ref, grad_ref, weight_ref, mixed_ref, d_proj_ref, sums_ref, mask_ref
):
    start, last = column_ref[:, 0:1], column_ref[:, 1:2]
    where = row_ref[0]
    mask_ref[...] = jnp.where((where >= start) & (where <= last), 0.0, MASKED)
    cosine, before, after = (table_ref[:, i * 128 : (i + 1) * 128] for i in range(3))
    lane = lax.broadcasted_iota(jnp.int32, (SEQ, 128), 1)

    def turn(value, sign):
        shifted = pltpu.roll(value, 112, 1) * before + pltpu.roll(value, 16, 1) * after
        return value * cosine + sign * shifted

    def part(index, pair):
        at = slice(index * 256 + pair * 128, index * 256 + pair * 128 + 128)
        return proj_ref[:, at] + shift_ref[:, at]

    def dot(a, b, dims):
        return lax.dot_general(a, b, (dims, ((), ())), preferred_element_type=F32)

    d_attended = jnp.dot(grad_ref[...], weight_ref[...].reshape(D, 256), preferred_element_type=F32).astype(BF)
    for pair in range(2):
        at = slice(pair * 128, pair * 128 + 128)
        queries = (turn(part(0, pair), 1.0).astype(BF).astype(F32) * HD**-0.5).astype(BF)
        keys = turn(part(1, pair), 1.0).astype(BF)
        values = part(2, pair).astype(BF)
        d_out = d_attended[:, at]
        results = []
        for head in range(2):
            own = (lane >= head * HD) & (lane < (head + 1) * HD)
            own_queries = jnp.where(own, queries, jnp.zeros_like(queries))
            own_d_out = jnp.where(own, d_out, jnp.zeros_like(d_out))
            scores = dot(own_queries, keys, ((1,), (1,))) + mask_ref[...]
            exponent = jnp.exp(scores - jnp.max(scores, axis=1, keepdims=True))
            soft = exponent * (1.0 / jnp.sum(exponent, axis=1, keepdims=True))
            soft_low = soft.astype(BF)
            mixed = dot(soft_low, values, ((1,), (0,)))
            d_soft = dot(own_d_out, values, ((1,), (1,)))
            inner = jnp.sum(soft * d_soft, axis=1, keepdims=True)
            d_scores = (soft * (d_soft - inner)).astype(BF)
            d_queries = dot(d_scores, keys, ((1,), (0,))) * HD**-0.5
            d_keys = dot(d_scores, own_queries, ((0,), (0,)))
            d_values = dot(soft_low, own_d_out, ((0,), (0,)))
            results.append((mixed, d_queries, d_keys, d_values))
        first, second = results
        mixed_ref[:, at] = jnp.where(lane < HD, first[0], second[0]).astype(BF)
        d_queries = turn(jnp.where(lane < HD, first[1], second[1]), -1.0).astype(BF)
        d_keys = turn(first[2] + second[2], -1.0).astype(BF)
        d_values = (first[3] + second[3]).astype(BF)
        for index, value in enumerate((d_queries, d_keys, d_values)):
            at = slice(index * 256 + pair * 128, index * 256 + pair * 128 + 128)
            d_proj_ref[:, at] = value
            sums_ref[0, :, at] = jnp.sum(value.astype(F32), axis=0, keepdims=True)


def attention(projected, shift, tables, columns, rows, gradients, weights):
    count = projected.shape[0] // SEQ
    return pl.pallas_call(
        attention_kernel,
        grid=(count,),
        in_specs=[
            pl.BlockSpec((SEQ, 768), lambda i: (i, 0)),
            pl.BlockSpec((1, 768), lambda i: (0, 0)),
            pl.BlockSpec((SEQ, 384), lambda i: (i, 0)),
            pl.BlockSpec((SEQ, 2), lambda i: (i, 0)),
            pl.BlockSpec((1, 1, SEQ), lambda i: (i, 0, 0)),
            pl.BlockSpec((SEQ, D), lambda i: (i, 0)),
            pl.BlockSpec((16, 128, 256), lambda i: (0, 0, 3), pipeline_mode=pl.Buffered(1)),
        ],
        out_specs=[
            pl.BlockSpec((SEQ, 256), lambda i: (i, 0)),
            pl.BlockSpec((SEQ, 768), lambda i: (i, 0)),
            pl.BlockSpec((1, 1, 768), lambda i: (i, 0, 0)),
        ],
        out_shape=[
            pltpu.HBM((count * SEQ, 256), BF),
            pltpu.HBM((count * SEQ, 768), BF),
            pltpu.HBM((count, 1, 768), F32),
        ],
        scratch_shapes=[pltpu.VMEM((SEQ, SEQ), F32)],
        compiler_params=pltpu.CompilerParams(vmem_limit_bytes=VMEM_LIMIT),
        cost_estimate=cost(),
        name="attention",
    )(*in_hbm(projected, shift, tables, columns, rows, gradients, weights))


def body(
    residual_in,
    segment_ids,
    out_grad,
    ln_gain,
    ln_bias,
    w_qkv,
    b_qkv,
    w_out,
    b_attn_out,
    w_up,
    b_up,
    w_down,
    b_mlp_out,
):
    y_lo, x, z, y_hi, core = (lax.axis_index(name).astype(jnp.int32) for name in AXES)
    low_index = y_lo[None]
    low = y_lo == 0

    def around(c):
        return [c, c ^ (1 + 2 * core), c ^ (3 - 2 * core), c ^ 2]

    y_places = [
        y_lo * 2 + y_hi,
        (1 - y_lo) * 2 + (y_hi ^ core),
        (1 - y_lo) * 2 + (y_hi ^ (1 - core)),
        y_lo * 2 + (1 - y_hi),
    ]
    ring_places = jnp.stack(
        around(x)
        + around(z)
        + [y_lo, 1 - y_lo]
        + y_places
        + [2 * k + core for k in range(4)]
        + [2 * k + 1 - core for k in range(4)]
    )
    part_places = jnp.stack(
        [2 * p + core for p in y_places] + [2 * y_places[k] + 1 - core for k in (0, 2, 1, 3)]
    )

    vectors = [value.reshape(1, -1) for value in (ln_gain, ln_bias, b_attn_out, b_mlp_out, b_up)]
    vectors += [b_qkv[i] for i in range(3)]
    residual, gradient, attn_own, attn_away, rest_own, rest_away, small = prepare(
        low_index, residual_in, out_grad, w_qkv.transpose(1, 0, 2), w_out.T, w_up, w_down.T, vectors
    )

    def widen(rows, axis, index):
        got = flip(rows, axis)
        return jnp.where(index == 0, jnp.concatenate([rows, got]), jnp.concatenate([got, rows]))

    attn_got = flip(attn_away, "y_lo")
    small = widen(small, "core", core)
    small = widen(small, "y_hi", y_hi)
    attn_got, small, residual, gradient, rest_away = bar((attn_got, small, residual, gradient, rest_away))
    small = jnp.pad(small.reshape(1, 1024), ((0, 15), (0, 0)))

    def token_positions():
        far_segments = flip(segment_ids, "y_lo")
        places = jnp.arange(SEQ, dtype=jnp.int32)
        positions = jnp.concatenate(
            [doc_positions(jnp.where(low, a, b)) for a, b in ((segment_ids, far_segments), (far_segments, segment_ids))]
        )
        places = jnp.concatenate([places, places])
        columns = places[:, None] - jnp.where(jnp.arange(2)[None] == 0, positions[:, None], 0)
        return columns, places.reshape(2, 1, SEQ), rotary_tables(positions)

    def joined(own, first):
        plan = [(source, 0, TOK, 0, D, 0, TOK * source, None, 0, 0) for source in range(2)]
        return plan, [(2 * TOK, D)], [own, Arrived(first)], False

    def of_core(own, first, second):
        plan = [
            (source, row, TOK, 0, D, 0, 0, 10 + k, TOK, 0)
            for k, (source, row) in enumerate(((0, 0), (1, 0), (2, 0), (2, TOK)))
        ]
        return plan, [(SEQ, D)], [own, Arrived(first), Arrived(second)], False

    def of_both(mine, other, stay=False):
        plan = [
            (source, k * TOK, TOK, 0, D, 0, 0, 14 + 4 * source + k, TOK, 0) for source in range(2) for k in range(4)
        ]
        return plan, [(1024, D)], [mine, Arrived(other)], stay

    plan = [(source, 0, BLK, 0, 1024, 0, 0, 8 + source, BLK, 0) for source in range(2)]
    plan.append((2, 0, 16, 0, 1024, 0, 128, None, 0, 0))
    ((shard,),) = copies(ring_places, (plan, [(144, 1024)], [attn_own, Arrived(attn_got), small], False))
    attn_all = lax.all_gather(shard, ("x", "z"), axis=0)
    token_first = swap_y(residual, 0)
    rest_got = flip(rest_away, "y_lo")
    shard, token_first, rest_got, gradient = bar((shard, token_first, rest_got, gradient))
    plan = [
        (source, 0, BLK, 1024 * h, 1024, h, 0, 8 + source, BLK, 0) for source in range(2) for h in range(2)
    ]
    (tokens_sent,), sends = copies(
        ring_places, joined(residual, token_first), (plan, [(128, 1024)] * 2, [rest_own, Arrived(rest_got)], False)
    )
    rest_gather = Gather(*sends)
    tokens_sent, sends, gradient = bar((tokens_sent, sends, gradient))
    token_second = swap_y(tokens_sent, 1)
    grad_first = swap_y(gradient, 0)
    got = gather_step(1, sends)
    token_second, grad_first, got = bar((token_second, grad_first, got))
    (mine,), (grads_sent,), sends = copies(
        ring_places,
        of_core(residual, token_first, token_second),
        joined(gradient, grad_first),
        rest_gather.sending(got),
    )
    mine, grads_sent, sends = bar((mine, grads_sent, sends))
    other = flip(mine, "core")
    grad_second = swap_y(grads_sent, 1)
    positions = token_positions()
    got, other, mine, grad_second, positions, table = bar(
        (gather_step(2, sends), other, mine, grad_second, positions, attn_all[:, 128, :][None])
    )
    tokens = (mine, other)
    other_table = flip(table, "y_lo")
    rest_gather.pair, (mine,) = copies(
        ring_places, rest_gather.joining(got, False), of_core(gradient, grad_first, grad_second)
    )
    sends, mine, table, other_table = bar((rest_gather.pair, mine, table, other_table))
    other = flip(mine, "core")
    got = gather_step(3, sends)
    columns, rows, tables = positions

    table = jnp.where(low, jnp.concatenate([table, other_table]), jnp.concatenate([other_table, table]))
    table = table.reshape(2, 16, 4, 256).astype(F32)
    vectors = table[..., :64].reshape(2, 16, 4, 4, 16).transpose(3, 1, 0, 2, 4).reshape(4, D)
    gain, shift, out_shift = vectors[0:1], vectors[1:2], vectors[2:3] + vectors[3:4]
    shifts = lax.dynamic_index_in_dim(table.reshape(2, 16, 4, 256), y_hi * 2 + core, 2, False)
    shifts = lax.dynamic_index_in_dim(shifts, y_lo, 0, False)
    up_shift = shifts[:, 64:128].reshape(1, 1024)
    qkv_shift = shifts[:, 128:176].reshape(16, 3, 16).transpose(1, 0, 2).reshape(1, 768)

    standard, normed, projected = norm_and_project(core[None], *tokens, gain, shift, attn_all)
    got, other, mine, normed, projected = bar((got, other, mine, normed, projected))
    (sends,) = copies(ring_places, rest_gather.sending(got))
    sends, mine, other, projected = bar((sends, mine, other, projected))
    rest_got = gather_step(4, sends)
    ((grad_all,),) = copies(ring_places, of_both(mine, other))
    mixed, d_projected, shift_sums = attention(projected, qkv_shift, tables, columns, rows, grad_all, attn_all)
    attn_sum = attention_gradient(normed, d_projected, grad_all, mixed)
    attn_sum, rest_got, normed = bar((attn_sum, rest_got, normed))
    attn_sum = lax.psum_scatter(attn_sum, ("x", "z"), scatter_dimension=0, tiled=True)

    ((up_all,),) = copies(ring_places, rest_gather.joining(rest_got, True))
    hidden, slope, down_all = hidden_units(ring_places, normed, up_all, up_shift, *rest_gather.right())
    down_sum = Scatter(ring_places, 0, grad_all, hidden)
    sends, mixed, hidden, slope, grad_all = bar((down_sum.first, mixed, hidden, slope, grad_all))
    down_got = scatter_step(1, sends)
    d_hidden, up_shift_part, near, away = hidden_back_and_apart(
        part_places, grad_all, down_all, slope, [mixed, hidden], [(attn_all, 3), (down_all.reshape(16, 128, 1024), 0)]
    )
    near, away, d_hidden, down_got = bar((near, away, d_hidden, down_got))
    out_got = flip(away, "core")
    up_sum = Scatter(ring_places, 1, normed, d_hidden)
    up_sends, out_got = bar((up_sum.first, out_got))
    ((out_send,),) = add(ring_places, token_sum1(near, out_got))

    up_sends, out_send, d_hidden = bar((up_sends, out_send, d_hidden))
    up_got = scatter_step(1, up_sends)
    out_back = swap_y(out_send, 1)
    d_near, d_away, vector_parts = apart(
        part_places,
        [d_projected, d_hidden],
        [(attn_all, 0), (up_all.reshape(16, 128, 1024), 0)],
        standard,
    )
    d_away, up_got, out_back, down_got, vector_parts = bar((d_away, up_got, out_back, down_got, vector_parts))
    sums = (down_sum, up_sum)
    sends, (out_send,) = add(
        ring_places,
        together(down_sum.send2(down_got), up_sum.send2(up_got)),
        token_sum2(near, out_got, out_back),
    )
    sends, out_send, d_away, vector_parts = bar((sends, out_send, d_away, vector_parts))
    d_got = flip(d_away, "core")
    got = scatter_step(2, sends)
    out_last = swap_y(out_send, 0)
    out_shift_part = jnp.sum(gradient.astype(F32), axis=0, keepdims=True)
    parts = jnp.concatenate([vector_parts, out_shift_part]).reshape(3, 16, 8, 16)
    parts = parts.transpose(1, 2, 0, 3).reshape(16, 384)
    shift_sums = jnp.sum(shift_sums, axis=(0, 1))
    line = jnp.concatenate(
        [
            parts,
            up_shift_part.reshape(16, 64),
            shift_sums.reshape(3, 16, 16).transpose(1, 0, 2).reshape(16, 48),
            jnp.zeros((16, 16), F32),
        ],
        axis=1,
    )
    offsets = [0]
    for _, _, bits in RING_STEPS:
        offsets = offsets + [o ^ bits for o in offsets]
    here = (4 * x + z) ^ jnp.array(offsets, jnp.int32)
    order = (here[:, None] == jnp.arange(16, dtype=jnp.int32)[None, :]).astype(F32)
    line = jnp.dot(order, line, precision=lax.Precision.HIGHEST)

    def fold(line, step):
        axis, mask, _ = RING_STEPS[step]
        count = line.shape[0] // 2
        return line[:count] + flip4(line[count:], axis, mask)

    def narrow(part, axis, index):
        part = part.reshape(2, -1)
        return jnp.where(index == 0, part[0], part[1]) + flip(jnp.where(index == 0, part[1], part[0]), axis)

    line = fold(fold(line, 3), 2)
    d_got, got, out_last, line = bar((d_got, got, out_last, line))
    sends, (d_send,) = add(
        ring_places, together(*(each.send3(got) for each in sums)), token_sum1(d_near, d_got)
    )
    down_sum.keep, up_sum.keep = sends[2:4], sends[4:]
    sends, d_send, line = bar((sends[:2], d_send, line))
    d_back = swap_y(d_send, 1)
    got = scatter_step(3, sends)
    line = fold(fold(line, 1), 0)[0]
    part = narrow(line[:384], "y_lo", y_lo)
    output = finish_output(near, out_got, out_back, out_last, residual, out_shift)
    lower, upper = attn_sum[:BLK], attn_sum[BLK:]
    attn_own, attn_away = jnp.where(low, lower, upper), jnp.where(low, upper, lower)
    attn_far = flip(attn_away, "y_lo")
    d_back, got, part, output, attn_far = bar((d_back, got, part, output, attn_far))
    sends, (d_send,) = add(
        ring_places, together(*(each.send4(got) for each in sums)), token_sum2(d_near, d_got, d_back)
    )
    sends, d_send, part = bar((sends, d_send, part))
    d_last = swap_y(d_send, 0)
    got = scatter_step(4, sends)
    part = narrow(part, "y_hi", y_hi)
    d_last, got, part = bar((d_last, got, part))
    ((own, away),) = add(ring_places, together(*(each.finish(got) for each in sums)), steps=1)
    away, part, d_last = bar((away, part, d_last))
    far = flip(away, "y_lo")
    part = narrow(part, "core", core)
    grad_in = finish_grad(d_near, d_got, d_back, d_last, residual, gradient, gain)
    far, part, grad_in = bar((far, part, grad_in))
    sum_down, sum_up, sum_qkv, sum_out = whole(
        low_index, (own, far, ((1024, 1), (1024, 1))), (attn_own, attn_far, ((256, 3), (256, 1)))
    )
    grad_gain, grad_shift, grad_out_shift = part[:16], part[16:32], part[32:]
    return (
        output,
        grad_in,
        grad_gain,
        grad_shift,
        sum_qkv.transpose(1, 0, 2),
        line[448:496].reshape(3, 1, 16),
        sum_out[0].T,
        grad_out_shift,
        sum_up[0],
        line[384:448].reshape(1, 64),
        sum_down[0].T,
        grad_out_shift,
    )


def solution(mesh):
    fine = Mesh(mesh.devices.reshape(2, 4, 4, 2, 2), AXES)
    dp = ("y_lo", "x", "z")
    tensor = ("y_hi", "core")
    every = AXES
    in_specs = (
        P(every, None),
        P(dp),
        P(every, None),
        P(every),
        P(every),
        P(dp, None, tensor),
        P(None, tensor, dp),
        P(tensor, dp),
        P(every),
        P(dp, tensor),
        P(tensor, dp),
        P(tensor, dp),
        P(every),
    )
    out_specs = (
        P(every, None),
        P(every, None),
        P(every),
        P(every),
        P(dp, None, tensor),
        P(None, tensor, dp),
        P(tensor, dp),
        P(every),
        P(dp, tensor),
        P(tensor, dp),
        P(tensor, dp),
        P(every),
    )
    return jax.shard_map(body, mesh=fine, in_specs=in_specs, out_specs=out_specs, check_vma=False)
```

```python
import jax
import jax.numpy as jnp
from jax import lax
from jax.experimental import pallas as pl
from jax.experimental.pallas import tpu as pltpu
from jax.sharding import Mesh, PartitionSpec as P

HD = 64
ROT = 32
EPS = 1e-05
MASKED = -1e30
D = 2048
SEQ = 512
TOK = 128
BLK = 64
VMEM_LIMIT = 24 * 1024 * 1024
BF = jnp.bfloat16
F32 = jnp.float32
AXES = ("y_lo", "x", "z", "y_hi", "core")


bar = lax.optimization_barrier


def params(limit=VMEM_LIMIT):
    return pltpu.CompilerParams(vmem_limit_bytes=limit)


def cost():
    return pl.CostEstimate(flops=1000, bytes_accessed=1000, transcendentals=0)


def like(rows, columns, kind=BF):
    return pltpu.HBM((rows, columns), kind)


class Arrived:
    def __init__(self, value):
        self.value, self.shape = value, value.shape


def in_hbm(*values):
    return tuple(
        value.value if isinstance(value, Arrived) else pltpu.with_memory_space_constraint(value, pltpu.HBM)
        for value in values
    )


def in_vmem(value):
    return pltpu.with_memory_space_constraint(value, pltpu.VMEM)


SMEM = pl.BlockSpec(memory_space=pltpu.SMEM)
VMEM = pl.BlockSpec(memory_space=pltpu.VMEM)
ANY = pl.BlockSpec(memory_space=pl.ANY)


def ring(value, axis, step):
    masks = (1, 3) if step == 0 else (3, 1)
    table = [(i * 2 + c, (i ^ masks[c]) * 2 + c) for i in range(4) for c in range(2)]
    return lax.ppermute(value, (axis, "core"), table)


def ring_pair(pair, axes, step):
    pair = bar(tuple(pair))
    return bar(tuple(ring(value, axis, step) for value, axis in zip(pair, axes)))


def swap_y(value, step):
    masks = (1, 3) if step == 0 else (3, 1)

    def place(y, c):
        return ((y % 2) * 2 + y // 2) * 2 + c

    table = [(place(y, c), place(y ^ masks[c], c)) for y in range(4) for c in range(2)]
    return lax.ppermute(value, ("y_lo", "y_hi", "core"), table)


def flip(value, axis):
    return lax.ppermute(value, axis, [(0, 1), (1, 0)])


def copies(places, *jobs):
    sources = [source for _, _, given, _ in jobs for source in given]
    shapes = [(shape, stay) for _, made, _, stay in jobs for shape in made]
    plans, low, made = [], 0, 0
    for plan, results, given, stay in jobs:
        for source, row, rows, column, columns, target, to, place, unit, across in plan:
            plans.append((source + low, row, rows, column, columns, target + made, to, place, unit, across, stay))
        low += len(given)
        made += len(results)

    def kernel(places_ref, *refs):
        inputs, refs = refs[: len(sources)], refs[len(sources) :]
        outputs, spare, sems = refs[: len(shapes)], list(refs[len(shapes) : -1]), refs[-1]
        stages = [output if stay else spare.pop(0) for output, (_, stay) in zip(outputs, shapes)]
        moves = []
        for i, (source, row, rows, column, columns, target, to, place, unit, across, stay) in enumerate(plans):
            if place is not None:
                to = pl.multiple_of(to + places_ref[place] * unit, rows)
            at = (pl.ds(to, rows), pl.ds(across, columns))
            stage = stages[target].at[at]
            arrive = pltpu.make_async_copy(
                inputs[source].at[pl.ds(row, rows), pl.ds(column, columns)], stage, sems.at[0, i]
            )
            arrive.start()
            leave = None if stay else pltpu.make_async_copy(stage, outputs[target].at[at], sems.at[1, i])
            moves.append((arrive, leave))
        for arrive, leave in moves:
            arrive.wait()
            if leave is not None:
                leave.start()
        for _, leave in moves:
            if leave is not None:
                leave.wait()

    outs = pl.pallas_call(
        kernel,
        in_specs=[SMEM] + [ANY] * len(sources),
        out_specs=[VMEM if stay else ANY for _, stay in shapes],
        out_shape=[pltpu.VMEM(shape, BF) if stay else like(*shape) for shape, stay in shapes],
        scratch_shapes=[pltpu.VMEM(shape, BF) for shape, stay in shapes if not stay]
        + [pltpu.SemaphoreType.DMA((2, len(plans)))],
        compiler_params=params(),
        cost_estimate=cost(),
        name="put_together",
    )(places, *in_hbm(*sources))
    results = []
    for _, made, _, _ in jobs:
        results.append(outs[: len(made)])
        outs = outs[len(made) :]
    return results


def flip4(value, axis, mask):
    return lax.ppermute(value, axis, [(i, i ^ mask) for i in range(4)])


RING_STEPS = (("z", 1, 1), ("z", 3, 3), ("x", 1, 4), ("x", 3, 12))


class Gather:
    def __init__(self, left, right):
        self.pair = (left, right)

    def sending(self, got):
        self.first = got
        rows, width = self.pair[0].shape
        plan = [(2 * h + k, 0, rows, 0, width, h, k * rows, None, 0, 0) for h in range(2) for k in range(2)]
        sources = [value for own, first in zip(self.pair, got) for value in (own, Arrived(first))]
        return plan, [(2 * rows, width)] * 2, sources, False

    def joining(self, got, last):
        self.last = tuple(Arrived(value) for value in got)
        rows, width = self.pair[0].shape
        sources = [value for each in zip(self.pair, self.first, self.last) for value in each]
        if last:
            return self.ordered(0), [(2048, width)], sources[:3], False
        plan = []
        for h in range(2):
            for k, (source, row) in enumerate(((0, 0), (1, 0), (2, 0), (2, rows))):
                plan.append((source + 3 * h, row, rows, 0, width, h, 0, 4 * h + k, rows, 0))
        return plan, [(4 * rows, width)] * 2, sources, False

    def ordered(self, h):
        rows, width = self.pair[0].shape
        plan = []
        for k, (source, row) in enumerate(((0, 0), (1, 0), (2, 0), (2, rows))):
            for i in range(4):
                to, unit = ((i * 512, 128), (i * 128, 512))[h]
                plan.append((source, row + i * 128, 128, 0, width, 0, to, 4 * (1 - h) + k, unit, 0))
        return plan

    def right(self):
        return self.ordered(1), (self.pair[1], self.first[1], self.last[1])


def gather_step(step, pair):
    return ring_pair(pair, ("x", "z") if step < 3 else ("z", "x"), 1 - step % 2)


def scatter_step(step, pair):
    return ring_pair(pair, ("x", "z") if step < 3 else ("z", "x"), step % 2)


class Scatter:
    def __init__(self, places, index, left, right):
        self.places, self.index = places, index
        tokens, width = right.shape
        self.width = half = width // 2

        def kernel(places_ref, left_ref, right_ref, *refs):
            outs, (rights, *stages), sems = refs[:6], refs[6:-1], refs[-1]
            fetch = [
                pltpu.make_async_copy(right_ref.at[:, pl.ds(h * half, half)], rights.at[h], sems.at[h]) for h in range(2)
            ]
            for copy in fetch:
                copy.start()
            order = [2, 3, 1, 0]
            stored = []
            for h in range(2):
                fetch[h].wait()
                for i, k in enumerate(order):
                    if h == 0:
                        block = left_ref[:, pl.ds(pl.multiple_of(places_ref[k] * 512, 512), 512)]
                    else:
                        z = places_ref[4 + k]
                        block = jnp.concatenate(
                            [left_ref[:, pl.ds(pl.multiple_of(n * 512 + z * 128, 128), 128)] for n in range(4)], axis=1
                        )
                    value = lax.dot_general(
                        block,
                        rights[h],
                        (((0,), (0,)), ((), ())),
                        preferred_element_type=F32,
                    ).astype(BF)
                    stage = stages[h].at[pl.ds(i * 512, 512)]
                    stage[...] = value
                    out = outs[h].at[pl.ds(i * 512, 512)] if i < 2 else outs[2 * i - 2 + h]
                    copy = pltpu.make_async_copy(stage, out, sems.at[2 + 4 * h + i])
                    copy.start()
                    stored.append(copy)
            for copy in stored:
                copy.wait()

        outs = pl.pallas_call(
            kernel,
            in_specs=[SMEM, VMEM, ANY],
            out_specs=[ANY] * 6,
            out_shape=[like(1024, half)] * 2 + [like(512, half)] * 4,
            scratch_shapes=[
                pltpu.VMEM((2, tokens, half), BF),
                pltpu.VMEM((2048, half), BF),
                pltpu.VMEM((2048, half), BF),
                pltpu.SemaphoreType.DMA((10,)),
            ],
            compiler_params=params(),
            cost_estimate=cost(),
            name="gradient",
        )(places, in_vmem(left), *in_hbm(right))
        self.first, self.next, self.keep = outs[:2], outs[2:4], outs[4:]

    def part(self, got, rows, at, new=True):
        half = self.width // 2
        alone = got[0].shape[1] == self.width
        return [
            (Arrived(value) if new else value, rows, at, half, (lambda i: i) if alone else (lambda i: 2 * i + self.index)) for value in got
        ]

    def send2(self, got):
        self.got = got

        def kernel(places_ref, *refs):
            for h in range(2):
                refs[4 + h][...] = (refs[h][...].astype(F32) + refs[2 + h][...].astype(F32)).astype(BF)

        return kernel, [*self.next, *self.part(got, 512, 1)], [(512, self.width, BF)] * 2, ()

    def send3(self, last):
        def kernel(places_ref, *refs):
            total = refs[-1]
            for h in range(2):
                keep, arrived, later, send, own = (refs[2 * k + h] for k in range(5))
                total[...] = keep[...].astype(F32) + arrived[...].astype(F32) + later[...].astype(F32)
                own_at, first, second, across = (
                    pl.ds(pl.multiple_of(places_ref[4 * (1 - h) + k] * 128, 128), 128) for k in range(4)
                )
                send[:128, :] = total[second, :].astype(BF)
                send[128:, :] = total[across, :].astype(BF)
                own[:128, :] = total[first, :].astype(BF)
                own[128:, :] = total[own_at, :].astype(BF)

        return (
            kernel,
            [*self.keep, *self.part(self.got, 512, 0, False), *self.part(last, 512, 0)],
            [(256, self.width, BF)] * 4,
            [pltpu.VMEM((512, self.width // 2), F32)],
        )

    def send4(self, got):
        self.got = got

        def kernel(places_ref, *refs):
            for h in range(2):
                refs[4 + h][...] = (refs[h][...].astype(F32) + refs[2 + h][...].astype(F32)).astype(BF)

        return (
            kernel,
            [*((value, 128, 0) for value in self.keep), *self.part(got, 128, 1)],
            [(128, self.width, BF)] * 2,
            (),
        )

    def finish(self, last):
        width, half = self.width, self.width // 2

        def kernel(places_ref, *refs):
            total = refs[-1]
            for h in range(2):
                for i in range(2):
                    at = slice(i * half, (i + 1) * half)
                    keep, arrived, later = refs[h][:, at], refs[2 + 2 * h + i][...], refs[6 + 2 * h + i][...]
                    total[:, h * width + i * half : h * width + (i + 1) * half] = (
                        keep.astype(F32) + arrived.astype(F32) + later.astype(F32)
                    )
            low = places_ref[8]
            refs[10][...] = total[pl.ds(pl.multiple_of(low * BLK, BLK), BLK), :]
            refs[11][...] = total[pl.ds(pl.multiple_of((1 - low) * BLK, BLK), BLK), :].astype(BF)

        def parts(got):
            return [(value, 128, 0, half, lambda i, k=k: 2 * k + self.index) for value in got for k in range(2)]

        return (
            kernel,
            [*((value, 128, 1) for value in self.keep), *parts(self.got), *parts([Arrived(value) for value in last])],
            [(BLK, 2 * width, F32), (BLK, 2 * width, BF)],
            [pltpu.VMEM((128, 2 * width), F32)],
        )


def add(places, *jobs, steps=2):
    def full(value, rows, at, columns=None, across=lambda i: i):
        return value, rows, at, columns or value.shape[1] // steps, across

    jobs = [
        (kernel, [full(*v) if isinstance(v, tuple) else full(v, v.shape[0], 0) for v in inputs], outs, scratch)
        for kernel, inputs, outs, scratch in jobs
    ]
    inputs = [value for _, given, _, _ in jobs for value in given]
    outs = [out for _, _, made, _ in jobs for out in made]

    def kernel(places_ref, *refs):
        given, made, spare = refs[: len(inputs)], refs[len(inputs) : len(inputs) + len(outs)], refs[len(inputs) + len(outs) :]
        for one, ins, results, scratch in jobs:
            one(places_ref, *given[: len(ins)], *made[: len(results)], *spare[: len(scratch)])
            given, made, spare = given[len(ins) :], made[len(results) :], spare[len(scratch) :]

    results = pl.pallas_call(
        kernel,
        grid=(steps,),
        in_specs=[SMEM]
        + [
            pl.BlockSpec((rows, columns), lambda i, at=at, across=across: (at, across(i)))
            for _, rows, at, columns, across in inputs
        ],
        out_specs=[pl.BlockSpec((rows, columns // steps), lambda i: (0, i)) for rows, columns, _ in outs],
        out_shape=[like(*shape) for shape in outs],
        scratch_shapes=[each for _, _, _, scratch in jobs for each in scratch],
        compiler_params=params(),
        cost_estimate=cost(),
        name="add",
    )(places, *in_hbm(*(value for value, *_ in inputs)))
    split = []
    for _, _, made, _ in jobs:
        split.append(results[: len(made)])
        results = results[len(made) :]
    return split


def together(*jobs):
    first = jobs[0][2][:2]

    def kernel(places_ref, *refs):
        counts = [len(inputs) for _, inputs, _, _ in jobs]
        refs, shared, rest = refs[: sum(counts)], refs[sum(counts) : sum(counts) + 2], list(refs[sum(counts) + 2 :])
        made = [[rest.pop(0) for _ in outs[2:]] for _, _, outs, _ in jobs]
        spare = [[rest.pop(0) for _ in scratch] for _, _, _, scratch in jobs]
        for k, (one, inputs, _, _) in enumerate(jobs):
            widths = [ref.shape[1] // len(jobs) for ref in shared]
            views = [ref.at[:, pl.ds(k * width, width)] for ref, width in zip(shared, widths)]
            one(places_ref, *refs[: counts[k]], *views, *made[k], *spare[k])
            refs = refs[counts[k] :]

    return (
        kernel,
        [value for _, inputs, _, _ in jobs for value in inputs],
        [(rows, len(jobs) * columns, kind) for rows, columns, kind in first]
        + [out for _, _, outs, _ in jobs for out in outs[2:]],
        [each for _, _, _, scratch in jobs for each in scratch],
    )


def attention_gradient(normed, d_projected, gradients, mixed):
    def kernel(normed_ref, d_ref, grad_ref, mixed_ref, out_ref):
        rows = pl.ds(pl.multiple_of(pl.program_id(0) * 512, 512), 512)
        sides = ((normed_ref[:, rows], d_ref, slice(0, 768)), (grad_ref[...], mixed_ref, slice(768, 1024)))
        for left, right, at in sides:
            out_ref[:, at] = lax.dot_general(
                left, right[...], (((0,), (0,)), ((), ())), preferred_element_type=F32
            ).astype(BF)

    def fixed(width):
        return pl.BlockSpec((1024, width), lambda i: (0, 0), pipeline_mode=pl.Buffered(1))

    return pl.pallas_call(
        kernel,
        grid=(D // 512,),
        in_specs=[VMEM, fixed(768), pl.BlockSpec((1024, 512), lambda i: (0, i)), fixed(256)],
        out_specs=pl.BlockSpec((512, 1024), lambda i: (i, 0)),
        out_shape=like(D, 1024),
        compiler_params=params(),
        cost_estimate=cost(),
        name="attention_gradient",
    )(in_vmem(normed), *in_hbm(d_projected, gradients, mixed))


def whole(low_index, *jobs):
    layouts = [each for _, _, layout in jobs for each in layout]

    def kernel(low_ref, *refs):
        halves, outs = refs[: 2 * len(jobs)], list(refs[2 * len(jobs) :])
        for k, (_, _, layout) in enumerate(jobs):
            at = 0
            for width, count in layout:
                out = outs.pop(0)
                mine = pl.ds(pl.multiple_of(low_ref[0] * width, width), width)
                theirs = pl.ds(pl.multiple_of((1 - low_ref[0]) * width, width), width)
                for i in range(count):
                    own, got = halves[2 * k], halves[2 * k + 1]
                    rows = pl.ds(0, BLK)
                    if own.shape[0] > BLK:
                        rows = pl.ds(pl.multiple_of(low_ref[0] * BLK, BLK), BLK)
                    out[i, :, mine] = own[rows, at : at + width].astype(F32)
                    out[i, :, theirs] = got[rows, at : at + width].astype(F32)
                    at += width

    return pl.pallas_call(
        kernel,
        in_specs=[SMEM] + [VMEM] * (2 * len(jobs)),
        out_specs=[VMEM] * len(layouts),
        out_shape=[pltpu.HBM((count, BLK, 2 * width), F32) for width, count in layouts],
        compiler_params=params(),
        cost_estimate=cost(),
        name="whole",
    )(low_index, *in_hbm(*(half for own, got, _ in jobs for half in (own, Arrived(got)))))


def inside(value):
    parts = [value[:, (low * 16 + n) * BLK : (low * 16 + n + 1) * BLK] for n in range(16) for low in range(2)]
    return jnp.concatenate(parts, axis=1)


def outside(value):
    parts = [value[:, (2 * n + low) * BLK : (2 * n + low + 1) * BLK] for low in range(2) for n in range(16)]
    return jnp.concatenate(parts, axis=1)


def prepare(low_index, residual, gradient, w_qkv, w_out, w_up, w_down, vectors):
    def kernel(low_ref, residual_ref, gradient_ref, qkv, out, up, down, *refs):
        *parts, tokens, grads, attn_own, attn_away, rest_own, rest_away, row = refs
        row[...] = jnp.concatenate([part[...].astype(F32) for part in parts] + [jnp.zeros((1, 80), F32)], axis=1).astype(BF)
        tokens[...] = inside(residual_ref[...])
        grads[...] = inside(gradient_ref[...])
        low = low_ref[0]
        for half, attn, rest in ((low, attn_own, rest_own), (1 - low, attn_away, rest_away)):
            narrow = pl.ds(pl.multiple_of(half * 256, 256), 256)
            wide = pl.ds(pl.multiple_of(half * 1024, 1024), 1024)
            for i in range(3):
                attn[:, i * 256 : (i + 1) * 256] = qkv[i, :, narrow]
            attn[:, 768:] = out[:, narrow]
            rest[:, :1024] = up[:, wide]
            rest[:, 1024:] = down[:, wide]

    return pl.pallas_call(
        kernel,
        in_specs=[SMEM] + [VMEM] * (6 + len(vectors)),
        out_specs=[VMEM] * 7,
        out_shape=[like(TOK, D)] * 2 + [like(BLK, 1024)] * 2 + [like(BLK, 2048)] * 2 + [like(1, 256)],
        compiler_params=params(),
        cost_estimate=cost(),
        name="prepare",
    )(low_index, *in_hbm(residual, gradient, w_qkv, w_out, w_up, w_down, *vectors))


def norm_and_project(core_index, mine, other, gain, shift, weights):
    def kernel(core_ref, mine_ref, other_ref, gain_ref, shift_ref, weight_ref, standard_ref, normed_ref, proj_ref):
        rows = (mine_ref[...], other_ref[...])
        first = core_ref[0] == 0
        value = jnp.concatenate([jnp.where(first, *rows), jnp.where(first, *rows[::-1])]).astype(F32)
        value = value - jnp.mean(value, axis=1, keepdims=True)
        value = value * lax.rsqrt(jnp.mean(value * value, axis=1, keepdims=True) + EPS)
        standard_ref[...] = value.astype(BF)
        normed = (value * gain_ref[...] + shift_ref[...]).astype(BF)
        normed_ref[...] = normed
        proj_ref[...] = jnp.dot(normed, weight_ref[...].reshape(D, 768), preferred_element_type=F32)

    def by_row(rows, width):
        return pl.BlockSpec((rows, width), lambda i: (i, 0))

    def fixed(*shape):
        return pl.BlockSpec(shape, lambda i: (0,) * len(shape), pipeline_mode=pl.Buffered(1))

    return pl.pallas_call(
        kernel,
        grid=(4,),
        in_specs=[SMEM, by_row(TOK, D), by_row(TOK, D), fixed(1, D), fixed(1, D), fixed(16, 128, 768)],
        out_specs=[by_row(256, D), by_row(256, D), by_row(256, 768)],
        out_shape=[like(1024, D), like(1024, D), like(1024, 768, F32)],
        compiler_params=params(),
        cost_estimate=cost(),
        name="norm_and_project",
    )(core_index, *in_hbm(mine, other, gain, shift, weights))


GELU_A = 0.7978845608028654
GELU_B = 0.044715


def hidden_units(places, normed, weights, shift, plan, pieces):
    width = 256
    steps = 1024 // width

    def kernel(places_ref, left, weight, shift_ref, *refs):
        inputs, (hidden_ref, slope_ref, whole_ref, stage, sems) = refs[: len(pieces)], refs[len(pieces) :]
        moves = []
        for i, (source, row, rows, _, _, _, to, place, unit, _) in enumerate(plan):
            at = pl.ds(pl.multiple_of(to + places_ref[place] * unit, rows), rows)
            moves.append(
                (
                    pltpu.make_async_copy(inputs[source].at[pl.ds(row, rows)], stage.at[at], sems.at[0, i]),
                    pltpu.make_async_copy(stage.at[at], whole_ref.at[at], sems.at[1, i]),
                )
            )

        @pl.when(pl.program_id(0) == 0)
        def _():
            for arrive, _ in moves:
                arrive.start()

        u = jnp.dot(left[...], weight[...], preferred_element_type=F32) + shift_ref[...]
        square = u * u
        t = jnp.tanh(GELU_A * u * (1.0 + GELU_B * square))
        half = 0.5 * (1.0 + t)
        hidden_ref[...] = (u * half).astype(BF)
        slope = half + 0.5 * u * (1.0 - t * t) * GELU_A * (1.0 + 3.0 * GELU_B * square)
        slope_ref[...] = slope.astype(BF)

        @pl.when(pl.program_id(0) == 1)
        def _():
            for arrive, leave in moves:
                arrive.wait()
                leave.start()

        @pl.when(pl.program_id(0) == steps - 1)
        def _():
            for _, leave in moves:
                leave.wait()

    column = pl.BlockSpec((1024, width), lambda i: (0, i))
    return pl.pallas_call(
        kernel,
        grid=(steps,),
        in_specs=[SMEM, VMEM, pl.BlockSpec((D, width), lambda i: (0, i)), pl.BlockSpec((1, width), lambda i: (0, i))]
        + [ANY] * len(pieces),
        out_specs=[column, column, ANY],
        out_shape=[like(1024, 1024), like(1024, 1024), like(D, 1024)],
        scratch_shapes=[pltpu.VMEM((D, 1024), BF), pltpu.SemaphoreType.DMA((2, len(plan)))],
        compiler_params=params(),
        cost_estimate=cost(),
        name="hidden_units",
    )(places, in_vmem(normed), *in_hbm(weights, shift, *pieces))


def hidden_back_kernel(left, weight, slope_ref, d_ref, sum_ref):
    value = jnp.dot(left[...], weight[...], preferred_element_type=F32) * slope_ref[...].astype(F32)
    value = value.astype(BF)
    d_ref[...] = value
    sum_ref[...] = jnp.sum(value.astype(F32), axis=0, keepdims=True)


def hidden_back_and_apart(places, gradients, weights, slope, lefts, others):
    width = 256
    kernel_apart, in_specs, out_specs, out_shape, scratch = apart_parts(lefts, others)
    count = len(in_specs)

    def kernel(places_ref, left, weight, slope_ref, *refs):
        given, (d_ref, sum_ref, *made) = refs[:count], refs[count:]
        hidden_back_kernel(left, weight, slope_ref, d_ref, sum_ref)
        kernel_apart(places_ref, *given, *made)

    column = pl.BlockSpec((1024, width), lambda i: (0, i))
    return pl.pallas_call(
        kernel,
        grid=(4,),
        in_specs=[
            SMEM,
            pl.BlockSpec((1024, D), lambda i: (0, 0), pipeline_mode=pl.Buffered(1)),
            pl.BlockSpec((D, width), lambda i: (0, i)),
            column,
        ]
        + in_specs,
        out_specs=[column, pl.BlockSpec((1, width), lambda i: (0, i))] + out_specs,
        out_shape=[like(1024, 1024), like(1, 1024, F32)] + out_shape,
        scratch_shapes=scratch,
        compiler_params=params(32 * 1024 * 1024),
        cost_estimate=cost(),
        name="hidden_back_and_apart",
    )(places, *in_hbm(gradients, weights, slope, *lefts, *(weight for weight, _ in others)))


def apart_parts(lefts, weights, standard=None, near=False):
    count = len(lefts)

    def kernel(places_ref, *refs):
        value_ref = refs[-1]
        value = sum(
            lax.dot_general(
                left[...],
                weight[...].reshape(-1, weight.shape[2]),
                (((1,), (1,)), ((), ())),
                preferred_element_type=F32,
            )
            for left, weight in zip(refs[:count], refs[count : 2 * count])
        )
        refs = refs[2 * count : -1]
        if standard is not None:
            standard_ref, refs = refs[0], refs[1:]
            refs[2][0:1, :] = jnp.sum(value * standard_ref[...].astype(F32), axis=0, keepdims=True)
            refs[2][1:2, :] = jnp.sum(value, axis=0, keepdims=True)
        value_ref[...] = value
        for h in range(2):
            for k in range(4):
                rows = pl.ds(pl.multiple_of(places_ref[4 * h + k] * TOK, TOK), TOK)
                refs[h][k * TOK : (k + 1) * TOK, :] = value_ref[rows, :].astype(BF)

    width = 512
    extra = standard is not None
    whole_left = [pl.BlockSpec(left.shape, lambda i: (0, 0), pipeline_mode=pl.Buffered(1)) for left in lefts]
    in_specs = [VMEM for _ in lefts] if near else whole_left
    in_specs += [
        pl.BlockSpec((4, 128, left.shape[1]), lambda i, at=at: (i, 0, at)) for left, (_, at) in zip(lefts, weights)
    ]
    in_specs += [pl.BlockSpec((1024, width), lambda i: (0, i))] * extra
    out_specs = [pl.BlockSpec((512, width), lambda i: (0, i))] * 2 + [pl.BlockSpec((2, width), lambda i: (0, i))] * extra
    out_shape = [like(512, D)] * 2 + [like(2, D, F32)] * extra
    return kernel, in_specs, out_specs, out_shape, [pltpu.VMEM((1024, width), F32)]


def apart(places, lefts, weights, standard):
    kernel, in_specs, out_specs, out_shape, scratch = apart_parts(lefts, weights, standard, True)
    return pl.pallas_call(
        kernel,
        grid=(4,),
        in_specs=[SMEM] + in_specs,
        out_specs=out_specs,
        out_shape=out_shape,
        scratch_shapes=scratch,
        compiler_params=params(),
        cost_estimate=cost(),
        name="apart",
    )(places, *(in_vmem(left) for left in lefts), *in_hbm(*(weight for weight, _ in weights), standard))


def token_sum1(near, got):
    def kernel(places_ref, near_ref, got_ref, send_ref):
        send_ref[...] = (near_ref[...].astype(F32) + got_ref[...].astype(F32)).astype(BF)

    return kernel, [(near, 256, 1), (Arrived(got), 256, 1)], [(256, D, BF)], ()


def token_sum2(near, got, back):
    def kernel(places_ref, near_ref, got_ref, back_ref, send_ref):
        value = near_ref[...].astype(F32) + got_ref[...].astype(F32) + back_ref[...].astype(F32)
        send_ref[...] = value.astype(BF)

    return kernel, [(near, TOK, 1), (got, TOK, 1), (Arrived(back), TOK, 1)], [(TOK, D, BF)], ()


ROWS = pl.BlockSpec((TOK // 4, D), lambda i: (i, 0))
ONE_ROW = pl.BlockSpec((1, D), lambda i: (0, 0))


def finish_output(near, got, back, last, residual, shift):
    def kernel(near_ref, got_ref, back_ref, last_ref, residual_ref, shift_ref, out_ref):
        value = sum(ref[...].astype(F32) for ref in (near_ref, got_ref, back_ref, last_ref))
        value = residual_ref[...].astype(F32) + value + shift_ref[...]
        out_ref[...] = outside(value.astype(BF))

    return pl.pallas_call(
        kernel,
        grid=(4,),
        in_specs=[ROWS] * 5 + [ONE_ROW],
        out_specs=ROWS,
        out_shape=like(TOK, D),
        compiler_params=params(),
        cost_estimate=cost(),
        name="finish_output",
    )(*in_hbm(near, got, back, Arrived(last), residual, shift))


def finish_grad(near, got, back, last, residual, gradient, gain):
    def kernel(near_ref, got_ref, back_ref, last_ref, residual_ref, gradient_ref, gain_ref, out_ref):
        value = sum(ref[...].astype(F32) for ref in (near_ref, got_ref, back_ref, last_ref))
        value = value * gain_ref[...]
        rows = residual_ref[...].astype(F32)
        rows = rows - jnp.mean(rows, axis=1, keepdims=True)
        inverse = lax.rsqrt(jnp.mean(rows * rows, axis=1, keepdims=True) + EPS)
        rows = rows * inverse
        plain = jnp.mean(value, axis=1, keepdims=True)
        cross = jnp.mean(value * rows, axis=1, keepdims=True)
        out_ref[...] = outside(gradient_ref[...].astype(F32) + inverse * (value - plain - rows * cross))

    return pl.pallas_call(
        kernel,
        grid=(4,),
        in_specs=[ROWS] * 6 + [ONE_ROW],
        out_specs=ROWS,
        out_shape=like(TOK, D, F32),
        compiler_params=params(),
        cost_estimate=cost(),
        name="finish_grad",
    )(*in_hbm(near, got, back, Arrived(last), residual, gradient, gain))


def doc_positions(segments):
    length = segments.shape[0]
    places = jnp.arange(length, dtype=jnp.int32)
    boundary = jnp.concatenate([jnp.ones((1,), dtype=jnp.bool_), segments[1:] != segments[:-1]])
    doc_start = lax.cummax(jnp.where(boundary, places, jnp.zeros_like(places)), axis=0)
    return places - doc_start


def rotary_tables(positions):
    lane = jnp.arange(128, dtype=jnp.int32) % HD
    half_rot = ROT // 2
    frequency = 10000.0 ** (-(2.0 * (lane % half_rot).astype(F32)) / ROT)
    angles = positions.astype(F32)[:, None] * jnp.where(lane < ROT, frequency, 0.0)
    sine = jnp.sin(angles)
    before = jnp.where(lane < half_rot, -sine, 0.0)
    after = jnp.where((lane >= half_rot) & (lane < ROT), sine, 0.0)
    return jnp.concatenate([jnp.cos(angles), before, after], axis=1)


def attention_kernel(
    core_ref,
    proj_ref,
    shift_ref,
    table_ref,
    column_ref,
    row_ref,
    mine_ref,
    other_ref,
    weight_ref,
    mixed_ref,
    d_proj_ref,
    sums_ref,
    grad_ref,
    mask_ref,
):
    start, last = column_ref[:, 0:1], column_ref[:, 1:2]
    where = row_ref[0]
    mask_ref[...] = jnp.where((where >= start) & (where <= last), 0.0, MASKED)
    cosine, before, after = (table_ref[:, i * 128 : (i + 1) * 128] for i in range(3))
    lane = lax.broadcasted_iota(jnp.int32, (SEQ, 128), 1)

    def turn(value, sign):
        shifted = pltpu.roll(value, 112, 1) * before + pltpu.roll(value, 16, 1) * after
        return value * cosine + sign * shifted

    def part(index, pair):
        at = slice(index * 256 + pair * 128, index * 256 + pair * 128 + 128)
        return proj_ref[:, at] + shift_ref[:, at]

    def dot(a, b, dims):
        return lax.dot_general(a, b, (dims, ((), ())), preferred_element_type=F32)

    first_core = core_ref[0] == 0
    for i in range(2):
        both = [ref[i * TOK : (i + 1) * TOK, :] for ref in (mine_ref, other_ref)]
        grad_ref[2 * i * TOK : (2 * i + 1) * TOK, :] = jnp.where(first_core, *both)
        grad_ref[(2 * i + 1) * TOK : (2 * i + 2) * TOK, :] = jnp.where(first_core, *both[::-1])
    d_attended = jnp.dot(grad_ref[...], weight_ref[...].reshape(D, 256), preferred_element_type=F32).astype(BF)
    for pair in range(2):
        at = slice(pair * 128, pair * 128 + 128)
        queries = (turn(part(0, pair), 1.0).astype(BF).astype(F32) * HD**-0.5).astype(BF)
        keys = turn(part(1, pair), 1.0).astype(BF)
        values = part(2, pair).astype(BF)
        d_out = d_attended[:, at]
        results = []
        for head in range(2):
            own = (lane >= head * HD) & (lane < (head + 1) * HD)
            own_queries = jnp.where(own, queries, jnp.zeros_like(queries))
            own_d_out = jnp.where(own, d_out, jnp.zeros_like(d_out))
            scores = dot(own_queries, keys, ((1,), (1,))) + mask_ref[...]
            exponent = jnp.exp(scores - jnp.max(scores, axis=1, keepdims=True))
            soft = exponent * (1.0 / jnp.sum(exponent, axis=1, keepdims=True))
            soft_low = soft.astype(BF)
            mixed = dot(soft_low, values, ((1,), (0,)))
            d_soft = dot(own_d_out, values, ((1,), (1,)))
            inner = jnp.sum(soft * d_soft, axis=1, keepdims=True)
            d_scores = (soft * (d_soft - inner)).astype(BF)
            d_queries = dot(d_scores, keys, ((1,), (0,))) * HD**-0.5
            d_keys = dot(d_scores, own_queries, ((0,), (0,)))
            d_values = dot(soft_low, own_d_out, ((0,), (0,)))
            results.append((mixed, d_queries, d_keys, d_values))
        first, second = results
        mixed_ref[:, at] = jnp.where(lane < HD, first[0], second[0]).astype(BF)
        d_queries = turn(jnp.where(lane < HD, first[1], second[1]), -1.0).astype(BF)
        d_keys = turn(first[2] + second[2], -1.0).astype(BF)
        d_values = (first[3] + second[3]).astype(BF)
        for index, value in enumerate((d_queries, d_keys, d_values)):
            at = slice(index * 256 + pair * 128, index * 256 + pair * 128 + 128)
            d_proj_ref[:, at] = value
            sums_ref[0, :, at] = jnp.sum(value.astype(F32), axis=0, keepdims=True)


def attention(core_index, projected, shift, tables, columns, rows, mine, other, weights):
    count = projected.shape[0] // SEQ
    return pl.pallas_call(
        attention_kernel,
        grid=(count,),
        in_specs=[
            SMEM,
            pl.BlockSpec((SEQ, 768), lambda i: (i, 0)),
            pl.BlockSpec((1, 768), lambda i: (0, 0)),
            pl.BlockSpec((SEQ, 384), lambda i: (i, 0)),
            pl.BlockSpec((SEQ, 2), lambda i: (i, 0)),
            pl.BlockSpec((1, 1, SEQ), lambda i: (i, 0, 0)),
            pl.BlockSpec((SEQ // 2, D), lambda i: (i, 0)),
            pl.BlockSpec((SEQ // 2, D), lambda i: (i, 0)),
            pl.BlockSpec((16, 128, 256), lambda i: (0, 0, 3), pipeline_mode=pl.Buffered(1)),
        ],
        out_specs=[
            pl.BlockSpec((SEQ, 256), lambda i: (i, 0)),
            pl.BlockSpec((SEQ, 768), lambda i: (i, 0)),
            pl.BlockSpec((1, 1, 768), lambda i: (i, 0, 0)),
            pl.BlockSpec((SEQ, D), lambda i: (i, 0)),
        ],
        out_shape=[
            pltpu.HBM((count * SEQ, 256), BF),
            pltpu.HBM((count * SEQ, 768), BF),
            pltpu.HBM((count, 1, 768), F32),
            like(count * SEQ, D),
        ],
        scratch_shapes=[pltpu.VMEM((SEQ, SEQ), F32)],
        compiler_params=pltpu.CompilerParams(vmem_limit_bytes=VMEM_LIMIT),
        cost_estimate=cost(),
        name="attention",
    )(core_index, *in_hbm(projected, shift, tables, columns, rows, mine, Arrived(other), weights))


def body(
    residual_in,
    segment_ids,
    out_grad,
    ln_gain,
    ln_bias,
    w_qkv,
    b_qkv,
    w_out,
    b_attn_out,
    w_up,
    b_up,
    w_down,
    b_mlp_out,
):
    y_lo, x, z, y_hi, core = (lax.axis_index(name).astype(jnp.int32) for name in AXES)
    low_index = y_lo[None]
    low = y_lo == 0

    def around(c):
        return [c, c ^ (1 + 2 * core), c ^ (3 - 2 * core), c ^ 2]

    y_places = [
        y_lo * 2 + y_hi,
        (1 - y_lo) * 2 + (y_hi ^ core),
        (1 - y_lo) * 2 + (y_hi ^ (1 - core)),
        y_lo * 2 + (1 - y_hi),
    ]
    ring_places = jnp.stack(
        around(x)
        + around(z)
        + [y_lo, 1 - y_lo]
        + y_places
        + [2 * k + core for k in range(4)]
        + [2 * k + 1 - core for k in range(4)]
    )
    part_places = jnp.stack(
        [2 * p + core for p in y_places] + [2 * y_places[k] + 1 - core for k in (0, 2, 1, 3)]
    )

    vectors = [value.reshape(1, -1) for value in (ln_gain, ln_bias, b_attn_out, b_mlp_out, b_up)]
    vectors += [b_qkv[i] for i in range(3)]
    residual, gradient, attn_own, attn_away, rest_own, rest_away, small = prepare(
        low_index, residual_in, out_grad, w_qkv.transpose(1, 0, 2), w_out.T, w_up, w_down.T, vectors
    )

    def widen(rows, axis, index):
        got = flip(rows, axis)
        return jnp.where(index == 0, jnp.concatenate([rows, got]), jnp.concatenate([got, rows]))

    attn_got = flip(attn_away, "y_lo")
    small = widen(small, "core", core)
    small = widen(small, "y_hi", y_hi)
    attn_got, small, residual, gradient, rest_away = bar((attn_got, small, residual, gradient, rest_away))
    small = jnp.pad(small.reshape(1, 1024), ((0, 15), (0, 0)))

    def token_positions():
        far_segments = flip(segment_ids, "y_lo")
        places = jnp.arange(SEQ, dtype=jnp.int32)
        positions = jnp.concatenate(
            [doc_positions(jnp.where(low, a, b)) for a, b in ((segment_ids, far_segments), (far_segments, segment_ids))]
        )
        places = jnp.concatenate([places, places])
        columns = places[:, None] - jnp.where(jnp.arange(2)[None] == 0, positions[:, None], 0)
        return columns, places.reshape(2, 1, SEQ), rotary_tables(positions)

    def joined(own, first):
        plan = [(source, 0, TOK, 0, D, 0, TOK * source, None, 0, 0) for source in range(2)]
        return plan, [(2 * TOK, D)], [own, Arrived(first)], False

    def of_core(own, first, second):
        plan = [
            (source, row, TOK, 0, D, 0, 0, 10 + k, TOK, 0)
            for k, (source, row) in enumerate(((0, 0), (1, 0), (2, 0), (2, TOK)))
        ]
        return plan, [(SEQ, D)], [own, Arrived(first), Arrived(second)], False

    plan = [(source, 0, BLK, 0, 1024, 0, 0, 8 + source, BLK, 0) for source in range(2)]
    plan.append((2, 0, 16, 0, 1024, 0, 128, None, 0, 0))
    ((shard,),) = copies(ring_places, (plan, [(144, 1024)], [attn_own, Arrived(attn_got), small], False))
    attn_all = lax.all_gather(shard, ("x", "z"), axis=0)
    token_first = swap_y(residual, 0)
    rest_got = flip(rest_away, "y_lo")
    shard, token_first, rest_got, gradient = bar((shard, token_first, rest_got, gradient))
    plan = [
        (source, 0, BLK, 1024 * h, 1024, h, 0, 8 + source, BLK, 0) for source in range(2) for h in range(2)
    ]
    (tokens_sent,), sends = copies(
        ring_places, joined(residual, token_first), (plan, [(128, 1024)] * 2, [rest_own, Arrived(rest_got)], False)
    )
    rest_gather = Gather(*sends)
    tokens_sent, sends, gradient = bar((tokens_sent, sends, gradient))
    token_second = swap_y(tokens_sent, 1)
    grad_first = swap_y(gradient, 0)
    got = gather_step(1, sends)
    token_second, grad_first, got = bar((token_second, grad_first, got))
    (mine,), (grads_sent,), sends = copies(
        ring_places,
        of_core(residual, token_first, token_second),
        joined(gradient, grad_first),
        rest_gather.sending(got),
    )
    mine, grads_sent, sends = bar((mine, grads_sent, sends))
    other = flip(mine, "core")
    grad_second = swap_y(grads_sent, 1)
    positions = token_positions()
    got, other, mine, grad_second, positions, table = bar(
        (gather_step(2, sends), other, mine, grad_second, positions, attn_all[:, 128, :][None])
    )
    tokens = (mine, other)
    other_table = flip(table, "y_lo")
    rest_gather.pair, (mine,) = copies(
        ring_places, rest_gather.joining(got, False), of_core(gradient, grad_first, grad_second)
    )
    sends, mine, table, other_table = bar((rest_gather.pair, mine, table, other_table))
    other = flip(mine, "core")
    got = gather_step(3, sends)
    columns, rows, tables = positions

    table = jnp.where(low, jnp.concatenate([table, other_table]), jnp.concatenate([other_table, table]))
    table = table.reshape(2, 16, 4, 256).astype(F32)
    vectors = table[..., :64].reshape(2, 16, 4, 4, 16).transpose(3, 1, 0, 2, 4).reshape(4, D)
    gain, shift, out_shift = vectors[0:1], vectors[1:2], vectors[2:3] + vectors[3:4]
    shifts = lax.dynamic_index_in_dim(table.reshape(2, 16, 4, 256), y_hi * 2 + core, 2, False)
    shifts = lax.dynamic_index_in_dim(shifts, y_lo, 0, False)
    up_shift = shifts[:, 64:128].reshape(1, 1024)
    qkv_shift = shifts[:, 128:176].reshape(16, 3, 16).transpose(1, 0, 2).reshape(1, 768)

    standard, normed, projected = norm_and_project(core[None], *tokens, gain, shift, attn_all)
    got, other, mine, normed, projected = bar((got, other, mine, normed, projected))
    (sends,) = copies(ring_places, rest_gather.sending(got))
    sends, mine, other, projected = bar((sends, mine, other, projected))
    rest_got = gather_step(4, sends)
    mixed, d_projected, shift_sums, grad_all = attention(
        core[None], projected, qkv_shift, tables, columns, rows, mine, other, attn_all
    )
    attn_sum = attention_gradient(normed, d_projected, grad_all, mixed)
    attn_sum, rest_got, normed = bar((attn_sum, rest_got, normed))
    attn_sum = lax.psum_scatter(attn_sum, ("x", "z"), scatter_dimension=0, tiled=True)

    ((up_all,),) = copies(ring_places, rest_gather.joining(rest_got, True))
    hidden, slope, down_all = hidden_units(ring_places, normed, up_all, up_shift, *rest_gather.right())
    down_sum = Scatter(ring_places, 0, grad_all, hidden)
    sends, mixed, hidden, slope, grad_all = bar((down_sum.first, mixed, hidden, slope, grad_all))
    down_got = scatter_step(1, sends)
    d_hidden, up_shift_part, near, away = hidden_back_and_apart(
        part_places, grad_all, down_all, slope, [mixed, hidden], [(attn_all, 3), (down_all.reshape(16, 128, 1024), 0)]
    )
    up_sum = Scatter(ring_places, 1, normed, d_hidden)
    up_sends, near, away, d_hidden, down_got = bar((up_sum.first, near, away, d_hidden, down_got))

    up_got = scatter_step(1, up_sends)
    out_got = flip(away, "core")
    d_near, d_away, vector_parts = apart(
        part_places,
        [d_projected, d_hidden],
        [(attn_all, 0), (up_all.reshape(16, 128, 1024), 0)],
        standard,
    )
    d_away, up_got, out_got, vector_parts = bar((d_away, up_got, out_got, vector_parts))
    sums = (down_sum, up_sum)
    sends, (out_send,) = add(
        ring_places,
        together(down_sum.send2(down_got), up_sum.send2(up_got)),
        token_sum1(near, out_got),
    )
    sends, out_send, d_away, vector_parts = bar((sends, out_send, d_away, vector_parts))
    d_got = flip(d_away, "core")
    got = scatter_step(2, sends)
    out_back = swap_y(out_send, 1)
    out_shift_part = jnp.sum(gradient.astype(F32), axis=0, keepdims=True)
    parts = jnp.concatenate([vector_parts, out_shift_part]).reshape(3, 16, 8, 16)
    parts = parts.transpose(1, 2, 0, 3).reshape(16, 384)
    shift_sums = jnp.sum(shift_sums, axis=(0, 1))
    line = jnp.concatenate(
        [
            parts,
            up_shift_part.reshape(16, 64),
            shift_sums.reshape(3, 16, 16).transpose(1, 0, 2).reshape(16, 48),
            jnp.zeros((16, 16), F32),
        ],
        axis=1,
    )
    offsets = [0]
    for _, _, bits in RING_STEPS:
        offsets = offsets + [o ^ bits for o in offsets]
    here = (4 * x + z) ^ jnp.array(offsets, jnp.int32)
    order = (here[:, None] == jnp.arange(16, dtype=jnp.int32)[None, :]).astype(F32)
    line = jnp.dot(order, line, precision=lax.Precision.HIGHEST)

    def fold(line, step):
        axis, mask, _ = RING_STEPS[step]
        count = line.shape[0] // 2
        return line[:count] + flip4(line[count:], axis, mask)

    def narrow(part, axis, index):
        part = part.reshape(2, -1)
        return jnp.where(index == 0, part[0], part[1]) + flip(jnp.where(index == 0, part[1], part[0]), axis)

    line = fold(fold(line, 3), 2)
    d_got, got, out_back, line = bar((d_got, got, out_back, line))
    sends, (d_send,), (out_send,) = add(
        ring_places,
        together(*(each.send3(got) for each in sums)),
        token_sum1(d_near, d_got),
        token_sum2(near, out_got, out_back),
    )
    down_sum.keep, up_sum.keep = sends[2:4], sends[4:]
    sends, d_send, out_send, line = bar((sends[:2], d_send, out_send, line))
    d_back = swap_y(d_send, 1)
    got = scatter_step(3, sends)
    line = fold(fold(line, 1), 0)[0]
    part = narrow(line[:384], "y_lo", y_lo)
    out_last = swap_y(out_send, 0)
    d_back, got, part, out_last, attn_sum = bar((d_back, got, part, out_last, attn_sum))
    sends, (d_send,) = add(
        ring_places, together(*(each.send4(got) for each in sums)), token_sum2(d_near, d_got, d_back)
    )
    sends, d_send, part, attn_sum, out_last = bar((sends, d_send, part, attn_sum, out_last))
    d_last = swap_y(d_send, 0)
    got = scatter_step(4, sends)
    attn_far = flip(attn_sum, "y_lo")
    part = narrow(part, "y_hi", y_hi)
    output = finish_output(near, out_got, out_back, out_last, residual, out_shift)
    d_last, got, part, attn_far, output = bar((d_last, got, part, attn_far, output))
    ((own, away),) = add(ring_places, together(*(each.finish(got) for each in sums)), steps=1)
    away, part, d_last = bar((away, part, d_last))
    far = flip(away, "y_lo")
    part = narrow(part, "core", core)
    grad_in = finish_grad(d_near, d_got, d_back, d_last, residual, gradient, gain)
    far, part, grad_in = bar((far, part, grad_in))
    sum_down, sum_up, sum_qkv, sum_out = whole(
        low_index, (own, far, ((1024, 1), (1024, 1))), (attn_sum, attn_far, ((256, 3), (256, 1)))
    )
    grad_gain, grad_shift, grad_out_shift = part[:16], part[16:32], part[32:]
    return (
        output,
        grad_in,
        grad_gain,
        grad_shift,
        sum_qkv.transpose(1, 0, 2),
        line[448:496].reshape(3, 1, 16),
        sum_out[0].T,
        grad_out_shift,
        sum_up[0],
        line[384:448].reshape(1, 64),
        sum_down[0].T,
        grad_out_shift,
    )


def solution(mesh):
    fine = Mesh(mesh.devices.reshape(2, 4, 4, 2, 2), AXES)
    dp = ("y_lo", "x", "z")
    tensor = ("y_hi", "core")
    every = AXES
    in_specs = (
        P(every, None),
        P(dp),
        P(every, None),
        P(every),
        P(every),
        P(dp, None, tensor),
        P(None, tensor, dp),
        P(tensor, dp),
        P(every),
        P(dp, tensor),
        P(tensor, dp),
        P(tensor, dp),
        P(every),
    )
    out_specs = (
        P(every, None),
        P(every, None),
        P(every),
        P(every),
        P(dp, None, tensor),
        P(None, tensor, dp),
        P(tensor, dp),
        P(every),
        P(dp, tensor),
        P(tensor, dp),
        P(tensor, dp),
        P(every),
    )
    return jax.shard_map(body, mesh=fine, in_specs=in_specs, out_specs=out_specs, check_vma=False)
```

```python
import jax
import jax.numpy as jnp
from jax import lax
from jax.experimental import pallas as pl
from jax.experimental.pallas import tpu as pltpu
from jax.sharding import Mesh, PartitionSpec as P

HD = 64
ROT = 32
EPS = 1e-05
MASKED = -1e30
D = 2048
SEQ = 512
TOK = 128
BLK = 64
VMEM_LIMIT = 24 * 1024 * 1024
BF = jnp.bfloat16
F32 = jnp.float32
AXES = ("y_lo", "x", "z", "y_hi", "core")


bar = lax.optimization_barrier


def params(limit=VMEM_LIMIT):
    return pltpu.CompilerParams(vmem_limit_bytes=limit)


def cost():
    return pl.CostEstimate(flops=1000, bytes_accessed=1000, transcendentals=0)


def like(rows, columns, kind=BF):
    return pltpu.HBM((rows, columns), kind)


class Arrived:
    def __init__(self, value):
        self.value, self.shape = value, value.shape


def in_hbm(*values):
    return tuple(
        value.value if isinstance(value, Arrived) else pltpu.with_memory_space_constraint(value, pltpu.HBM)
        for value in values
    )


def in_vmem(value):
    return pltpu.with_memory_space_constraint(value, pltpu.VMEM)


SMEM = pl.BlockSpec(memory_space=pltpu.SMEM)
VMEM = pl.BlockSpec(memory_space=pltpu.VMEM)
ANY = pl.BlockSpec(memory_space=pl.ANY)


def ring(value, axis, step):
    masks = (1, 3) if step == 0 else (3, 1)
    table = [(i * 2 + c, (i ^ masks[c]) * 2 + c) for i in range(4) for c in range(2)]
    return lax.ppermute(value, (axis, "core"), table)


def ring_pair(pair, axes, step):
    pair = bar(tuple(pair))
    return bar(tuple(ring(value, axis, step) for value, axis in zip(pair, axes)))


def swap_y(value, step):
    masks = (1, 3) if step == 0 else (3, 1)

    def place(y, c):
        return ((y % 2) * 2 + y // 2) * 2 + c

    table = [(place(y, c), place(y ^ masks[c], c)) for y in range(4) for c in range(2)]
    return lax.ppermute(value, ("y_lo", "y_hi", "core"), table)


def flip(value, axis):
    return lax.ppermute(value, axis, [(0, 1), (1, 0)])


def copies(places, *jobs):
    sources = [source for _, _, given, _ in jobs for source in given]
    shapes = [(shape, stay) for _, made, _, stay in jobs for shape in made]
    plans, low, made = [], 0, 0
    for plan, results, given, stay in jobs:
        for source, row, rows, column, columns, target, to, place, unit, across in plan:
            plans.append((source + low, row, rows, column, columns, target + made, to, place, unit, across, stay))
        low += len(given)
        made += len(results)

    def kernel(places_ref, *refs):
        inputs, refs = refs[: len(sources)], refs[len(sources) :]
        outputs, spare, sems = refs[: len(shapes)], list(refs[len(shapes) : -1]), refs[-1]
        stages = [output if stay else spare.pop(0) for output, (_, stay) in zip(outputs, shapes)]
        moves = []
        for i, (source, row, rows, column, columns, target, to, place, unit, across, stay) in enumerate(plans):
            if place is not None:
                to = pl.multiple_of(to + places_ref[place] * unit, rows)
            at = (pl.ds(to, rows), pl.ds(across, columns))
            stage = stages[target].at[at]
            arrive = pltpu.make_async_copy(
                inputs[source].at[pl.ds(row, rows), pl.ds(column, columns)], stage, sems.at[0, i]
            )
            arrive.start()
            leave = None if stay else pltpu.make_async_copy(stage, outputs[target].at[at], sems.at[1, i])
            moves.append((arrive, leave))
        for arrive, leave in moves:
            arrive.wait()
            if leave is not None:
                leave.start()
        for _, leave in moves:
            if leave is not None:
                leave.wait()

    outs = pl.pallas_call(
        kernel,
        in_specs=[SMEM] + [ANY] * len(sources),
        out_specs=[VMEM if stay else ANY for _, stay in shapes],
        out_shape=[pltpu.VMEM(shape, BF) if stay else like(*shape) for shape, stay in shapes],
        scratch_shapes=[pltpu.VMEM(shape, BF) for shape, stay in shapes if not stay]
        + [pltpu.SemaphoreType.DMA((2, len(plans)))],
        compiler_params=params(),
        cost_estimate=cost(),
        name="put_together",
    )(places, *in_hbm(*sources))
    results = []
    for _, made, _, _ in jobs:
        results.append(outs[: len(made)])
        outs = outs[len(made) :]
    return results


def flip4(value, axis, mask):
    return lax.ppermute(value, axis, [(i, i ^ mask) for i in range(4)])


RING_STEPS = (("z", 1, 1), ("z", 3, 3), ("x", 1, 4), ("x", 3, 12))


class Gather:
    def __init__(self, left, right):
        self.pair = (left, right)

    def sending(self, got):
        self.first = got
        rows, width = self.pair[0].shape
        plan = [(2 * h + k, 0, rows, 0, width, h, k * rows, None, 0, 0) for h in range(2) for k in range(2)]
        sources = [value for own, first in zip(self.pair, got) for value in (own, Arrived(first))]
        return plan, [(2 * rows, width)] * 2, sources, False

    def joining(self, got):
        rows, width = self.pair[0].shape
        sources = [value for own, first, last in zip(self.pair, self.first, got) for value in (own, first, Arrived(last))]
        plan = []
        for h in range(2):
            for k, (source, row) in enumerate(((0, 0), (1, 0), (2, 0), (2, rows))):
                plan.append((source + 3 * h, row, rows, 0, width, h, 0, 4 * h + k, rows, 0))
        return plan, [(4 * rows, width)] * 2, sources, False

    def ordered(self, h):
        rows, width = self.pair[0].shape
        plan = []
        for k, (source, row) in enumerate(((0, 0), (1, 0), (2, 0), (2, rows))):
            for i in range(4):
                to, unit = ((i * 512, 128), (i * 128, 512))[h]
                plan.append((source, row + i * 128, 128, 0, width, 0, to, 4 * (1 - h) + k, unit, 0))
        return plan

    def side(self, h):
        return self.ordered(h), (self.pair[h], self.first[h], self.last[h])


def gather_step(step, pair):
    return ring_pair(pair, ("x", "z") if step < 3 else ("z", "x"), 1 - step % 2)


def scatter_step(step, pair):
    return ring_pair(pair, ("x", "z") if step < 3 else ("z", "x"), step % 2)


class Scatter:
    def __init__(self, places, index, left, right):
        self.places, self.index = places, index
        tokens, width = right.shape
        self.width = half = width // 2

        def kernel(places_ref, left_ref, right_ref, *refs):
            outs, (rights, *stages), sems = refs[:6], refs[6:-1], refs[-1]
            fetch = [
                pltpu.make_async_copy(right_ref.at[:, pl.ds(h * half, half)], rights.at[h], sems.at[h]) for h in range(2)
            ]
            for copy in fetch:
                copy.start()
            order = [2, 3, 1, 0]
            stored = []
            for h in range(2):
                fetch[h].wait()
                for i, k in enumerate(order):
                    if h == 0:
                        block = left_ref[:, pl.ds(pl.multiple_of(places_ref[k] * 512, 512), 512)]
                    else:
                        z = places_ref[4 + k]
                        block = jnp.concatenate(
                            [left_ref[:, pl.ds(pl.multiple_of(n * 512 + z * 128, 128), 128)] for n in range(4)], axis=1
                        )
                    value = lax.dot_general(
                        block,
                        rights[h],
                        (((0,), (0,)), ((), ())),
                        preferred_element_type=F32,
                    ).astype(BF)
                    stage = stages[h].at[pl.ds(i * 512, 512)]
                    stage[...] = value
                    out = outs[h].at[pl.ds(i * 512, 512)] if i < 2 else outs[2 * i - 2 + h]
                    copy = pltpu.make_async_copy(stage, out, sems.at[2 + 4 * h + i])
                    copy.start()
                    stored.append(copy)
            for copy in stored:
                copy.wait()

        outs = pl.pallas_call(
            kernel,
            in_specs=[SMEM, VMEM, ANY],
            out_specs=[ANY] * 6,
            out_shape=[like(1024, half)] * 2 + [like(512, half)] * 4,
            scratch_shapes=[
                pltpu.VMEM((2, tokens, half), BF),
                pltpu.VMEM((2048, half), BF),
                pltpu.VMEM((2048, half), BF),
                pltpu.SemaphoreType.DMA((10,)),
            ],
            compiler_params=params(),
            cost_estimate=cost(),
            name="gradient",
        )(places, in_vmem(left), *in_hbm(right))
        self.first, self.next, self.keep = outs[:2], outs[2:4], outs[4:]

    def part(self, got, rows, at, new=True):
        half = self.width // 2
        alone = got[0].shape[1] == self.width
        return [
            (Arrived(value) if new else value, rows, at, half, (lambda i: i) if alone else (lambda i: 2 * i + self.index)) for value in got
        ]

    def send2(self, got):
        self.got = got

        def kernel(places_ref, *refs):
            for h in range(2):
                refs[4 + h][...] = (refs[h][...].astype(F32) + refs[2 + h][...].astype(F32)).astype(BF)

        return kernel, [*self.next, *self.part(got, 512, 1)], [(512, self.width, BF)] * 2, ()

    def send3(self, last):
        def kernel(places_ref, *refs):
            total = refs[-1]
            for h in range(2):
                keep, arrived, later, send, own = (refs[2 * k + h] for k in range(5))
                total[...] = keep[...].astype(F32) + arrived[...].astype(F32) + later[...].astype(F32)
                own_at, first, second, across = (
                    pl.ds(pl.multiple_of(places_ref[4 * (1 - h) + k] * 128, 128), 128) for k in range(4)
                )
                send[:128, :] = total[second, :].astype(BF)
                send[128:, :] = total[across, :].astype(BF)
                own[:128, :] = total[first, :].astype(BF)
                own[128:, :] = total[own_at, :].astype(BF)

        return (
            kernel,
            [*self.keep, *self.part(self.got, 512, 0, False), *self.part(last, 512, 0)],
            [(256, self.width, BF)] * 4,
            [pltpu.VMEM((512, self.width // 2), F32)],
        )

    def send4(self, got):
        self.got = got

        def kernel(places_ref, *refs):
            for h in range(2):
                refs[4 + h][...] = (refs[h][...].astype(F32) + refs[2 + h][...].astype(F32)).astype(BF)

        return (
            kernel,
            [*((value, 128, 0) for value in self.keep), *self.part(got, 128, 1)],
            [(128, self.width, BF)] * 2,
            (),
        )

    def finish(self, last):
        width, half = self.width, self.width // 2

        def kernel(places_ref, *refs):
            total = refs[-1]
            for h in range(2):
                for i in range(2):
                    at = slice(i * half, (i + 1) * half)
                    keep, arrived, later = refs[h][:, at], refs[2 + 2 * h + i][...], refs[6 + 2 * h + i][...]
                    total[:, h * width + i * half : h * width + (i + 1) * half] = (
                        keep.astype(F32) + arrived.astype(F32) + later.astype(F32)
                    )
            low = places_ref[8]
            refs[10][...] = total[pl.ds(pl.multiple_of(low * BLK, BLK), BLK), :]
            refs[11][...] = total[pl.ds(pl.multiple_of((1 - low) * BLK, BLK), BLK), :].astype(BF)

        def parts(got):
            return [(value, 128, 0, half, lambda i, k=k: 2 * k + self.index) for value in got for k in range(2)]

        return (
            kernel,
            [*((value, 128, 1) for value in self.keep), *parts(self.got), *parts([Arrived(value) for value in last])],
            [(BLK, 2 * width, F32), (BLK, 2 * width, BF)],
            [pltpu.VMEM((128, 2 * width), F32)],
        )


def add(places, *jobs, steps=2):
    def full(value, rows, at, columns=None, across=lambda i: i):
        return value, rows, at, columns or value.shape[1] // steps, across

    jobs = [
        (kernel, [full(*v) if isinstance(v, tuple) else full(v, v.shape[0], 0) for v in inputs], outs, scratch)
        for kernel, inputs, outs, scratch in jobs
    ]
    inputs = [value for _, given, _, _ in jobs for value in given]
    outs = [out for _, _, made, _ in jobs for out in made]

    def kernel(places_ref, *refs):
        given, made, spare = refs[: len(inputs)], refs[len(inputs) : len(inputs) + len(outs)], refs[len(inputs) + len(outs) :]
        for one, ins, results, scratch in jobs:
            one(places_ref, *given[: len(ins)], *made[: len(results)], *spare[: len(scratch)])
            given, made, spare = given[len(ins) :], made[len(results) :], spare[len(scratch) :]

    results = pl.pallas_call(
        kernel,
        grid=(steps,),
        in_specs=[SMEM]
        + [
            pl.BlockSpec((rows, columns), lambda i, at=at, across=across: (at, across(i)))
            for _, rows, at, columns, across in inputs
        ],
        out_specs=[pl.BlockSpec((rows, columns // steps), lambda i: (0, i)) for rows, columns, _ in outs],
        out_shape=[like(*shape) for shape in outs],
        scratch_shapes=[each for _, _, _, scratch in jobs for each in scratch],
        compiler_params=params(),
        cost_estimate=cost(),
        name="add",
    )(places, *in_hbm(*(value for value, *_ in inputs)))
    split = []
    for _, _, made, _ in jobs:
        split.append(results[: len(made)])
        results = results[len(made) :]
    return split


def together(*jobs):
    first = jobs[0][2][:2]

    def kernel(places_ref, *refs):
        counts = [len(inputs) for _, inputs, _, _ in jobs]
        refs, shared, rest = refs[: sum(counts)], refs[sum(counts) : sum(counts) + 2], list(refs[sum(counts) + 2 :])
        made = [[rest.pop(0) for _ in outs[2:]] for _, _, outs, _ in jobs]
        spare = [[rest.pop(0) for _ in scratch] for _, _, _, scratch in jobs]
        for k, (one, inputs, _, _) in enumerate(jobs):
            widths = [ref.shape[1] // len(jobs) for ref in shared]
            views = [ref.at[:, pl.ds(k * width, width)] for ref, width in zip(shared, widths)]
            one(places_ref, *refs[: counts[k]], *views, *made[k], *spare[k])
            refs = refs[counts[k] :]

    return (
        kernel,
        [value for _, inputs, _, _ in jobs for value in inputs],
        [(rows, len(jobs) * columns, kind) for rows, columns, kind in first]
        + [out for _, _, outs, _ in jobs for out in outs[2:]],
        [each for _, _, _, scratch in jobs for each in scratch],
    )


def attention_gradient(normed, d_projected, gradients, mixed):
    def kernel(normed_ref, d_ref, grad_ref, mixed_ref, out_ref):
        rows = pl.ds(pl.multiple_of(pl.program_id(0) * 512, 512), 512)
        sides = ((normed_ref[:, rows], d_ref, slice(0, 768)), (grad_ref[...], mixed_ref, slice(768, 1024)))
        for left, right, at in sides:
            out_ref[:, at] = lax.dot_general(
                left, right[...], (((0,), (0,)), ((), ())), preferred_element_type=F32
            ).astype(BF)

    def fixed(width):
        return pl.BlockSpec((1024, width), lambda i: (0, 0), pipeline_mode=pl.Buffered(1))

    return pl.pallas_call(
        kernel,
        grid=(D // 512,),
        in_specs=[VMEM, fixed(768), pl.BlockSpec((1024, 512), lambda i: (0, i)), fixed(256)],
        out_specs=pl.BlockSpec((512, 1024), lambda i: (i, 0)),
        out_shape=like(D, 1024),
        compiler_params=params(),
        cost_estimate=cost(),
        name="attention_gradient",
    )(in_vmem(normed), *in_hbm(d_projected, gradients, mixed))


def whole(low_index, *jobs):
    layouts = [each for _, _, layout in jobs for each in layout]

    def kernel(low_ref, *refs):
        halves, outs = refs[: 2 * len(jobs)], list(refs[2 * len(jobs) :])
        for k, (_, _, layout) in enumerate(jobs):
            at = 0
            for width, count in layout:
                out = outs.pop(0)
                mine = pl.ds(pl.multiple_of(low_ref[0] * width, width), width)
                theirs = pl.ds(pl.multiple_of((1 - low_ref[0]) * width, width), width)
                for i in range(count):
                    own, got = halves[2 * k], halves[2 * k + 1]
                    rows = pl.ds(0, BLK)
                    if own.shape[0] > BLK:
                        rows = pl.ds(pl.multiple_of(low_ref[0] * BLK, BLK), BLK)
                    out[i, :, mine] = own[rows, at : at + width].astype(F32)
                    out[i, :, theirs] = got[rows, at : at + width].astype(F32)
                    at += width

    return pl.pallas_call(
        kernel,
        in_specs=[SMEM] + [VMEM] * (2 * len(jobs)),
        out_specs=[VMEM] * len(layouts),
        out_shape=[pltpu.HBM((count, BLK, 2 * width), F32) for width, count in layouts],
        compiler_params=params(),
        cost_estimate=cost(),
        name="whole",
    )(low_index, *in_hbm(*(half for own, got, _ in jobs for half in (own, Arrived(got)))))


def inside(value):
    parts = [value[:, (low * 16 + n) * BLK : (low * 16 + n + 1) * BLK] for n in range(16) for low in range(2)]
    return jnp.concatenate(parts, axis=1)


def outside(value):
    parts = [value[:, (2 * n + low) * BLK : (2 * n + low + 1) * BLK] for low in range(2) for n in range(16)]
    return jnp.concatenate(parts, axis=1)


def prepare(low_index, residual, gradient, w_qkv, w_out, w_up, w_down, vectors):
    def kernel(low_ref, residual_ref, gradient_ref, qkv, out, up, down, *refs):
        *parts, tokens, grads, attn_own, attn_away, rest_own, rest_away, row = refs
        row[...] = jnp.concatenate([part[...].astype(F32) for part in parts] + [jnp.zeros((1, 80), F32)], axis=1).astype(BF)
        tokens[...] = inside(residual_ref[...])
        grads[...] = inside(gradient_ref[...])
        low = low_ref[0]
        for half, attn, rest in ((low, attn_own, rest_own), (1 - low, attn_away, rest_away)):
            narrow = pl.ds(pl.multiple_of(half * 256, 256), 256)
            wide = pl.ds(pl.multiple_of(half * 1024, 1024), 1024)
            for i in range(3):
                attn[:, i * 256 : (i + 1) * 256] = qkv[i, :, narrow]
            attn[:, 768:] = out[:, narrow]
            rest[:, :1024] = up[:, wide]
            rest[:, 1024:] = down[:, wide]

    return pl.pallas_call(
        kernel,
        in_specs=[SMEM] + [VMEM] * (6 + len(vectors)),
        out_specs=[VMEM] * 7,
        out_shape=[like(TOK, D)] * 2 + [like(BLK, 1024)] * 2 + [like(BLK, 2048)] * 2 + [like(1, 256)],
        compiler_params=params(),
        cost_estimate=cost(),
        name="prepare",
    )(low_index, *in_hbm(residual, gradient, w_qkv, w_out, w_up, w_down, *vectors))


def norm_and_project(core_index, mine, other, gain, shift, weights):
    def kernel(core_ref, mine_ref, other_ref, gain_ref, shift_ref, weight_ref, standard_ref, normed_ref, proj_ref):
        rows = (mine_ref[...], other_ref[...])
        first = core_ref[0] == 0
        value = jnp.concatenate([jnp.where(first, *rows), jnp.where(first, *rows[::-1])]).astype(F32)
        value = value - jnp.mean(value, axis=1, keepdims=True)
        value = value * lax.rsqrt(jnp.mean(value * value, axis=1, keepdims=True) + EPS)
        standard_ref[...] = value.astype(BF)
        normed = (value * gain_ref[...] + shift_ref[...]).astype(BF)
        normed_ref[...] = normed
        proj_ref[...] = jnp.dot(normed, weight_ref[...].reshape(D, 768), preferred_element_type=F32)

    def by_row(rows, width):
        return pl.BlockSpec((rows, width), lambda i: (i, 0))

    def fixed(*shape):
        return pl.BlockSpec(shape, lambda i: (0,) * len(shape), pipeline_mode=pl.Buffered(1))

    return pl.pallas_call(
        kernel,
        grid=(4,),
        in_specs=[SMEM, by_row(TOK, D), by_row(TOK, D), fixed(1, D), fixed(1, D), fixed(16, 128, 768)],
        out_specs=[by_row(256, D), by_row(256, D), by_row(256, 768)],
        out_shape=[like(1024, D), like(1024, D), like(1024, 768, F32)],
        compiler_params=params(),
        cost_estimate=cost(),
        name="norm_and_project",
    )(core_index, *in_hbm(mine, other, gain, shift, weights))


GELU_A = 0.7978845608028654
GELU_B = 0.044715


def hidden_units(places, normed, shift, left_plan, left_pieces, right_plan, right_pieces):
    pieces = [*left_pieces, *right_pieces]
    plan = [(*move, 0) for move in left_plan] + [(move[0] + 3, *move[1:], 1) for move in right_plan]
    width = 256
    steps = 1024 // width

    def kernel(places_ref, left, own, first, second, shift_ref, *refs):
        inputs, (hidden_ref, slope_ref, *wholes, stage, other_stage, sems) = refs[: len(pieces)], refs[len(pieces) :]
        stages = (stage, other_stage)
        moves = []
        for i, (source, row, rows, _, _, _, to, place, unit, _, side) in enumerate(plan):
            at = pl.ds(pl.multiple_of(to + places_ref[place] * unit, rows), rows)
            moves.append(
                (
                    pltpu.make_async_copy(inputs[source].at[pl.ds(row, rows)], stages[side].at[at], sems.at[0, i]),
                    pltpu.make_async_copy(stages[side].at[at], wholes[side].at[at], sems.at[1, i]),
                )
            )

        @pl.when(pl.program_id(0) == 0)
        def _():
            for arrive, _ in moves:
                arrive.start()

        u = shift_ref[...]
        for k, weight in enumerate((own[...], first[...], second[:512, :], second[512:, :])):
            z = places_ref[4 + k]
            block = jnp.concatenate(
                [left[:, pl.ds(pl.multiple_of(n * 512 + z * 128, 128), 128)] for n in range(4)], axis=1
            )
            u = u + jnp.dot(block, weight, preferred_element_type=F32)
        square = u * u
        t = jnp.tanh(GELU_A * u * (1.0 + GELU_B * square))
        half = 0.5 * (1.0 + t)
        hidden_ref[...] = (u * half).astype(BF)
        slope = half + 0.5 * u * (1.0 - t * t) * GELU_A * (1.0 + 3.0 * GELU_B * square)
        slope_ref[...] = slope.astype(BF)

        @pl.when(pl.program_id(0) == 1)
        def _():
            for arrive, leave in moves:
                arrive.wait()
                leave.start()

        @pl.when(pl.program_id(0) == steps - 1)
        def _():
            for _, leave in moves:
                leave.wait()

    column = pl.BlockSpec((1024, width), lambda i: (0, i))
    return pl.pallas_call(
        kernel,
        grid=(steps,),
        in_specs=[SMEM, VMEM]
        + [pl.BlockSpec((rows, width), lambda i: (0, i)) for rows in (512, 512, 1024, 1)]
        + [ANY] * len(pieces),
        out_specs=[column, column, ANY, ANY],
        out_shape=[like(1024, 1024), like(1024, 1024), like(D, 1024), like(D, 1024)],
        scratch_shapes=[pltpu.VMEM((D, 1024), BF)] * 2 + [pltpu.SemaphoreType.DMA((2, len(plan)))],
        compiler_params=params(),
        cost_estimate=cost(),
        name="hidden_units",
    )(places, in_vmem(normed), *in_hbm(*left_pieces, shift, *pieces))


def hidden_back_kernel(left, weight, slope_ref, d_ref, sum_ref):
    value = jnp.dot(left[...], weight[...], preferred_element_type=F32) * slope_ref[...].astype(F32)
    value = value.astype(BF)
    d_ref[...] = value
    sum_ref[...] = jnp.sum(value.astype(F32), axis=0, keepdims=True)


def hidden_back_and_apart(places, gradients, weights, slope, lefts, others):
    width = 256
    kernel_apart, in_specs, out_specs, out_shape, scratch = apart_parts(lefts, others)
    count = len(in_specs)

    def kernel(places_ref, left, weight, slope_ref, *refs):
        given, (d_ref, sum_ref, *made) = refs[:count], refs[count:]
        hidden_back_kernel(left, weight, slope_ref, d_ref, sum_ref)
        kernel_apart(places_ref, *given, *made)

    column = pl.BlockSpec((1024, width), lambda i: (0, i))
    return pl.pallas_call(
        kernel,
        grid=(4,),
        in_specs=[
            SMEM,
            pl.BlockSpec((1024, D), lambda i: (0, 0), pipeline_mode=pl.Buffered(1)),
            pl.BlockSpec((D, width), lambda i: (0, i)),
            column,
        ]
        + in_specs,
        out_specs=[column, pl.BlockSpec((1, width), lambda i: (0, i))] + out_specs,
        out_shape=[like(1024, 1024), like(1, 1024, F32)] + out_shape,
        scratch_shapes=scratch,
        compiler_params=params(32 * 1024 * 1024),
        cost_estimate=cost(),
        name="hidden_back_and_apart",
    )(places, *in_hbm(gradients, weights, slope, *lefts, *(weight for weight, _ in others)))


def apart_parts(lefts, weights, standard=None, near=False):
    count = len(lefts)

    def kernel(places_ref, *refs):
        value_ref = refs[-1]
        value = sum(
            lax.dot_general(
                left[...],
                weight[...].reshape(-1, weight.shape[2]),
                (((1,), (1,)), ((), ())),
                preferred_element_type=F32,
            )
            for left, weight in zip(refs[:count], refs[count : 2 * count])
        )
        refs = refs[2 * count : -1]
        if standard is not None:
            standard_ref, refs = refs[0], refs[1:]
            refs[2][0:1, :] = jnp.sum(value * standard_ref[...].astype(F32), axis=0, keepdims=True)
            refs[2][1:2, :] = jnp.sum(value, axis=0, keepdims=True)
        value_ref[...] = value
        for h in range(2):
            for k in range(4):
                rows = pl.ds(pl.multiple_of(places_ref[4 * h + k] * TOK, TOK), TOK)
                refs[h][k * TOK : (k + 1) * TOK, :] = value_ref[rows, :].astype(BF)

    width = 512
    extra = standard is not None
    whole_left = [pl.BlockSpec(left.shape, lambda i: (0, 0), pipeline_mode=pl.Buffered(1)) for left in lefts]
    in_specs = [VMEM for _ in lefts] if near else whole_left
    in_specs += [
        pl.BlockSpec((4, 128, left.shape[1]), lambda i, at=at: (i, 0, at)) for left, (_, at) in zip(lefts, weights)
    ]
    in_specs += [pl.BlockSpec((1024, width), lambda i: (0, i))] * extra
    out_specs = [pl.BlockSpec((512, width), lambda i: (0, i))] * 2 + [pl.BlockSpec((2, width), lambda i: (0, i))] * extra
    out_shape = [like(512, D)] * 2 + [like(2, D, F32)] * extra
    return kernel, in_specs, out_specs, out_shape, [pltpu.VMEM((1024, width), F32)]


def apart(places, lefts, weights, standard):
    kernel, in_specs, out_specs, out_shape, scratch = apart_parts(lefts, weights, standard, True)
    return pl.pallas_call(
        kernel,
        grid=(4,),
        in_specs=[SMEM] + in_specs,
        out_specs=out_specs,
        out_shape=out_shape,
        scratch_shapes=scratch,
        compiler_params=params(),
        cost_estimate=cost(),
        name="apart",
    )(places, *(in_vmem(left) for left in lefts), *in_hbm(*(weight for weight, _ in weights), standard))


def token_sum1(near, got):
    def kernel(places_ref, near_ref, got_ref, send_ref):
        send_ref[...] = (near_ref[...].astype(F32) + got_ref[...].astype(F32)).astype(BF)

    return kernel, [(near, 256, 1), (Arrived(got), 256, 1)], [(256, D, BF)], ()


def token_sum2(near, got, back):
    def kernel(places_ref, near_ref, got_ref, back_ref, send_ref):
        value = near_ref[...].astype(F32) + got_ref[...].astype(F32) + back_ref[...].astype(F32)
        send_ref[...] = value.astype(BF)

    return kernel, [(near, TOK, 1), (got, TOK, 1), (Arrived(back), TOK, 1)], [(TOK, D, BF)], ()


ROWS = pl.BlockSpec((TOK // 4, D), lambda i: (i, 0))
ONE_ROW = pl.BlockSpec((1, D), lambda i: (0, 0))


def finish_output(near, got, back, last, residual, shift):
    def kernel(near_ref, got_ref, back_ref, last_ref, residual_ref, shift_ref, out_ref):
        value = sum(ref[...].astype(F32) for ref in (near_ref, got_ref, back_ref, last_ref))
        value = residual_ref[...].astype(F32) + value + shift_ref[...]
        out_ref[...] = outside(value.astype(BF))

    return pl.pallas_call(
        kernel,
        grid=(4,),
        in_specs=[ROWS] * 5 + [ONE_ROW],
        out_specs=ROWS,
        out_shape=like(TOK, D),
        compiler_params=params(),
        cost_estimate=cost(),
        name="finish_output",
    )(*in_hbm(near, got, back, Arrived(last), residual, shift))


def finish_grad(near, got, back, last, residual, gradient, gain):
    def kernel(near_ref, got_ref, back_ref, last_ref, residual_ref, gradient_ref, gain_ref, out_ref):
        value = sum(ref[...].astype(F32) for ref in (near_ref, got_ref, back_ref, last_ref))
        value = value * gain_ref[...]
        rows = residual_ref[...].astype(F32)
        rows = rows - jnp.mean(rows, axis=1, keepdims=True)
        inverse = lax.rsqrt(jnp.mean(rows * rows, axis=1, keepdims=True) + EPS)
        rows = rows * inverse
        plain = jnp.mean(value, axis=1, keepdims=True)
        cross = jnp.mean(value * rows, axis=1, keepdims=True)
        out_ref[...] = outside(gradient_ref[...].astype(F32) + inverse * (value - plain - rows * cross))

    return pl.pallas_call(
        kernel,
        grid=(4,),
        in_specs=[ROWS] * 6 + [ONE_ROW],
        out_specs=ROWS,
        out_shape=like(TOK, D, F32),
        compiler_params=params(),
        cost_estimate=cost(),
        name="finish_grad",
    )(*in_hbm(near, got, back, Arrived(last), residual, gradient, gain))


def doc_positions(segments):
    length = segments.shape[0]
    places = jnp.arange(length, dtype=jnp.int32)
    boundary = jnp.concatenate([jnp.ones((1,), dtype=jnp.bool_), segments[1:] != segments[:-1]])
    doc_start = lax.cummax(jnp.where(boundary, places, jnp.zeros_like(places)), axis=0)
    return places - doc_start


def rotary_tables(positions):
    lane = jnp.arange(128, dtype=jnp.int32) % HD
    half_rot = ROT // 2
    frequency = 10000.0 ** (-(2.0 * (lane % half_rot).astype(F32)) / ROT)
    angles = positions.astype(F32)[:, None] * jnp.where(lane < ROT, frequency, 0.0)
    sine = jnp.sin(angles)
    before = jnp.where(lane < half_rot, -sine, 0.0)
    after = jnp.where((lane >= half_rot) & (lane < ROT), sine, 0.0)
    return jnp.concatenate([jnp.cos(angles), before, after], axis=1)


def attention_kernel(
    core_ref,
    proj_ref,
    shift_ref,
    table_ref,
    column_ref,
    row_ref,
    mine_ref,
    other_ref,
    weight_ref,
    mixed_ref,
    d_proj_ref,
    sums_ref,
    grad_ref,
    mask_ref,
):
    start, last = column_ref[:, 0:1], column_ref[:, 1:2]
    where = row_ref[0]
    mask_ref[...] = jnp.where((where >= start) & (where <= last), 0.0, MASKED)
    cosine, before, after = (table_ref[:, i * 128 : (i + 1) * 128] for i in range(3))
    lane = lax.broadcasted_iota(jnp.int32, (SEQ, 128), 1)

    def turn(value, sign):
        shifted = pltpu.roll(value, 112, 1) * before + pltpu.roll(value, 16, 1) * after
        return value * cosine + sign * shifted

    def part(index, pair):
        at = slice(index * 256 + pair * 128, index * 256 + pair * 128 + 128)
        return proj_ref[:, at] + shift_ref[:, at]

    def dot(a, b, dims):
        return lax.dot_general(a, b, (dims, ((), ())), preferred_element_type=F32)

    first_core = core_ref[0] == 0
    for i in range(2):
        both = [ref[i * TOK : (i + 1) * TOK, :] for ref in (mine_ref, other_ref)]
        grad_ref[2 * i * TOK : (2 * i + 1) * TOK, :] = jnp.where(first_core, *both)
        grad_ref[(2 * i + 1) * TOK : (2 * i + 2) * TOK, :] = jnp.where(first_core, *both[::-1])
    d_attended = jnp.dot(grad_ref[...], weight_ref[...].reshape(D, 256), preferred_element_type=F32).astype(BF)
    for pair in range(2):
        at = slice(pair * 128, pair * 128 + 128)
        queries = (turn(part(0, pair), 1.0).astype(BF).astype(F32) * HD**-0.5).astype(BF)
        keys = turn(part(1, pair), 1.0).astype(BF)
        values = part(2, pair).astype(BF)
        d_out = d_attended[:, at]
        results = []
        for head in range(2):
            own = (lane >= head * HD) & (lane < (head + 1) * HD)
            own_queries = jnp.where(own, queries, jnp.zeros_like(queries))
            own_d_out = jnp.where(own, d_out, jnp.zeros_like(d_out))
            scores = dot(own_queries, keys, ((1,), (1,))) + mask_ref[...]
            exponent = jnp.exp(scores - jnp.max(scores, axis=1, keepdims=True))
            soft = exponent * (1.0 / jnp.sum(exponent, axis=1, keepdims=True))
            soft_low = soft.astype(BF)
            mixed = dot(soft_low, values, ((1,), (0,)))
            d_soft = dot(own_d_out, values, ((1,), (1,)))
            inner = jnp.sum(soft * d_soft, axis=1, keepdims=True)
            d_scores = (soft * (d_soft - inner)).astype(BF)
            d_queries = dot(d_scores, keys, ((1,), (0,))) * HD**-0.5
            d_keys = dot(d_scores, own_queries, ((0,), (0,)))
            d_values = dot(soft_low, own_d_out, ((0,), (0,)))
            results.append((mixed, d_queries, d_keys, d_values))
        first, second = results
        mixed_ref[:, at] = jnp.where(lane < HD, first[0], second[0]).astype(BF)
        d_queries = turn(jnp.where(lane < HD, first[1], second[1]), -1.0).astype(BF)
        d_keys = turn(first[2] + second[2], -1.0).astype(BF)
        d_values = (first[3] + second[3]).astype(BF)
        for index, value in enumerate((d_queries, d_keys, d_values)):
            at = slice(index * 256 + pair * 128, index * 256 + pair * 128 + 128)
            d_proj_ref[:, at] = value
            sums_ref[0, :, at] = jnp.sum(value.astype(F32), axis=0, keepdims=True)


def attention(core_index, projected, shift, tables, columns, rows, mine, other, weights):
    count = projected.shape[0] // SEQ
    return pl.pallas_call(
        attention_kernel,
        grid=(count,),
        in_specs=[
            SMEM,
            pl.BlockSpec((SEQ, 768), lambda i: (i, 0)),
            pl.BlockSpec((1, 768), lambda i: (0, 0)),
            pl.BlockSpec((SEQ, 384), lambda i: (i, 0)),
            pl.BlockSpec((SEQ, 2), lambda i: (i, 0)),
            pl.BlockSpec((1, 1, SEQ), lambda i: (i, 0, 0)),
            pl.BlockSpec((SEQ // 2, D), lambda i: (i, 0)),
            pl.BlockSpec((SEQ // 2, D), lambda i: (i, 0)),
            pl.BlockSpec((16, 128, 256), lambda i: (0, 0, 3), pipeline_mode=pl.Buffered(1)),
        ],
        out_specs=[
            pl.BlockSpec((SEQ, 256), lambda i: (i, 0)),
            pl.BlockSpec((SEQ, 768), lambda i: (i, 0)),
            pl.BlockSpec((1, 1, 768), lambda i: (i, 0, 0)),
            pl.BlockSpec((SEQ, D), lambda i: (i, 0)),
        ],
        out_shape=[
            pltpu.HBM((count * SEQ, 256), BF),
            pltpu.HBM((count * SEQ, 768), BF),
            pltpu.HBM((count, 1, 768), F32),
            like(count * SEQ, D),
        ],
        scratch_shapes=[pltpu.VMEM((SEQ, SEQ), F32)],
        compiler_params=pltpu.CompilerParams(vmem_limit_bytes=VMEM_LIMIT),
        cost_estimate=cost(),
        name="attention",
    )(core_index, *in_hbm(projected, shift, tables, columns, rows, mine, Arrived(other), weights))


def body(
    residual_in,
    segment_ids,
    out_grad,
    ln_gain,
    ln_bias,
    w_qkv,
    b_qkv,
    w_out,
    b_attn_out,
    w_up,
    b_up,
    w_down,
    b_mlp_out,
):
    y_lo, x, z, y_hi, core = (lax.axis_index(name).astype(jnp.int32) for name in AXES)
    low_index = y_lo[None]
    low = y_lo == 0

    def around(c):
        return [c, c ^ (1 + 2 * core), c ^ (3 - 2 * core), c ^ 2]

    y_places = [
        y_lo * 2 + y_hi,
        (1 - y_lo) * 2 + (y_hi ^ core),
        (1 - y_lo) * 2 + (y_hi ^ (1 - core)),
        y_lo * 2 + (1 - y_hi),
    ]
    ring_places = jnp.stack(
        around(x)
        + around(z)
        + [y_lo, 1 - y_lo]
        + y_places
        + [2 * k + core for k in range(4)]
        + [2 * k + 1 - core for k in range(4)]
    )
    part_places = jnp.stack(
        [2 * p + core for p in y_places] + [2 * y_places[k] + 1 - core for k in (0, 2, 1, 3)]
    )

    vectors = [value.reshape(1, -1) for value in (ln_gain, ln_bias, b_attn_out, b_mlp_out, b_up)]
    vectors += [b_qkv[i] for i in range(3)]
    residual, gradient, attn_own, attn_away, rest_own, rest_away, small = prepare(
        low_index, residual_in, out_grad, w_qkv.transpose(1, 0, 2), w_out.T, w_up, w_down.T, vectors
    )

    def widen(rows, axis, index):
        got = flip(rows, axis)
        return jnp.where(index == 0, jnp.concatenate([rows, got]), jnp.concatenate([got, rows]))

    attn_got = flip(attn_away, "y_lo")
    small = widen(small, "core", core)
    small = widen(small, "y_hi", y_hi)
    attn_got, small, residual, gradient, rest_away = bar((attn_got, small, residual, gradient, rest_away))
    small = jnp.pad(small.reshape(1, 1024), ((0, 15), (0, 0)))

    def token_positions():
        far_segments = flip(segment_ids, "y_lo")
        places = jnp.arange(SEQ, dtype=jnp.int32)
        positions = jnp.concatenate(
            [doc_positions(jnp.where(low, a, b)) for a, b in ((segment_ids, far_segments), (far_segments, segment_ids))]
        )
        places = jnp.concatenate([places, places])
        columns = places[:, None] - jnp.where(jnp.arange(2)[None] == 0, positions[:, None], 0)
        return columns, places.reshape(2, 1, SEQ), rotary_tables(positions)

    def joined(own, first):
        plan = [(source, 0, TOK, 0, D, 0, TOK * source, None, 0, 0) for source in range(2)]
        return plan, [(2 * TOK, D)], [own, Arrived(first)], False

    def of_core(own, first, second):
        plan = [
            (source, row, TOK, 0, D, 0, 0, 10 + k, TOK, 0)
            for k, (source, row) in enumerate(((0, 0), (1, 0), (2, 0), (2, TOK)))
        ]
        return plan, [(SEQ, D)], [own, Arrived(first), Arrived(second)], False

    plan = [(source, 0, BLK, 0, 1024, 0, 0, 8 + source, BLK, 0) for source in range(2)]
    plan.append((2, 0, 16, 0, 1024, 0, 128, None, 0, 0))
    ((shard,),) = copies(ring_places, (plan, [(144, 1024)], [attn_own, Arrived(attn_got), small], False))
    attn_all = lax.all_gather(shard, ("x", "z"), axis=0)
    token_first = swap_y(residual, 0)
    rest_got = flip(rest_away, "y_lo")
    shard, token_first, rest_got, gradient = bar((shard, token_first, rest_got, gradient))
    plan = [
        (source, 0, BLK, 1024 * h, 1024, h, 0, 8 + source, BLK, 0) for source in range(2) for h in range(2)
    ]
    (tokens_sent,), sends = copies(
        ring_places, joined(residual, token_first), (plan, [(128, 1024)] * 2, [rest_own, Arrived(rest_got)], False)
    )
    rest_gather = Gather(*sends)
    tokens_sent, sends, gradient = bar((tokens_sent, sends, gradient))
    token_second = swap_y(tokens_sent, 1)
    grad_first = swap_y(gradient, 0)
    got = gather_step(1, sends)
    token_second, grad_first, got = bar((token_second, grad_first, got))
    (mine,), (grads_sent,), sends = copies(
        ring_places,
        of_core(residual, token_first, token_second),
        joined(gradient, grad_first),
        rest_gather.sending(got),
    )
    mine, grads_sent, sends = bar((mine, grads_sent, sends))
    other = flip(mine, "core")
    grad_second = swap_y(grads_sent, 1)
    positions = token_positions()
    got, other, mine, grad_second, positions, table = bar(
        (gather_step(2, sends), other, mine, grad_second, positions, attn_all[:, 128, :][None])
    )
    tokens = (mine, other)
    other_table = flip(table, "y_lo")
    rest_gather.pair, (mine,) = copies(
        ring_places, rest_gather.joining(got), of_core(gradient, grad_first, grad_second)
    )
    sends, mine, table, other_table = bar((rest_gather.pair, mine, table, other_table))
    other = flip(mine, "core")
    got = gather_step(3, sends)
    columns, rows, tables = positions

    table = jnp.where(low, jnp.concatenate([table, other_table]), jnp.concatenate([other_table, table]))
    table = table.reshape(2, 16, 4, 256).astype(F32)
    vectors = table[..., :64].reshape(2, 16, 4, 4, 16).transpose(3, 1, 0, 2, 4).reshape(4, D)
    gain, shift, out_shift = vectors[0:1], vectors[1:2], vectors[2:3] + vectors[3:4]
    shifts = lax.dynamic_index_in_dim(table.reshape(2, 16, 4, 256), y_hi * 2 + core, 2, False)
    shifts = lax.dynamic_index_in_dim(shifts, y_lo, 0, False)
    up_shift = shifts[:, 64:128].reshape(1, 1024)
    qkv_shift = shifts[:, 128:176].reshape(16, 3, 16).transpose(1, 0, 2).reshape(1, 768)

    standard, normed, projected = norm_and_project(core[None], *tokens, gain, shift, attn_all)
    got, other, mine, normed, projected = bar((got, other, mine, normed, projected))
    (sends,) = copies(ring_places, rest_gather.sending(got))
    sends, mine, other, projected = bar((sends, mine, other, projected))
    rest_got = gather_step(4, sends)
    mixed, d_projected, shift_sums, grad_all = attention(
        core[None], projected, qkv_shift, tables, columns, rows, mine, other, attn_all
    )
    attn_sum = attention_gradient(normed, d_projected, grad_all, mixed)
    attn_sum, rest_got, normed = bar((attn_sum, rest_got, normed))
    attn_sum = lax.psum_scatter(attn_sum, ("x", "z"), scatter_dimension=0, tiled=True)

    rest_gather.last = tuple(Arrived(value) for value in rest_got)
    hidden, slope, up_all, down_all = hidden_units(
        ring_places, normed, up_shift, *rest_gather.side(0), *rest_gather.side(1)
    )
    down_sum = Scatter(ring_places, 0, grad_all, hidden)
    sends, mixed, hidden, slope, grad_all = bar((down_sum.first, mixed, hidden, slope, grad_all))
    down_got = scatter_step(1, sends)
    d_hidden, up_shift_part, near, away = hidden_back_and_apart(
        part_places, grad_all, down_all, slope, [mixed, hidden], [(attn_all, 3), (down_all.reshape(16, 128, 1024), 0)]
    )
    up_sum = Scatter(ring_places, 1, normed, d_hidden)
    up_sends, near, away, d_hidden, down_got = bar((up_sum.first, near, away, d_hidden, down_got))

    up_got = scatter_step(1, up_sends)
    out_got = flip(away, "core")
    d_near, d_away, vector_parts = apart(
        part_places,
        [d_projected, d_hidden],
        [(attn_all, 0), (up_all.reshape(16, 128, 1024), 0)],
        standard,
    )
    d_away, up_got, out_got, vector_parts = bar((d_away, up_got, out_got, vector_parts))
    sums = (down_sum, up_sum)
    sends, (out_send,) = add(
        ring_places,
        together(down_sum.send2(down_got), up_sum.send2(up_got)),
        token_sum1(near, out_got),
    )
    sends, out_send, d_away, vector_parts = bar((sends, out_send, d_away, vector_parts))
    d_got = flip(d_away, "core")
    got = scatter_step(2, sends)
    out_back = swap_y(out_send, 1)
    out_shift_part = jnp.sum(gradient.astype(F32), axis=0, keepdims=True)
    parts = jnp.concatenate([vector_parts, out_shift_part]).reshape(3, 16, 8, 16)
    parts = parts.transpose(1, 2, 0, 3).reshape(16, 384)
    shift_sums = jnp.sum(shift_sums, axis=(0, 1))
    line = jnp.concatenate(
        [
            parts,
            up_shift_part.reshape(16, 64),
            shift_sums.reshape(3, 16, 16).transpose(1, 0, 2).reshape(16, 48),
            jnp.zeros((16, 16), F32),
        ],
        axis=1,
    )
    offsets = [0]
    for _, _, bits in RING_STEPS:
        offsets = offsets + [o ^ bits for o in offsets]
    here = (4 * x + z) ^ jnp.array(offsets, jnp.int32)
    order = (here[:, None] == jnp.arange(16, dtype=jnp.int32)[None, :]).astype(F32)
    line = jnp.dot(order, line, precision=lax.Precision.HIGHEST)

    def fold(line, step):
        axis, mask, _ = RING_STEPS[step]
        count = line.shape[0] // 2
        return line[:count] + flip4(line[count:], axis, mask)

    def narrow(part, axis, index):
        part = part.reshape(2, -1)
        return jnp.where(index == 0, part[0], part[1]) + flip(jnp.where(index == 0, part[1], part[0]), axis)

    line = fold(fold(line, 3), 2)
    d_got, got, out_back, line = bar((d_got, got, out_back, line))
    sends, (d_send,), (out_send,) = add(
        ring_places,
        together(*(each.send3(got) for each in sums)),
        token_sum1(d_near, d_got),
        token_sum2(near, out_got, out_back),
    )
    down_sum.keep, up_sum.keep = sends[2:4], sends[4:]
    sends, d_send, out_send, line = bar((sends[:2], d_send, out_send, line))
    d_back = swap_y(d_send, 1)
    got = scatter_step(3, sends)
    line = fold(fold(line, 1), 0)[0]
    part = narrow(line[:384], "y_lo", y_lo)
    out_last = swap_y(out_send, 0)
    d_back, got, part, out_last, attn_sum = bar((d_back, got, part, out_last, attn_sum))
    sends, (d_send,) = add(
        ring_places, together(*(each.send4(got) for each in sums)), token_sum2(d_near, d_got, d_back)
    )
    sends, d_send, part, attn_sum, out_last = bar((sends, d_send, part, attn_sum, out_last))
    d_last = swap_y(d_send, 0)
    got = scatter_step(4, sends)
    attn_far = flip(attn_sum, "y_lo")
    part = narrow(part, "y_hi", y_hi)
    output = finish_output(near, out_got, out_back, out_last, residual, out_shift)
    d_last, got, part, attn_far, output = bar((d_last, got, part, attn_far, output))
    ((own, away),) = add(ring_places, together(*(each.finish(got) for each in sums)), steps=1)
    away, part, d_last = bar((away, part, d_last))
    far = flip(away, "y_lo")
    part = narrow(part, "core", core)
    grad_in = finish_grad(d_near, d_got, d_back, d_last, residual, gradient, gain)
    far, part, grad_in = bar((far, part, grad_in))
    sum_down, sum_up, sum_qkv, sum_out = whole(
        low_index, (own, far, ((1024, 1), (1024, 1))), (attn_sum, attn_far, ((256, 3), (256, 1)))
    )
    grad_gain, grad_shift, grad_out_shift = part[:16], part[16:32], part[32:]
    return (
        output,
        grad_in,
        grad_gain,
        grad_shift,
        sum_qkv.transpose(1, 0, 2),
        line[448:496].reshape(3, 1, 16),
        sum_out[0].T,
        grad_out_shift,
        sum_up[0],
        line[384:448].reshape(1, 64),
        sum_down[0].T,
        grad_out_shift,
    )


def solution(mesh):
    fine = Mesh(mesh.devices.reshape(2, 4, 4, 2, 2), AXES)
    dp = ("y_lo", "x", "z")
    tensor = ("y_hi", "core")
    every = AXES
    in_specs = (
        P(every, None),
        P(dp),
        P(every, None),
        P(every),
        P(every),
        P(dp, None, tensor),
        P(None, tensor, dp),
        P(tensor, dp),
        P(every),
        P(dp, tensor),
        P(tensor, dp),
        P(tensor, dp),
        P(every),
    )
    out_specs = (
        P(every, None),
        P(every, None),
        P(every),
        P(every),
        P(dp, None, tensor),
        P(None, tensor, dp),
        P(tensor, dp),
        P(every),
        P(dp, tensor),
        P(tensor, dp),
        P(tensor, dp),
        P(every),
    )
    return jax.shard_map(body, mesh=fine, in_specs=in_specs, out_specs=out_specs, check_vma=False)
```

```python
import jax
import jax.numpy as jnp
from jax import lax
from jax.experimental import pallas as pl
from jax.experimental.pallas import tpu as pltpu
from jax.sharding import Mesh, PartitionSpec as P

HD = 64
ROT = 32
EPS = 1e-05
MASKED = -1e30
D = 2048
SEQ = 512
TOK = 128
BLK = 64
VMEM_LIMIT = 24 * 1024 * 1024
BF = jnp.bfloat16
F32 = jnp.float32
AXES = ("y_lo", "x", "z", "y_hi", "core")


bar = lax.optimization_barrier


def params(limit=VMEM_LIMIT):
    return pltpu.CompilerParams(vmem_limit_bytes=limit)


def cost():
    return pl.CostEstimate(flops=1000, bytes_accessed=1000, transcendentals=0)


def like(rows, columns, kind=BF):
    return pltpu.HBM((rows, columns), kind)


class Arrived:
    def __init__(self, value):
        self.value, self.shape = value, value.shape


def in_hbm(*values):
    return tuple(
        value.value if isinstance(value, Arrived) else pltpu.with_memory_space_constraint(value, pltpu.HBM)
        for value in values
    )


def in_vmem(value):
    return pltpu.with_memory_space_constraint(value, pltpu.VMEM)


SMEM = pl.BlockSpec(memory_space=pltpu.SMEM)
VMEM = pl.BlockSpec(memory_space=pltpu.VMEM)
ANY = pl.BlockSpec(memory_space=pl.ANY)


def ring(value, axis, step):
    masks = (1, 3) if step == 0 else (3, 1)
    table = [(i * 2 + c, (i ^ masks[c]) * 2 + c) for i in range(4) for c in range(2)]
    return lax.ppermute(value, (axis, "core"), table)


def ring_pair(pair, axes, step):
    pair = bar(tuple(pair))
    return bar(tuple(ring(value, axis, step) for value, axis in zip(pair, axes)))


def swap_y(value, step):
    masks = (1, 3) if step == 0 else (3, 1)

    def place(y, c):
        return ((y % 2) * 2 + y // 2) * 2 + c

    table = [(place(y, c), place(y ^ masks[c], c)) for y in range(4) for c in range(2)]
    return lax.ppermute(value, ("y_lo", "y_hi", "core"), table)


def flip(value, axis):
    return lax.ppermute(value, axis, [(0, 1), (1, 0)])


def copies(places, *jobs):
    sources = [source for _, _, given, _ in jobs for source in given]
    shapes = [(shape, stay) for _, made, _, stay in jobs for shape in made]
    plans, low, made = [], 0, 0
    for plan, results, given, stay in jobs:
        for source, row, rows, column, columns, target, to, place, unit, across in plan:
            plans.append((source + low, row, rows, column, columns, target + made, to, place, unit, across, stay))
        low += len(given)
        made += len(results)

    def kernel(places_ref, *refs):
        inputs, refs = refs[: len(sources)], refs[len(sources) :]
        outputs, spare, sems = refs[: len(shapes)], list(refs[len(shapes) : -1]), refs[-1]
        stages = [output if stay else spare.pop(0) for output, (_, stay) in zip(outputs, shapes)]
        moves = []
        for i, (source, row, rows, column, columns, target, to, place, unit, across, stay) in enumerate(plans):
            if place is not None:
                to = pl.multiple_of(to + places_ref[place] * unit, rows)
            at = (pl.ds(to, rows), pl.ds(across, columns))
            stage = stages[target].at[at]
            arrive = pltpu.make_async_copy(
                inputs[source].at[pl.ds(row, rows), pl.ds(column, columns)], stage, sems.at[0, i]
            )
            arrive.start()
            leave = None if stay else pltpu.make_async_copy(stage, outputs[target].at[at], sems.at[1, i])
            moves.append((arrive, leave))
        for arrive, leave in moves:
            arrive.wait()
            if leave is not None:
                leave.start()
        for _, leave in moves:
            if leave is not None:
                leave.wait()

    outs = pl.pallas_call(
        kernel,
        in_specs=[SMEM] + [ANY] * len(sources),
        out_specs=[VMEM if stay else ANY for _, stay in shapes],
        out_shape=[pltpu.VMEM(shape, BF) if stay else like(*shape) for shape, stay in shapes],
        scratch_shapes=[pltpu.VMEM(shape, BF) for shape, stay in shapes if not stay]
        + [pltpu.SemaphoreType.DMA((2, len(plans)))],
        compiler_params=params(),
        cost_estimate=cost(),
        name="put_together",
    )(places, *in_hbm(*sources))
    results = []
    for _, made, _, _ in jobs:
        results.append(outs[: len(made)])
        outs = outs[len(made) :]
    return results


def flip4(value, axis, mask):
    return lax.ppermute(value, axis, [(i, i ^ mask) for i in range(4)])


RING_STEPS = (("z", 1, 1), ("z", 3, 3), ("x", 1, 4), ("x", 3, 12))


class Gather:
    def __init__(self, left, right):
        self.pair = (left, right)

    def sending(self, got):
        self.first = got
        rows, width = self.pair[0].shape
        plan = [(2 * h + k, 0, rows, 0, width, h, k * rows, None, 0, 0) for h in range(2) for k in range(2)]
        sources = [value for own, first in zip(self.pair, got) for value in (own, Arrived(first))]
        return plan, [(2 * rows, width)] * 2, sources, False

    def joining(self, got):
        rows, width = self.pair[0].shape
        sources = [value for own, first, last in zip(self.pair, self.first, got) for value in (own, first, Arrived(last))]
        plan = []
        for h in range(2):
            for k, (source, row) in enumerate(((0, 0), (1, 0), (2, 0), (2, rows))):
                plan.append((source + 3 * h, row, rows, 0, width, h, 0, 4 * h + k, rows, 0))
        return plan, [(4 * rows, width)] * 2, sources, False

    def ordered(self, h):
        rows, width = self.pair[0].shape
        plan = []
        for k, (source, row) in enumerate(((0, 0), (1, 0), (2, 0), (2, rows))):
            for i in range(4):
                to, unit = ((i * 512, 128), (i * 128, 512))[h]
                plan.append((source, row + i * 128, 128, 0, width, 0, to, 4 * (1 - h) + k, unit, 0))
        return plan

    def side(self, h):
        return self.ordered(h), (self.pair[h], self.first[h], self.last[h])


def gather_step(step, pair):
    return ring_pair(pair, ("x", "z") if step < 3 else ("z", "x"), 1 - step % 2)


def scatter_step(step, pair):
    return ring_pair(pair, ("x", "z") if step < 3 else ("z", "x"), step % 2)


class Scatter:
    def __init__(self, places, index, left, right):
        self.places, self.index = places, index
        tokens, width = right.shape
        self.width = half = width // 2

        def kernel(places_ref, left_ref, right_ref, *refs):
            outs, (rights, *stages), sems = refs[:6], refs[6:-1], refs[-1]
            fetch = [
                pltpu.make_async_copy(right_ref.at[:, pl.ds(h * half, half)], rights.at[h], sems.at[h]) for h in range(2)
            ]
            for copy in fetch:
                copy.start()
            order = [2, 3, 1, 0]
            stored = []
            for h in range(2):
                fetch[h].wait()
                for i, k in enumerate(order):
                    if h == 0:
                        block = left_ref[:, pl.ds(pl.multiple_of(places_ref[k] * 512, 512), 512)]
                    else:
                        z = places_ref[4 + k]
                        block = jnp.concatenate(
                            [left_ref[:, pl.ds(pl.multiple_of(n * 512 + z * 128, 128), 128)] for n in range(4)], axis=1
                        )
                    value = lax.dot_general(
                        block,
                        rights[h],
                        (((0,), (0,)), ((), ())),
                        preferred_element_type=F32,
                    ).astype(BF)
                    stage = stages[h].at[pl.ds(i * 512, 512)]
                    stage[...] = value
                    out = outs[h].at[pl.ds(i * 512, 512)] if i < 2 else outs[2 * i - 2 + h]
                    copy = pltpu.make_async_copy(stage, out, sems.at[2 + 4 * h + i])
                    copy.start()
                    stored.append(copy)
            for copy in stored:
                copy.wait()

        outs = pl.pallas_call(
            kernel,
            in_specs=[SMEM, VMEM, ANY],
            out_specs=[ANY] * 6,
            out_shape=[like(1024, half)] * 2 + [like(512, half)] * 4,
            scratch_shapes=[
                pltpu.VMEM((2, tokens, half), BF),
                pltpu.VMEM((2048, half), BF),
                pltpu.VMEM((2048, half), BF),
                pltpu.SemaphoreType.DMA((10,)),
            ],
            compiler_params=params(),
            cost_estimate=cost(),
            name="gradient",
        )(places, in_vmem(left), *in_hbm(right))
        self.first, self.next, self.keep = outs[:2], outs[2:4], outs[4:]

    def part(self, got, rows, at, new=True):
        half = self.width // 2
        alone = got[0].shape[1] == self.width
        return [
            (Arrived(value) if new else value, rows, at, half, (lambda i: i) if alone else (lambda i: 2 * i + self.index)) for value in got
        ]

    def send2(self, got):
        self.got = got

        def kernel(places_ref, *refs):
            for h in range(2):
                refs[4 + h][...] = (refs[h][...].astype(F32) + refs[2 + h][...].astype(F32)).astype(BF)

        return kernel, [*self.next, *self.part(got, 512, 1)], [(512, self.width, BF)] * 2, ()

    def send3(self, last):
        def kernel(places_ref, *refs):
            total = refs[-1]
            for h in range(2):
                keep, arrived, later, send, own = (refs[2 * k + h] for k in range(5))
                total[...] = keep[...].astype(F32) + arrived[...].astype(F32) + later[...].astype(F32)
                own_at, first, second, across = (
                    pl.ds(pl.multiple_of(places_ref[4 * (1 - h) + k] * 128, 128), 128) for k in range(4)
                )
                send[:128, :] = total[second, :].astype(BF)
                send[128:, :] = total[across, :].astype(BF)
                own[:128, :] = total[first, :].astype(BF)
                own[128:, :] = total[own_at, :].astype(BF)

        return (
            kernel,
            [*self.keep, *self.part(self.got, 512, 0, False), *self.part(last, 512, 0)],
            [(256, self.width, BF)] * 4,
            [pltpu.VMEM((512, self.width // 2), F32)],
        )

    def send4(self, got):
        self.got = got

        def kernel(places_ref, *refs):
            for h in range(2):
                refs[4 + h][...] = (refs[h][...].astype(F32) + refs[2 + h][...].astype(F32)).astype(BF)

        return (
            kernel,
            [*((value, 128, 0) for value in self.keep), *self.part(got, 128, 1)],
            [(128, self.width, BF)] * 2,
            (),
        )

    def finish(self, last):
        width, half = self.width, self.width // 2

        def kernel(places_ref, *refs):
            total = refs[-1]
            for h in range(2):
                for i in range(2):
                    at = slice(i * half, (i + 1) * half)
                    keep, arrived, later = refs[h][:, at], refs[2 + 2 * h + i][...], refs[6 + 2 * h + i][...]
                    total[:, h * width + i * half : h * width + (i + 1) * half] = (
                        keep.astype(F32) + arrived.astype(F32) + later.astype(F32)
                    )
            low = places_ref[8]
            refs[10][...] = total[pl.ds(pl.multiple_of(low * BLK, BLK), BLK), :]
            refs[11][...] = total[pl.ds(pl.multiple_of((1 - low) * BLK, BLK), BLK), :].astype(BF)

        def parts(got):
            return [(value, 128, 0, half, lambda i, k=k: 2 * k + self.index) for value in got for k in range(2)]

        return (
            kernel,
            [*((value, 128, 1) for value in self.keep), *parts(self.got), *parts([Arrived(value) for value in last])],
            [(BLK, 2 * width, F32), (BLK, 2 * width, BF)],
            [pltpu.VMEM((128, 2 * width), F32)],
        )


def add(places, *jobs, steps=2):
    def full(value, rows, at, columns=None, across=lambda i: i):
        return value, rows, at, columns or value.shape[1] // steps, across

    jobs = [
        (kernel, [full(*v) if isinstance(v, tuple) else full(v, v.shape[0], 0) for v in inputs], outs, scratch)
        for kernel, inputs, outs, scratch in jobs
    ]
    inputs = [value for _, given, _, _ in jobs for value in given]
    outs = [out for _, _, made, _ in jobs for out in made]

    def kernel(places_ref, *refs):
        given, made, spare = refs[: len(inputs)], refs[len(inputs) : len(inputs) + len(outs)], refs[len(inputs) + len(outs) :]
        for one, ins, results, scratch in jobs:
            one(places_ref, *given[: len(ins)], *made[: len(results)], *spare[: len(scratch)])
            given, made, spare = given[len(ins) :], made[len(results) :], spare[len(scratch) :]

    results = pl.pallas_call(
        kernel,
        grid=(steps,),
        in_specs=[SMEM]
        + [
            pl.BlockSpec((rows, columns), lambda i, at=at, across=across: (at, across(i)))
            for _, rows, at, columns, across in inputs
        ],
        out_specs=[pl.BlockSpec((rows, columns // steps), lambda i: (0, i)) for rows, columns, _ in outs],
        out_shape=[like(*shape) for shape in outs],
        scratch_shapes=[each for _, _, _, scratch in jobs for each in scratch],
        compiler_params=params(),
        cost_estimate=cost(),
        name="add",
    )(places, *in_hbm(*(value for value, *_ in inputs)))
    split = []
    for _, _, made, _ in jobs:
        split.append(results[: len(made)])
        results = results[len(made) :]
    return split


def together(*jobs):
    first = jobs[0][2][:2]

    def kernel(places_ref, *refs):
        counts = [len(inputs) for _, inputs, _, _ in jobs]
        refs, shared, rest = refs[: sum(counts)], refs[sum(counts) : sum(counts) + 2], list(refs[sum(counts) + 2 :])
        made = [[rest.pop(0) for _ in outs[2:]] for _, _, outs, _ in jobs]
        spare = [[rest.pop(0) for _ in scratch] for _, _, _, scratch in jobs]
        for k, (one, inputs, _, _) in enumerate(jobs):
            widths = [ref.shape[1] // len(jobs) for ref in shared]
            views = [ref.at[:, pl.ds(k * width, width)] for ref, width in zip(shared, widths)]
            one(places_ref, *refs[: counts[k]], *views, *made[k], *spare[k])
            refs = refs[counts[k] :]

    return (
        kernel,
        [value for _, inputs, _, _ in jobs for value in inputs],
        [(rows, len(jobs) * columns, kind) for rows, columns, kind in first]
        + [out for _, _, outs, _ in jobs for out in outs[2:]],
        [each for _, _, _, scratch in jobs for each in scratch],
    )


def attention_gradient(normed, d_projected, gradients, mixed):
    def kernel(normed_ref, d_ref, grad_ref, mixed_ref, out_ref):
        rows = pl.ds(pl.multiple_of(pl.program_id(0) * 512, 512), 512)
        sides = ((normed_ref[:, rows], d_ref, slice(0, 768)), (grad_ref[...], mixed_ref, slice(768, 1024)))
        for left, right, at in sides:
            out_ref[:, at] = lax.dot_general(
                left, right[...], (((0,), (0,)), ((), ())), preferred_element_type=F32
            ).astype(BF)

    def fixed(width):
        return pl.BlockSpec((1024, width), lambda i: (0, 0), pipeline_mode=pl.Buffered(1))

    return pl.pallas_call(
        kernel,
        grid=(D // 512,),
        in_specs=[VMEM, fixed(768), pl.BlockSpec((1024, 512), lambda i: (0, i)), fixed(256)],
        out_specs=pl.BlockSpec((512, 1024), lambda i: (i, 0)),
        out_shape=like(D, 1024),
        compiler_params=params(),
        cost_estimate=cost(),
        name="attention_gradient",
    )(in_vmem(normed), *in_hbm(d_projected, gradients, mixed))


def whole(low_index, *jobs):
    layouts = [each for _, _, layout in jobs for each in layout]

    def kernel(low_ref, *refs):
        halves, outs = refs[: 2 * len(jobs)], list(refs[2 * len(jobs) :])
        for k, (_, _, layout) in enumerate(jobs):
            at = 0
            for width, count in layout:
                out = outs.pop(0)
                mine = pl.ds(pl.multiple_of(low_ref[0] * width, width), width)
                theirs = pl.ds(pl.multiple_of((1 - low_ref[0]) * width, width), width)
                for i in range(count):
                    own, got = halves[2 * k], halves[2 * k + 1]
                    rows = pl.ds(0, BLK)
                    if own.shape[0] > BLK:
                        rows = pl.ds(pl.multiple_of(low_ref[0] * BLK, BLK), BLK)
                    out[i, :, mine] = own[rows, at : at + width].astype(F32)
                    out[i, :, theirs] = got[rows, at : at + width].astype(F32)
                    at += width

    return pl.pallas_call(
        kernel,
        in_specs=[SMEM] + [VMEM] * (2 * len(jobs)),
        out_specs=[VMEM] * len(layouts),
        out_shape=[pltpu.HBM((count, BLK, 2 * width), F32) for width, count in layouts],
        compiler_params=params(),
        cost_estimate=cost(),
        name="whole",
    )(low_index, *in_hbm(*(half for own, got, _ in jobs for half in (own, Arrived(got)))))


def inside(value):
    parts = [value[:, (low * 16 + n) * BLK : (low * 16 + n + 1) * BLK] for n in range(16) for low in range(2)]
    return jnp.concatenate(parts, axis=1)


def outside(value):
    parts = [value[:, (2 * n + low) * BLK : (2 * n + low + 1) * BLK] for low in range(2) for n in range(16)]
    return jnp.concatenate(parts, axis=1)


def prepare(low_index, residual, gradient, w_qkv, w_out, w_up, w_down, vectors):
    def kernel(low_ref, residual_ref, gradient_ref, qkv, out, up, down, *refs):
        *parts, tokens, grads, attn_own, attn_away, rest_own, rest_away, row = refs
        row[...] = jnp.concatenate([part[...].astype(F32) for part in parts] + [jnp.zeros((1, 80), F32)], axis=1).astype(BF)
        tokens[...] = inside(residual_ref[...])
        grads[...] = inside(gradient_ref[...])
        low = low_ref[0]
        for half, attn, rest in ((low, attn_own, rest_own), (1 - low, attn_away, rest_away)):
            narrow = pl.ds(pl.multiple_of(half * 256, 256), 256)
            wide = pl.ds(pl.multiple_of(half * 1024, 1024), 1024)
            for i in range(3):
                attn[:, i * 256 : (i + 1) * 256] = qkv[i, :, narrow]
            attn[:, 768:] = out[:, narrow]
            rest[:, :1024] = up[:, wide]
            rest[:, 1024:] = down[:, wide]

    return pl.pallas_call(
        kernel,
        in_specs=[SMEM] + [VMEM] * (6 + len(vectors)),
        out_specs=[VMEM] * 7,
        out_shape=[like(TOK, D)] * 2 + [like(BLK, 1024)] * 2 + [like(BLK, 2048)] * 2 + [like(1, 256)],
        compiler_params=params(),
        cost_estimate=cost(),
        name="prepare",
    )(low_index, *in_hbm(residual, gradient, w_qkv, w_out, w_up, w_down, *vectors))


def norm_and_project(core_index, mine, other, gain, shift, weights):
    def kernel(core_ref, mine_ref, other_ref, gain_ref, shift_ref, weight_ref, standard_ref, normed_ref, proj_ref):
        rows = (mine_ref[...], other_ref[...])
        first = core_ref[0] == 0
        value = jnp.concatenate([jnp.where(first, *rows), jnp.where(first, *rows[::-1])]).astype(F32)
        value = value - jnp.mean(value, axis=1, keepdims=True)
        value = value * lax.rsqrt(jnp.mean(value * value, axis=1, keepdims=True) + EPS)
        standard_ref[...] = value.astype(BF)
        normed = (value * gain_ref[...] + shift_ref[...]).astype(BF)
        normed_ref[...] = normed
        proj_ref[...] = jnp.dot(normed, weight_ref[...].reshape(D, 768), preferred_element_type=F32)

    def by_row(rows, width):
        return pl.BlockSpec((rows, width), lambda i: (i, 0))

    def fixed(*shape):
        return pl.BlockSpec(shape, lambda i: (0,) * len(shape), pipeline_mode=pl.Buffered(1))

    return pl.pallas_call(
        kernel,
        grid=(4,),
        in_specs=[SMEM, by_row(TOK, D), by_row(TOK, D), fixed(1, D), fixed(1, D), fixed(16, 128, 768)],
        out_specs=[by_row(256, D), by_row(256, D), by_row(256, 768)],
        out_shape=[like(1024, D), like(1024, D), like(1024, 768, F32)],
        compiler_params=params(),
        cost_estimate=cost(),
        name="norm_and_project",
    )(core_index, *in_hbm(mine, other, gain, shift, weights))


GELU_A = 0.7978845608028654
GELU_B = 0.044715


def hidden_units(places, normed, shift, left_plan, left_pieces, right_plan, right_pieces):
    pieces = [*left_pieces, *right_pieces]
    plan = [(*move, 0) for move in left_plan] + [(move[0] + 3, *move[1:], 1) for move in right_plan]
    width = 256
    steps = 1024 // width

    def kernel(places_ref, left, own, first, second, shift_ref, *refs):
        inputs, (hidden_ref, slope_ref, *wholes, stage, other_stage, sems) = refs[: len(pieces)], refs[len(pieces) :]
        stages = (stage, other_stage)
        moves = []
        for i, (source, row, rows, _, _, _, to, place, unit, _, side) in enumerate(plan):
            at = pl.ds(pl.multiple_of(to + places_ref[place] * unit, rows), rows)
            moves.append(
                (
                    pltpu.make_async_copy(inputs[source].at[pl.ds(row, rows)], stages[side].at[at], sems.at[0, i]),
                    pltpu.make_async_copy(stages[side].at[at], wholes[side].at[at], sems.at[1, i]),
                )
            )

        @pl.when(pl.program_id(0) == 0)
        def _():
            for arrive, _ in moves:
                arrive.start()

        u = shift_ref[...]
        for k, weight in enumerate((own[...], first[...], second[:512, :], second[512:, :])):
            z = places_ref[4 + k]
            block = jnp.concatenate(
                [left[:, pl.ds(pl.multiple_of(n * 512 + z * 128, 128), 128)] for n in range(4)], axis=1
            )
            u = u + jnp.dot(block, weight, preferred_element_type=F32)
        square = u * u
        t = jnp.tanh(GELU_A * u * (1.0 + GELU_B * square))
        half = 0.5 * (1.0 + t)
        hidden_ref[...] = (u * half).astype(BF)
        slope = half + 0.5 * u * (1.0 - t * t) * GELU_A * (1.0 + 3.0 * GELU_B * square)
        slope_ref[...] = slope.astype(BF)

        @pl.when(pl.program_id(0) == 1)
        def _():
            for arrive, leave in moves:
                arrive.wait()
                leave.start()

        @pl.when(pl.program_id(0) == steps - 1)
        def _():
            for _, leave in moves:
                leave.wait()

    column = pl.BlockSpec((1024, width), lambda i: (0, i))
    return pl.pallas_call(
        kernel,
        grid=(steps,),
        in_specs=[SMEM, VMEM]
        + [pl.BlockSpec((rows, width), lambda i: (0, i)) for rows in (512, 512, 1024, 1)]
        + [ANY] * len(pieces),
        out_specs=[column, column, ANY, ANY],
        out_shape=[like(1024, 1024), like(1024, 1024), like(D, 1024), like(D, 1024)],
        scratch_shapes=[pltpu.VMEM((D, 1024), BF)] * 2 + [pltpu.SemaphoreType.DMA((2, len(plan)))],
        compiler_params=params(),
        cost_estimate=cost(),
        name="hidden_units",
    )(places, in_vmem(normed), *in_hbm(*left_pieces, shift, *pieces))


def hidden_back_kernel(left, weight, slope_ref, d_ref, sum_ref):
    value = jnp.dot(left[...], weight[...], preferred_element_type=F32) * slope_ref[...].astype(F32)
    value = value.astype(BF)
    d_ref[...] = value
    sum_ref[...] = jnp.sum(value.astype(F32), axis=0, keepdims=True)


def hidden_back_and_apart(places, gradients, weights, slope, lefts, others):
    width = 256
    kernel_apart, in_specs, out_specs, out_shape, scratch = apart_parts(lefts, others)
    count = len(in_specs)

    def kernel(places_ref, left, weight, slope_ref, *refs):
        given, (d_ref, sum_ref, *made) = refs[:count], refs[count:]
        hidden_back_kernel(left, weight, slope_ref, d_ref, sum_ref)
        kernel_apart(places_ref, *given, *made)

    column = pl.BlockSpec((1024, width), lambda i: (0, i))
    return pl.pallas_call(
        kernel,
        grid=(4,),
        in_specs=[
            SMEM,
            pl.BlockSpec((1024, D), lambda i: (0, 0), pipeline_mode=pl.Buffered(1)),
            pl.BlockSpec((D, width), lambda i: (0, i)),
            column,
        ]
        + in_specs,
        out_specs=[column, pl.BlockSpec((1, width), lambda i: (0, i))] + out_specs,
        out_shape=[like(1024, 1024), like(1, 1024, F32)] + out_shape,
        scratch_shapes=scratch,
        compiler_params=params(32 * 1024 * 1024),
        cost_estimate=cost(),
        name="hidden_back_and_apart",
    )(places, *in_hbm(gradients, weights, slope, *lefts, *(weight for weight, _ in others)))


def apart_parts(lefts, weights, standard=None, near=False):
    count = len(lefts)

    def kernel(places_ref, *refs):
        value_ref = refs[-1]
        value = sum(
            lax.dot_general(
                left[...],
                weight[...].reshape(-1, weight.shape[2]),
                (((1,), (1,)), ((), ())),
                preferred_element_type=F32,
            )
            for left, weight in zip(refs[:count], refs[count : 2 * count])
        )
        refs = refs[2 * count : -1]
        if standard is not None:
            standard_ref, refs = refs[0], refs[1:]
            refs[2][0:1, :] = jnp.sum(value * standard_ref[...].astype(F32), axis=0, keepdims=True)
            refs[2][1:2, :] = jnp.sum(value, axis=0, keepdims=True)
        value_ref[...] = value
        for h in range(2):
            for k in range(4):
                rows = pl.ds(pl.multiple_of(places_ref[4 * h + k] * TOK, TOK), TOK)
                refs[h][k * TOK : (k + 1) * TOK, :] = value_ref[rows, :].astype(BF)

    width = 512
    extra = standard is not None
    whole_left = [pl.BlockSpec(left.shape, lambda i: (0, 0), pipeline_mode=pl.Buffered(1)) for left in lefts]
    in_specs = [VMEM for _ in lefts] if near else whole_left
    in_specs += [
        pl.BlockSpec((4, 128, left.shape[1]), lambda i, at=at: (i, 0, at)) for left, (_, at) in zip(lefts, weights)
    ]
    in_specs += [pl.BlockSpec((1024, width), lambda i: (0, i))] * extra
    out_specs = [pl.BlockSpec((512, width), lambda i: (0, i))] * 2 + [pl.BlockSpec((2, width), lambda i: (0, i))] * extra
    out_shape = [like(512, D)] * 2 + [like(2, D, F32)] * extra
    return kernel, in_specs, out_specs, out_shape, [pltpu.VMEM((1024, width), F32)]


def apart(places, lefts, weights, standard):
    kernel, in_specs, out_specs, out_shape, scratch = apart_parts(lefts, weights, standard, True)
    return pl.pallas_call(
        kernel,
        grid=(4,),
        in_specs=[SMEM] + in_specs,
        out_specs=out_specs,
        out_shape=out_shape,
        scratch_shapes=scratch,
        compiler_params=params(),
        cost_estimate=cost(),
        name="apart",
    )(places, *(in_vmem(left) for left in lefts), *in_hbm(*(weight for weight, _ in weights), standard))


def token_sum1(near, got):
    def kernel(places_ref, near_ref, got_ref, send_ref):
        send_ref[...] = (near_ref[...].astype(F32) + got_ref[...].astype(F32)).astype(BF)

    return kernel, [(near, 256, 1), (Arrived(got), 256, 1)], [(256, D, BF)], ()


def token_sum2(near, got, back):
    def kernel(places_ref, near_ref, got_ref, back_ref, send_ref):
        value = near_ref[...].astype(F32) + got_ref[...].astype(F32) + back_ref[...].astype(F32)
        send_ref[...] = value.astype(BF)

    return kernel, [(near, TOK, 1), (got, TOK, 1), (Arrived(back), TOK, 1)], [(TOK, D, BF)], ()


ROWS = pl.BlockSpec((TOK // 4, D), lambda i: (i, 0))
ONE_ROW = pl.BlockSpec((1, D), lambda i: (0, 0))


def finish_output(near, got, back, last, residual, shift):
    def kernel(near_ref, got_ref, back_ref, last_ref, residual_ref, shift_ref, out_ref):
        value = sum(ref[...].astype(F32) for ref in (near_ref, got_ref, back_ref, last_ref))
        value = residual_ref[...].astype(F32) + value + shift_ref[...]
        out_ref[...] = outside(value.astype(BF))

    return pl.pallas_call(
        kernel,
        grid=(4,),
        in_specs=[ROWS] * 5 + [ONE_ROW],
        out_specs=ROWS,
        out_shape=like(TOK, D),
        compiler_params=params(),
        cost_estimate=cost(),
        name="finish_output",
    )(*in_hbm(near, got, back, Arrived(last), residual, shift))


def finish_grad(near, got, back, last, residual, gradient, gain):
    def kernel(near_ref, got_ref, back_ref, last_ref, residual_ref, gradient_ref, gain_ref, out_ref):
        value = sum(ref[...].astype(F32) for ref in (near_ref, got_ref, back_ref, last_ref))
        value = value * gain_ref[...]
        rows = residual_ref[...].astype(F32)
        rows = rows - jnp.mean(rows, axis=1, keepdims=True)
        inverse = lax.rsqrt(jnp.mean(rows * rows, axis=1, keepdims=True) + EPS)
        rows = rows * inverse
        plain = jnp.mean(value, axis=1, keepdims=True)
        cross = jnp.mean(value * rows, axis=1, keepdims=True)
        out_ref[...] = outside(gradient_ref[...].astype(F32) + inverse * (value - plain - rows * cross))

    return pl.pallas_call(
        kernel,
        grid=(4,),
        in_specs=[ROWS] * 6 + [ONE_ROW],
        out_specs=ROWS,
        out_shape=like(TOK, D, F32),
        compiler_params=params(),
        cost_estimate=cost(),
        name="finish_grad",
    )(*in_hbm(near, got, back, Arrived(last), residual, gradient, gain))


def doc_positions(segments):
    length = segments.shape[0]
    places = jnp.arange(length, dtype=jnp.int32)
    boundary = jnp.concatenate([jnp.ones((1,), dtype=jnp.bool_), segments[1:] != segments[:-1]])
    doc_start = lax.cummax(jnp.where(boundary, places, jnp.zeros_like(places)), axis=0)
    return places - doc_start


def rotary_tables(positions):
    lane = jnp.arange(128, dtype=jnp.int32) % HD
    half_rot = ROT // 2
    frequency = 10000.0 ** (-(2.0 * (lane % half_rot).astype(F32)) / ROT)
    angles = positions.astype(F32)[:, None] * jnp.where(lane < ROT, frequency, 0.0)
    sine = jnp.sin(angles)
    before = jnp.where(lane < half_rot, -sine, 0.0)
    after = jnp.where((lane >= half_rot) & (lane < ROT), sine, 0.0)
    return jnp.concatenate([jnp.cos(angles), before, after], axis=1)


def attention_kernel(
    core_ref,
    proj_ref,
    shift_ref,
    table_ref,
    column_ref,
    row_ref,
    mine_ref,
    other_ref,
    weight_ref,
    mixed_ref,
    d_proj_ref,
    sums_ref,
    grad_ref,
    mask_ref,
):
    start, last = column_ref[:, 0:1], column_ref[:, 1:2]
    where = row_ref[0]
    mask_ref[...] = jnp.where((where >= start) & (where <= last), 0.0, MASKED)
    cosine, before, after = (table_ref[:, i * 128 : (i + 1) * 128] for i in range(3))
    lane = lax.broadcasted_iota(jnp.int32, (SEQ, 128), 1)

    def turn(value, sign):
        shifted = pltpu.roll(value, 112, 1) * before + pltpu.roll(value, 16, 1) * after
        return value * cosine + sign * shifted

    def part(index, pair):
        at = slice(index * 256 + pair * 128, index * 256 + pair * 128 + 128)
        return proj_ref[:, at] + shift_ref[:, at]

    def dot(a, b, dims):
        return lax.dot_general(a, b, (dims, ((), ())), preferred_element_type=F32)

    first_core = core_ref[0] == 0
    for i in range(2):
        both = [ref[i * TOK : (i + 1) * TOK, :] for ref in (mine_ref, other_ref)]
        grad_ref[2 * i * TOK : (2 * i + 1) * TOK, :] = jnp.where(first_core, *both)
        grad_ref[(2 * i + 1) * TOK : (2 * i + 2) * TOK, :] = jnp.where(first_core, *both[::-1])
    d_attended = jnp.dot(grad_ref[...], weight_ref[...].reshape(D, 256), preferred_element_type=F32).astype(BF)
    for pair in range(2):
        at = slice(pair * 128, pair * 128 + 128)
        queries = (turn(part(0, pair), 1.0).astype(BF).astype(F32) * HD**-0.5).astype(BF)
        keys = turn(part(1, pair), 1.0).astype(BF)
        values = part(2, pair).astype(BF)
        d_out = d_attended[:, at]
        results = []
        for head in range(2):
            own = (lane >= head * HD) & (lane < (head + 1) * HD)
            own_queries = jnp.where(own, queries, jnp.zeros_like(queries))
            own_d_out = jnp.where(own, d_out, jnp.zeros_like(d_out))
            scores = dot(own_queries, keys, ((1,), (1,))) + mask_ref[...]
            exponent = jnp.exp(scores - jnp.max(scores, axis=1, keepdims=True))
            scale = 1.0 / jnp.sum(exponent, axis=1, keepdims=True)
            low = exponent.astype(BF)
            mixed = dot(low, values, ((1,), (0,))) * scale
            own_d_out = (own_d_out.astype(F32) * scale).astype(BF)
            d_soft = dot(own_d_out, values, ((1,), (1,)))
            inner = jnp.sum(exponent * d_soft, axis=1, keepdims=True) * scale
            d_scores = (exponent * (d_soft - inner)).astype(BF)
            d_queries = dot(d_scores, keys, ((1,), (0,))) * HD**-0.5
            d_keys = dot(d_scores, own_queries, ((0,), (0,)))
            d_values = dot(low, own_d_out, ((0,), (0,)))
            results.append((mixed, d_queries, d_keys, d_values))
        first, second = results
        mixed_ref[:, at] = jnp.where(lane < HD, first[0], second[0]).astype(BF)
        d_queries = turn(jnp.where(lane < HD, first[1], second[1]), -1.0).astype(BF)
        d_keys = turn(first[2] + second[2], -1.0).astype(BF)
        d_values = (first[3] + second[3]).astype(BF)
        for index, value in enumerate((d_queries, d_keys, d_values)):
            at = slice(index * 256 + pair * 128, index * 256 + pair * 128 + 128)
            d_proj_ref[:, at] = value
            sums_ref[0, :, at] = jnp.sum(value.astype(F32), axis=0, keepdims=True)


def attention(core_index, projected, shift, tables, columns, rows, mine, other, weights):
    count = projected.shape[0] // SEQ
    return pl.pallas_call(
        attention_kernel,
        grid=(count,),
        in_specs=[
            SMEM,
            pl.BlockSpec((SEQ, 768), lambda i: (i, 0)),
            pl.BlockSpec((1, 768), lambda i: (0, 0)),
            pl.BlockSpec((SEQ, 384), lambda i: (i, 0)),
            pl.BlockSpec((SEQ, 2), lambda i: (i, 0)),
            pl.BlockSpec((1, 1, SEQ), lambda i: (i, 0, 0)),
            pl.BlockSpec((SEQ // 2, D), lambda i: (i, 0)),
            pl.BlockSpec((SEQ // 2, D), lambda i: (i, 0)),
            pl.BlockSpec((16, 128, 256), lambda i: (0, 0, 3), pipeline_mode=pl.Buffered(1)),
        ],
        out_specs=[
            pl.BlockSpec((SEQ, 256), lambda i: (i, 0)),
            pl.BlockSpec((SEQ, 768), lambda i: (i, 0)),
            pl.BlockSpec((1, 1, 768), lambda i: (i, 0, 0)),
            pl.BlockSpec((SEQ, D), lambda i: (i, 0)),
        ],
        out_shape=[
            pltpu.HBM((count * SEQ, 256), BF),
            pltpu.HBM((count * SEQ, 768), BF),
            pltpu.HBM((count, 1, 768), F32),
            like(count * SEQ, D),
        ],
        scratch_shapes=[pltpu.VMEM((SEQ, SEQ), F32)],
        compiler_params=pltpu.CompilerParams(vmem_limit_bytes=VMEM_LIMIT),
        cost_estimate=cost(),
        name="attention",
    )(core_index, *in_hbm(projected, shift, tables, columns, rows, mine, Arrived(other), weights))


def body(
    residual_in,
    segment_ids,
    out_grad,
    ln_gain,
    ln_bias,
    w_qkv,
    b_qkv,
    w_out,
    b_attn_out,
    w_up,
    b_up,
    w_down,
    b_mlp_out,
):
    y_lo, x, z, y_hi, core = (lax.axis_index(name).astype(jnp.int32) for name in AXES)
    low_index = y_lo[None]
    low = y_lo == 0

    def around(c):
        return [c, c ^ (1 + 2 * core), c ^ (3 - 2 * core), c ^ 2]

    y_places = [
        y_lo * 2 + y_hi,
        (1 - y_lo) * 2 + (y_hi ^ core),
        (1 - y_lo) * 2 + (y_hi ^ (1 - core)),
        y_lo * 2 + (1 - y_hi),
    ]
    ring_places = jnp.stack(
        around(x)
        + around(z)
        + [y_lo, 1 - y_lo]
        + y_places
        + [2 * k + core for k in range(4)]
        + [2 * k + 1 - core for k in range(4)]
    )
    part_places = jnp.stack(
        [2 * p + core for p in y_places] + [2 * y_places[k] + 1 - core for k in (0, 2, 1, 3)]
    )

    vectors = [value.reshape(1, -1) for value in (ln_gain, ln_bias, b_attn_out, b_mlp_out, b_up)]
    vectors += [b_qkv[i] for i in range(3)]
    residual, gradient, attn_own, attn_away, rest_own, rest_away, small = prepare(
        low_index, residual_in, out_grad, w_qkv.transpose(1, 0, 2), w_out.T, w_up, w_down.T, vectors
    )

    def widen(rows, axis, index):
        got = flip(rows, axis)
        return jnp.where(index == 0, jnp.concatenate([rows, got]), jnp.concatenate([got, rows]))

    attn_got = flip(attn_away, "y_lo")
    small = widen(small, "core", core)
    small = widen(small, "y_hi", y_hi)
    attn_got, small, residual, gradient, rest_away = bar((attn_got, small, residual, gradient, rest_away))
    small = jnp.pad(small.reshape(1, 1024), ((0, 15), (0, 0)))

    def token_positions():
        far_segments = flip(segment_ids, "y_lo")
        places = jnp.arange(SEQ, dtype=jnp.int32)
        positions = jnp.concatenate(
            [doc_positions(jnp.where(low, a, b)) for a, b in ((segment_ids, far_segments), (far_segments, segment_ids))]
        )
        places = jnp.concatenate([places, places])
        columns = places[:, None] - jnp.where(jnp.arange(2)[None] == 0, positions[:, None], 0)
        return columns, places.reshape(2, 1, SEQ), rotary_tables(positions)

    def joined(own, first):
        plan = [(source, 0, TOK, 0, D, 0, TOK * source, None, 0, 0) for source in range(2)]
        return plan, [(2 * TOK, D)], [own, Arrived(first)], False

    def of_core(own, first, second):
        plan = [
            (source, row, TOK, 0, D, 0, 0, 10 + k, TOK, 0)
            for k, (source, row) in enumerate(((0, 0), (1, 0), (2, 0), (2, TOK)))
        ]
        return plan, [(SEQ, D)], [own, Arrived(first), Arrived(second)], False

    plan = [(source, 0, BLK, 0, 1024, 0, 0, 8 + source, BLK, 0) for source in range(2)]
    plan.append((2, 0, 16, 0, 1024, 0, 128, None, 0, 0))
    ((shard,),) = copies(ring_places, (plan, [(144, 1024)], [attn_own, Arrived(attn_got), small], False))
    attn_all = lax.all_gather(shard, ("x", "z"), axis=0)
    token_first = swap_y(residual, 0)
    rest_got = flip(rest_away, "y_lo")
    shard, token_first, rest_got, gradient = bar((shard, token_first, rest_got, gradient))
    plan = [
        (source, 0, BLK, 1024 * h, 1024, h, 0, 8 + source, BLK, 0) for source in range(2) for h in range(2)
    ]
    (tokens_sent,), sends = copies(
        ring_places, joined(residual, token_first), (plan, [(128, 1024)] * 2, [rest_own, Arrived(rest_got)], False)
    )
    rest_gather = Gather(*sends)
    tokens_sent, sends, gradient = bar((tokens_sent, sends, gradient))
    token_second = swap_y(tokens_sent, 1)
    grad_first = swap_y(gradient, 0)
    got = gather_step(1, sends)
    token_second, grad_first, got = bar((token_second, grad_first, got))
    (mine,), (grads_sent,), sends = copies(
        ring_places,
        of_core(residual, token_first, token_second),
        joined(gradient, grad_first),
        rest_gather.sending(got),
    )
    mine, grads_sent, sends = bar((mine, grads_sent, sends))
    other = flip(mine, "core")
    grad_second = swap_y(grads_sent, 1)
    positions = token_positions()
    got, other, mine, grad_second, positions, table = bar(
        (gather_step(2, sends), other, mine, grad_second, positions, attn_all[:, 128, :][None])
    )
    tokens = (mine, other)
    other_table = flip(table, "y_lo")
    rest_gather.pair, (mine,) = copies(
        ring_places, rest_gather.joining(got), of_core(gradient, grad_first, grad_second)
    )
    sends, mine, table, other_table = bar((rest_gather.pair, mine, table, other_table))
    other = flip(mine, "core")
    got = gather_step(3, sends)
    columns, rows, tables = positions

    table = jnp.where(low, jnp.concatenate([table, other_table]), jnp.concatenate([other_table, table]))
    table = table.reshape(2, 16, 4, 256).astype(F32)
    vectors = table[..., :64].reshape(2, 16, 4, 4, 16).transpose(3, 1, 0, 2, 4).reshape(4, D)
    gain, shift, out_shift = vectors[0:1], vectors[1:2], vectors[2:3] + vectors[3:4]
    shifts = lax.dynamic_index_in_dim(table.reshape(2, 16, 4, 256), y_hi * 2 + core, 2, False)
    shifts = lax.dynamic_index_in_dim(shifts, y_lo, 0, False)
    up_shift = shifts[:, 64:128].reshape(1, 1024)
    qkv_shift = shifts[:, 128:176].reshape(16, 3, 16).transpose(1, 0, 2).reshape(1, 768)

    standard, normed, projected = norm_and_project(core[None], *tokens, gain, shift, attn_all)
    got, other, mine, normed, projected = bar((got, other, mine, normed, projected))
    (sends,) = copies(ring_places, rest_gather.sending(got))
    sends, mine, other, projected = bar((sends, mine, other, projected))
    rest_got = gather_step(4, sends)
    mixed, d_projected, shift_sums, grad_all = attention(
        core[None], projected, qkv_shift, tables, columns, rows, mine, other, attn_all
    )
    attn_sum = attention_gradient(normed, d_projected, grad_all, mixed)
    attn_sum, rest_got, normed = bar((attn_sum, rest_got, normed))
    attn_sum = lax.psum_scatter(attn_sum, ("x", "z"), scatter_dimension=0, tiled=True)

    rest_gather.last = tuple(Arrived(value) for value in rest_got)
    hidden, slope, up_all, down_all = hidden_units(
        ring_places, normed, up_shift, *rest_gather.side(0), *rest_gather.side(1)
    )
    down_sum = Scatter(ring_places, 0, grad_all, hidden)
    sends, mixed, hidden, slope, grad_all = bar((down_sum.first, mixed, hidden, slope, grad_all))
    down_got = scatter_step(1, sends)
    d_hidden, up_shift_part, near, away = hidden_back_and_apart(
        part_places, grad_all, down_all, slope, [mixed, hidden], [(attn_all, 3), (down_all.reshape(16, 128, 1024), 0)]
    )
    up_sum = Scatter(ring_places, 1, normed, d_hidden)
    up_sends, near, away, d_hidden, down_got = bar((up_sum.first, near, away, d_hidden, down_got))

    up_got = scatter_step(1, up_sends)
    out_got = flip(away, "core")
    d_near, d_away, vector_parts = apart(
        part_places,
        [d_projected, d_hidden],
        [(attn_all, 0), (up_all.reshape(16, 128, 1024), 0)],
        standard,
    )
    d_away, up_got, out_got, vector_parts = bar((d_away, up_got, out_got, vector_parts))
    sums = (down_sum, up_sum)
    sends, (out_send,) = add(
        ring_places,
        together(down_sum.send2(down_got), up_sum.send2(up_got)),
        token_sum1(near, out_got),
    )
    sends, out_send, d_away, vector_parts = bar((sends, out_send, d_away, vector_parts))
    d_got = flip(d_away, "core")
    got = scatter_step(2, sends)
    out_back = swap_y(out_send, 1)
    out_shift_part = jnp.sum(gradient.astype(F32), axis=0, keepdims=True)
    parts = jnp.concatenate([vector_parts, out_shift_part]).reshape(3, 16, 8, 16)
    parts = parts.transpose(1, 2, 0, 3).reshape(16, 384)
    shift_sums = jnp.sum(shift_sums, axis=(0, 1))
    line = jnp.concatenate(
        [
            parts,
            up_shift_part.reshape(16, 64),
            shift_sums.reshape(3, 16, 16).transpose(1, 0, 2).reshape(16, 48),
            jnp.zeros((16, 16), F32),
        ],
        axis=1,
    )
    offsets = [0]
    for _, _, bits in RING_STEPS:
        offsets = offsets + [o ^ bits for o in offsets]
    here = (4 * x + z) ^ jnp.array(offsets, jnp.int32)
    order = (here[:, None] == jnp.arange(16, dtype=jnp.int32)[None, :]).astype(F32)
    line = jnp.dot(order, line, precision=lax.Precision.HIGHEST)

    def fold(line, step):
        axis, mask, _ = RING_STEPS[step]
        count = line.shape[0] // 2
        return line[:count] + flip4(line[count:], axis, mask)

    def narrow(part, axis, index):
        part = part.reshape(2, -1)
        return jnp.where(index == 0, part[0], part[1]) + flip(jnp.where(index == 0, part[1], part[0]), axis)

    line = fold(fold(line, 3), 2)
    d_got, got, out_back, line = bar((d_got, got, out_back, line))
    sends, (d_send,), (out_send,) = add(
        ring_places,
        together(*(each.send3(got) for each in sums)),
        token_sum1(d_near, d_got),
        token_sum2(near, out_got, out_back),
    )
    down_sum.keep, up_sum.keep = sends[2:4], sends[4:]
    sends, d_send, out_send, line = bar((sends[:2], d_send, out_send, line))
    d_back = swap_y(d_send, 1)
    got = scatter_step(3, sends)
    line = fold(fold(line, 1), 0)[0]
    part = narrow(line[:384], "y_lo", y_lo)
    out_last = swap_y(out_send, 0)
    d_back, got, part, out_last, attn_sum = bar((d_back, got, part, out_last, attn_sum))
    sends, (d_send,) = add(
        ring_places, together(*(each.send4(got) for each in sums)), token_sum2(d_near, d_got, d_back)
    )
    sends, d_send, part, attn_sum, out_last = bar((sends, d_send, part, attn_sum, out_last))
    d_last = swap_y(d_send, 0)
    got = scatter_step(4, sends)
    attn_far = flip(attn_sum, "y_lo")
    part = narrow(part, "y_hi", y_hi)
    output = finish_output(near, out_got, out_back, out_last, residual, out_shift)
    d_last, got, part, attn_far, output = bar((d_last, got, part, attn_far, output))
    ((own, away),) = add(ring_places, together(*(each.finish(got) for each in sums)), steps=1)
    away, part, d_last = bar((away, part, d_last))
    far = flip(away, "y_lo")
    part = narrow(part, "core", core)
    grad_in = finish_grad(d_near, d_got, d_back, d_last, residual, gradient, gain)
    far, part, grad_in = bar((far, part, grad_in))
    sum_down, sum_up, sum_qkv, sum_out = whole(
        low_index, (own, far, ((1024, 1), (1024, 1))), (attn_sum, attn_far, ((256, 3), (256, 1)))
    )
    grad_gain, grad_shift, grad_out_shift = part[:16], part[16:32], part[32:]
    return (
        output,
        grad_in,
        grad_gain,
        grad_shift,
        sum_qkv.transpose(1, 0, 2),
        line[448:496].reshape(3, 1, 16),
        sum_out[0].T,
        grad_out_shift,
        sum_up[0],
        line[384:448].reshape(1, 64),
        sum_down[0].T,
        grad_out_shift,
    )


def solution(mesh):
    fine = Mesh(mesh.devices.reshape(2, 4, 4, 2, 2), AXES)
    dp = ("y_lo", "x", "z")
    tensor = ("y_hi", "core")
    every = AXES
    in_specs = (
        P(every, None),
        P(dp),
        P(every, None),
        P(every),
        P(every),
        P(dp, None, tensor),
        P(None, tensor, dp),
        P(tensor, dp),
        P(every),
        P(dp, tensor),
        P(tensor, dp),
        P(tensor, dp),
        P(every),
    )
    out_specs = (
        P(every, None),
        P(every, None),
        P(every),
        P(every),
        P(dp, None, tensor),
        P(None, tensor, dp),
        P(tensor, dp),
        P(every),
        P(dp, tensor),
        P(tensor, dp),
        P(tensor, dp),
        P(every),
    )
    return jax.shard_map(body, mesh=fine, in_specs=in_specs, out_specs=out_specs, check_vma=False)
```
